256 devices in a mesh: branch: 8 (over y, core), leaf: 32 (over z, x).
Axes of the slice: x: 4, y: 4, z: 8, core: 2. Of those that a mesh axis runs over, the one named last changes fastest.
Arguments:
- values: bfloat16 [2, 16, 131072], P(None, None, ('branch', 'leaf')), may hold values from -6 to 6
- leaf_basis: bfloat16 [2048, 64, 64], P(('branch', 'leaf')), may hold values from -0.75 to 0.75
- transfer: bfloat16 [3584, 64, 64], P(('branch', 'leaf')), may hold values from -0.625 to 0.625
- local_coupling: bfloat16 [2, 3584, 12, 64, 64], P(None, ('branch', 'leaf')), may hold values from -0.21875 to 0.21875
- coupling_source: int32 [3584, 12], P(('branch', 'leaf')), may hold values from 0 to 23, as said below
- near_field: bfloat16 [2, 2048, 12, 64, 64], P(None, ('branch', 'leaf')), may hold values from -0.21875 to 0.21875
- near_source: int32 [2048, 12], P(('branch', 'leaf')), may hold values from 0 to 23, as said below
- upper_transfer: bfloat16 [8, 62, 64, 64], P('branch'), may hold values from -0.625 to 0.625
- upper_coupling: bfloat16 [2, 8, 62, 64, 64], P(None, 'branch'), may hold values from -0.75 to 0.75
- top_coupling: bfloat16 [2, 8, 7, 64, 64], P(None, 'branch'), may hold values from -0.25 to 0.25
Outputs:
- result: float32 [2, 16, 131072], P(None, None, ('branch', 'leaf'))
The draws below stay inside these ranges and needn't reach their ends.
Inputs may be any that keep to these rules, and one draw needn't show every extreme that they name: `coupling_source`: entry of row r(l, p, t) lies in t to t + 2 * n_l, so its source is within n_l clusters of the target along the device order. `near_source`: entry of leaf t of a device lies in t to t + 16, so its source leaf is within 8 leaves of the target.
All inputs are finite; a program needn't handle non-finite values.
Results may differ from the reference program's by a relative error of at most 0.027.
Values may be sent and summed in bfloat16 or wider, within the bound.
No kernel may reach another device: no remote copies, remote signals or barrier semaphores. Data moves between devices by JAX's collectives and lax.ppermute only.
A program may use at most 64 MiB of HBM per device.

```python
import jax
import jax.numpy as jnp
from jax import lax

R = 64
LS = 64
RHS = 16
LOG_LEAF = 3
CPL = 12
NEAR = 12
LEAF_DEV = 8
NLEAF = 2048
POINTS = 131072
CROWS = 3584
UPPER = 62
N_BRANCH = 8
N_LEAF = 32


def draw_coupling_source(key, part):
    key = jax.random.fold_in(key, 11)
    rows = 2 * LEAF_DEV - 2
    local = jnp.arange(CROWS, dtype=jnp.int32) % rows
    count = jnp.zeros((CROWS,), jnp.int32)
    position = jnp.zeros((CROWS,), jnp.int32)
    for level in range(LOG_LEAF):
        size_here = LEAF_DEV >> level
        begin = 2 * LEAF_DEV - 2 * size_here
        inside = (local >= begin) & (local < begin + size_here)
        count = jnp.where(inside, size_here, count)
        position = jnp.where(inside, local - begin, position)
    lower = position[:, None]
    upper = (position + 2 * count + 1)[:, None]
    return jax.random.randint(key, (CROWS, CPL), lower, upper, dtype=jnp.int32)


def draw_near_source(key, part):
    key = jax.random.fold_in(key, 23)
    position = jnp.arange(NLEAF, dtype=jnp.int32) % LEAF_DEV
    lower = position[:, None]
    upper = (position + 2 * LEAF_DEV + 1)[:, None]
    return jax.random.randint(key, (NLEAF, NEAR), lower, upper, dtype=jnp.int32)


def level_of(key, dims, pieces, low, top_value):
    factor_of, own = 1.0, jax.random.fold_in(key, 6)
    for dim, shards_of in pieces:
        steps = jnp.exp(jax.random.uniform(jax.random.fold_in(own, dim), (shards_of,), jnp.float32, low / len(pieces), top_value / len(pieces)))
        factor_of = factor_of * jnp.repeat(steps, dims[dim] // shards_of).reshape([-1 if axis == dim else 1 for axis in range(len(dims))])
    return factor_of


def bell_draw(own_key, extent, width, most, cuts=(), kind=jnp.bfloat16):
    entries = width * jax.random.normal(own_key, extent, jnp.float32)
    if cuts:
        entries = entries * level_of(own_key, extent, cuts, -0.22, 0.18)
    return jnp.clip(entries, -most, most).astype(kind)


def setup_inputs(seed: int = 0) -> dict:
    splits = jax.random.split(jax.random.key(seed), 11)
    values = bell_draw(splits[0], (2, RHS, POINTS), 1.0, 6.0, ((2, 256),))
    leaf_basis = bell_draw(splits[1], (NLEAF, LS, R), LS ** -0.5, 0.75, ((0, 256),))
    transfer = bell_draw(splits[2], (CROWS, R, R), (3 * R // 2) ** -0.5, 0.625, ((0, 256),))
    local_coupling = bell_draw(splits[3], (2, CROWS, CPL, R, R), (CPL * R) ** -0.5, 0.21875, ((1, 256),))
    coupling_source = draw_coupling_source(jax.random.fold_in(splits[10], 71), 0)
    near_field = bell_draw(splits[5], (2, NLEAF, NEAR, LS, LS), (NEAR * LS) ** -0.5, 0.21875, ((1, 256),))
    near_source = draw_near_source(jax.random.fold_in(splits[10], 71), 0)
    upper_transfer = bell_draw(splits[7], (N_BRANCH, UPPER, R, R), (3 * R // 2) ** -0.5, 0.625, ((0, 8),))
    upper_coupling = bell_draw(splits[8], (2, N_BRANCH, UPPER, R, R), R ** -0.5, 0.75, ((1, 8),))
    top_coupling = bell_draw(splits[9], (2, N_BRANCH, N_BRANCH - 1, R, R), ((N_BRANCH - 1) * R) ** -0.5, 0.25, ((1, 8),))
    return dict(values=values, leaf_basis=leaf_basis, transfer=transfer, local_coupling=local_coupling, coupling_source=coupling_source, near_field=near_field, near_source=near_source, upper_transfer=upper_transfer, upper_coupling=upper_coupling, top_coupling=top_coupling)


def window(blocks):
    zero = jnp.zeros_like(blocks[:1])
    before = jnp.concatenate([zero, blocks[:-1]], axis=0)
    after = jnp.concatenate([blocks[1:], zero], axis=0)
    return jnp.stack([before, blocks, after], axis=1)


def reference(values, leaf_basis, transfer, local_coupling, coupling_source, near_field, near_source, upper_transfer, upper_coupling, top_coupling):
    f32 = jnp.float32
    bf16 = jnp.bfloat16
    devs = N_BRANCH * N_LEAF
    rows = 2 * LEAF_DEV - 2
    xv = values.reshape(2, RHS, devs, LEAF_DEV, LS)
    basis = leaf_basis.reshape(devs, LEAF_DEV, LS, R)
    trans = transfer.reshape(devs, rows, R, R)
    coef = jnp.einsum('grplq,plqk->plgrk', xv.astype(f32), basis.astype(f32)).astype(bf16)
    levels = [coef]
    begin = 0
    for level in range(1, LOG_LEAF + 1):
        count = LEAF_DEV >> (level - 1)
        part = jnp.einsum('pcgrk,pckm->pcgrm', levels[-1].astype(f32), trans[:, begin:begin + count].astype(f32))
        part = part.reshape(devs, count // 2, 2, 2, RHS, R)
        levels.append((part[:, :, 0] + part[:, :, 1]).astype(bf16))
        begin += count
    roots = levels[-1][:, 0]
    depth = N_LEAF.bit_length() - 1
    current = roots.reshape(N_BRANCH, N_LEAF, 2, RHS, R)
    uppers = [current]
    offsets = []
    for step in range(1, depth + 1):
        count = N_LEAF >> (step - 1)
        offset = 2 * N_LEAF - 2 * count
        offsets.append(offset)
        part = jnp.einsum('bjgrk,bjkm->bjgrm', current.astype(f32), upper_transfer[:, offset:offset + count].astype(f32))
        part = part.reshape(N_BRANCH, count // 2, 2, 2, RHS, R)
        current = (part[:, :, 0] + part[:, :, 1]).astype(bf16)
        uppers.append(current)
    subtree_roots = current[:, 0]
    order = (jnp.arange(N_BRANCH, dtype=jnp.int32)[:, None] + 1 + jnp.arange(N_BRANCH - 1, dtype=jnp.int32)[None, :]) % N_BRANCH
    others = subtree_roots[order]
    down = jnp.einsum('bjgrm,gbjkm->bgrk', others.astype(f32), top_coupling.astype(f32)).astype(bf16)[:, None]
    for step in range(depth, 0, -1):
        count = N_LEAF >> (step - 1)
        offset = offsets[step - 1]
        child = uppers[step - 1]
        sibling = child.reshape(N_BRANCH, count // 2, 2, 2, RHS, R)[:, :, ::-1].reshape(N_BRANCH, count, 2, RHS, R)
        coupled = jnp.einsum('bjgrm,gbjkm->bjgrk', sibling.astype(f32), upper_coupling[:, :, offset:offset + count].astype(f32))
        parent = jnp.repeat(down, 2, axis=1)
        carried = jnp.einsum('bjgrm,bjkm->bjgrk', parent.astype(f32), upper_transfer[:, offset:offset + count].astype(f32))
        down = (coupled + carried).astype(bf16)
    device_roots = down.reshape(devs, 2, RHS, R)
    stack = jnp.concatenate(levels[:LOG_LEAF], axis=1)
    coef_window = window(stack)
    value_window = window(jnp.moveaxis(xv, 2, 0))
    coupling_all = local_coupling.reshape(2, devs, rows, CPL, R, R)
    sources_all = coupling_source.reshape(devs, rows, CPL)
    near_all = near_field.reshape(2, devs, LEAF_DEV, NEAR, LS, LS)
    near_src_all = near_source.reshape(devs, LEAF_DEV, NEAR)

    def per_device(index):
        win = lax.dynamic_index_in_dim(coef_window, index, 0, keepdims=False)
        couple = lax.dynamic_index_in_dim(coupling_all, index, 1, keepdims=False)
        sources = lax.dynamic_index_in_dim(sources_all, index, 0, keepdims=False)
        mats = lax.dynamic_index_in_dim(trans, index, 0, keepdims=False)
        parent = lax.dynamic_index_in_dim(device_roots, index, 0, keepdims=True)
        for level in range(LOG_LEAF - 1, -1, -1):
            count = LEAF_DEV >> level
            start = 2 * LEAF_DEV - 2 * count
            rows_win = win[:, start:start + count].reshape(3 * count, 2, RHS, R)
            picked = rows_win[sources[start:start + count]]
            coupled = jnp.einsum('cjgrm,gcjkm->cgrk', picked.astype(f32), couple[:, start:start + count].astype(f32))
            carried = jnp.einsum('cgrm,ckm->cgrk', jnp.repeat(parent, 2, axis=0).astype(f32), mats[start:start + count].astype(f32))
            parent = (coupled + carried).astype(bf16)
        own_basis = lax.dynamic_index_in_dim(basis, index, 0, keepdims=False)
        far = jnp.einsum('lgrk,lqk->grlq', parent.astype(f32), own_basis.astype(f32))
        xw = lax.dynamic_index_in_dim(value_window, index, 0, keepdims=False)
        cells = jnp.transpose(xw, (1, 2, 0, 3, 4)).reshape(2, RHS, 3 * LEAF_DEV, LS)
        near_src = lax.dynamic_index_in_dim(near_src_all, index, 0, keepdims=False)
        picked_cells = cells[:, :, near_src]
        blocks = lax.dynamic_index_in_dim(near_all, index, 1, keepdims=False)
        near = jnp.einsum('grljq,gljpq->grlp', picked_cells.astype(f32), blocks.astype(f32))
        return (far + near).reshape(2, RHS, LEAF_DEV * LS)

    outputs = lax.map(per_device, jnp.arange(devs, dtype=jnp.int32))
    return jnp.transpose(outputs, (1, 2, 0, 3)).reshape(2, RHS, devs * LEAF_DEV * LS)
```

```python
import functools

import jax
import jax.numpy as jnp
from jax import lax
from jax.experimental import pallas as pl
from jax.experimental.pallas import tpu as pltpu
from jax.sharding import PartitionSpec as P

f32 = jnp.float32
bf16 = jnp.bfloat16
R = 64
RHS = 16
LEAVES = 8
LOCAL = 14
ROWS = 22
DEPTH = 5
N_LEAF = 32
N_BRANCH = 8
LINKS = 12
ANY = pl.BlockSpec(memory_space=pl.ANY)
VMEM = pl.BlockSpec(memory_space=pltpu.VMEM)
SMEM = pl.BlockSpec(memory_space=pltpu.SMEM)


def dot(a, b):
    return jnp.dot(a, b, preferred_element_type=f32)


def dot_nt(a, b):
    return lax.dot_general(a, b, (((1,), (1,)), ((), ())), preferred_element_type=f32)


def turned(v):
    return jnp.concatenate([v[:, R:], v[:, :R]], axis=1)


def packed(c):
    return jnp.concatenate([c[:RHS], c[RHS:]], axis=1)


def upper_index(leaf, step):
    return 2 * N_LEAF - 2 * (N_LEAF >> step) + jnp.right_shift(leaf, step)


def up_kernel(values, basis, transfer, upper, rows, chain, fan, vals, bas, tra, upp, sem):
    leaf = lax.axis_index("leaf")
    copies = [
        pltpu.make_async_copy(values, vals, sem.at[0]),
        pltpu.make_async_copy(basis, bas, sem.at[1]),
        pltpu.make_async_copy(transfer, tra, sem.at[2]),
    ]
    for step in range(DEPTH):
        copies.append(
            pltpu.make_async_copy(
                upper.at[0, upper_index(leaf, step)], upp.at[step], sem.at[3 + step]
            )
        )
    for copy in copies:
        copy.start()
    copies[0].wait()
    left = lax.broadcasted_iota(jnp.int32, (RHS, 2 * R), 1) < R
    cells = []
    for pair in range(LEAVES // 2):
        x0 = vals[0, :, pl.ds(pair * 2 * R, 2 * R)]
        x1 = vals[1, :, pl.ds(pair * 2 * R, 2 * R)]
        y0, y1 = turned(x0), turned(x1)
        rows[2 * pair] = jnp.where(left, x0, y1)
        rows[2 * pair + 1] = jnp.where(left, y0, x1)
        cells.append(jnp.concatenate([x0[:, :R], x1[:, :R]], axis=0))
        cells.append(jnp.concatenate([y0[:, :R], y1[:, :R]], axis=0))
    copies[1].wait()
    coefs = [dot(cells[i], bas[i]).astype(bf16) for i in range(LEAVES)]
    copies[2].wait()
    begin, place = 0, LEAVES
    while len(coefs) > 1:
        for i, c in enumerate(coefs):
            rows[place + i] = packed(c)
        place += len(coefs)
        merged = [
            (
                dot(coefs[i], tra[begin + i]) + dot(coefs[i + 1], tra[begin + i + 1])
            ).astype(bf16)
            for i in range(0, len(coefs), 2)
        ]
        begin += len(coefs)
        coefs = merged
    coef = coefs[0]
    for step in range(DEPTH):
        chain[step] = packed(coef)
        copies[3 + step].wait()
        coef = dot(coef, upp[step]).astype(bf16)
    top = packed(coef)
    for b in range(N_BRANCH):
        fan[b] = top


def up_call(values, basis, transfer, upper):
    return pl.pallas_call(
        up_kernel,
        out_shape=[
            jax.ShapeDtypeStruct((ROWS, RHS, 2 * R), bf16),
            jax.ShapeDtypeStruct((DEPTH, RHS, 2 * R), bf16),
            jax.ShapeDtypeStruct((N_BRANCH, RHS, 2 * R), bf16),
        ],
        in_specs=[ANY] * 4,
        out_specs=[VMEM] * 3,
        scratch_shapes=[
            pltpu.VMEM((2, RHS, LEAVES * R), bf16),
            pltpu.VMEM((LEAVES, R, R), bf16),
            pltpu.VMEM((LOCAL, R, R), bf16),
            pltpu.VMEM((DEPTH, R, R), bf16),
            pltpu.SemaphoreType.DMA((3 + DEPTH,)),
        ],
        compiler_params=pltpu.CompilerParams(vmem_limit_bytes=56 * 2**20),
        name="up",
    )(values, basis, transfer, upper)


def prep_kernel(upper, couple, top, basis, transfer, over, fold, leafs, upp, cou, tops, sem):
    leaf = lax.axis_index("leaf")
    copies = []
    for step in range(DEPTH):
        index = upper_index(leaf, step)
        copies.append(pltpu.make_async_copy(upper.at[0, index], upp.at[step], sem.at[step]))
        copies.append(
            pltpu.make_async_copy(couple.at[:, 0, index], cou.at[step], sem.at[DEPTH + step])
        )
    last = pltpu.make_async_copy(top, tops, sem.at[2 * DEPTH])
    for copy in copies:
        copy.start()
    last.start()
    zero = jnp.zeros((R, R), bf16)
    tops2 = [transfer[12 + t] for t in range(2)]
    tops1 = [dot(transfer[8 + t], tops2[t // 2]).astype(bf16) for t in range(4)]
    tops0 = [dot(transfer[t], tops1[t // 2]).astype(bf16) for t in range(8)]
    for t in range(LEAVES):
        full = dot(basis[t], tops0[t]).astype(bf16)
        leafs[pl.ds(t * R, R), :] = jnp.concatenate([full, zero], axis=1)
        leafs[pl.ds((LEAVES + t) * R, R), :] = jnp.concatenate([zero, full], axis=1)
    for copy in copies:
        copy.wait()
    down = None
    for step in range(DEPTH + 1):
        lanes = pl.ds(step * 2 * R, 2 * R)
        for g in range(2):
            if step == DEPTH:
                mat = down
            elif step == 0:
                mat = cou[step, g]
            else:
                mat = dot(down, cou[step, g]).astype(bf16)
            pair = [mat, zero] if g == 0 else [zero, mat]
            fold[pl.ds(g * R, R), lanes] = jnp.concatenate(pair, axis=1)
        if step < DEPTH:
            down = upp[0] if step == 0 else dot(down, upp[step]).astype(bf16)
    last.wait()
    for i in range(N_BRANCH - 1):
        lanes = pl.ds(i * 2 * R, 2 * R)
        over[pl.ds(0, R), lanes] = jnp.concatenate([tops[0, 0, i], zero], axis=1)
        over[pl.ds(R, R), lanes] = jnp.concatenate([zero, tops[1, 0, i]], axis=1)


def prep_call(upper, couple, top, basis, transfer):
    return pl.pallas_call(
        prep_kernel,
        out_shape=[
            jax.ShapeDtypeStruct((2 * R, (N_BRANCH - 1) * 2 * R), bf16),
            jax.ShapeDtypeStruct((2 * R, (DEPTH + 1) * 2 * R), bf16),
            jax.ShapeDtypeStruct((2 * LEAVES * R, 2 * R), bf16),
        ],
        in_specs=[ANY] * 3 + [VMEM] * 2,
        out_specs=[VMEM] * 3,
        scratch_shapes=[
            pltpu.VMEM((DEPTH, R, R), bf16),
            pltpu.VMEM((DEPTH, 2, R, R), bf16),
            pltpu.VMEM((2, 1, N_BRANCH - 1, R, R), bf16),
            pltpu.SemaphoreType.DMA((2 * DEPTH + 1,)),
        ],
        compiler_params=pltpu.CompilerParams(vmem_limit_bytes=8 * 2**20),
        cost_estimate=pl.CostEstimate(
            flops=10**8, bytes_accessed=4 * 10**6, transcendentals=0
        ),
        name="prep",
    )(upper, couple, top, basis, transfer)


def mid_kernel(roots, over, chain, out):
    leaf = lax.axis_index("leaf")
    branch = lax.axis_index("branch")
    others = [roots[(branch + 1 + i) % N_BRANCH] for i in range(N_BRANCH - 1)]
    part = dot_nt(jnp.concatenate(others, axis=1), over[...]).astype(bf16)
    for i in range(N_LEAF):
        to = jnp.bitwise_xor(leaf, i)
        out[to, 0] = chain[max(i.bit_length() - 1, 0)]
        out[to, 1] = part


def mid_call(roots, over, chain):
    return pl.pallas_call(
        mid_kernel,
        out_shape=jax.ShapeDtypeStruct((N_LEAF, 2, RHS, 2 * R), bf16),
        in_specs=[VMEM] * 3,
        out_specs=VMEM,
        compiler_params=pltpu.CompilerParams(vmem_limit_bytes=8 * 2**20),
        name="mid",
    )(roots, over, chain)


def local_kernel(
    own, before, after, coupling_source, near_source, coupling, near, transfer, basis,
    base, wide, sums, cells,
):
    left = lax.broadcasted_iota(jnp.int32, (RHS, 2 * R), 1) < R
    for part, ref in enumerate((before, own, after)):
        for row in range(ROWS):
            v = ref[row]
            s = turned(v)
            wide[0, part * ROWS + row] = jnp.where(left, v, s)
            wide[1, part * ROWS + row] = jnp.where(left, s, v)

    def block(picked, mats):
        result = []
        for g in range(2):
            acc = jnp.zeros((RHS, R), f32)
            for j in range(0, LINKS, 4):
                v = jnp.concatenate(
                    [
                        jnp.where(left, wide[g, picked[j]], wide[g, picked[j + 1]]),
                        jnp.where(left, wide[g, picked[j + 2]], wide[g, picked[j + 3]]),
                    ],
                    axis=1,
                )
                m = jnp.concatenate([mats(g, j + n) for n in range(4)], axis=1)
                acc += dot_nt(v, m)
            result.append(acc)
        return jnp.concatenate(result, axis=0)

    def near_body(t, carry):
        picked = []
        for j in range(LINKS):
            s = near_source[t, j]
            picked.append(jnp.right_shift(s, 3) * ROWS + jnp.bitwise_and(s, 7))
        cells[t] = block(picked, lambda g, j: near[g, t, j])
        return carry

    lax.fori_loop(0, LEAVES, near_body, 0)

    def far_body(log, start, t, carry):
        r = start + t
        picked = []
        for j in range(LINKS):
            s = coupling_source[r, j]
            picked.append(
                jnp.right_shift(s, log) * ROWS
                + LEAVES
                + start
                + jnp.bitwise_and(s, (1 << log) - 1)
            )
        sums[r] = block(picked, lambda g, j: coupling[g, r, j])
        return carry

    for log, start in ((1, 12), (2, 8), (3, 0)):
        lax.fori_loop(0, 1 << log, functools.partial(far_body, log, start), 0)
    up2 = [sums[12 + t].astype(bf16) for t in range(2)]
    up1 = [
        (sums[8 + t] + dot_nt(up2[t // 2], transfer[8 + t])).astype(bf16) for t in range(4)
    ]
    up0 = [(sums[t] + dot_nt(up1[t // 2], transfer[t])).astype(bf16) for t in range(8)]
    full = [cells[t] + dot_nt(up0[t], basis[t]) for t in range(8)]
    for pair in range(LEAVES // 2):
        both = jnp.concatenate([full[2 * pair], full[2 * pair + 1]], axis=1)
        for g in range(2):
            base[g, :, pl.ds(pair * 2 * R, 2 * R)] = both[g * RHS : (g + 1) * RHS]


def local_call(own, before, after, coupling_source, near_source, coupling, near, transfer, basis):
    return pl.pallas_call(
        local_kernel,
        out_shape=jax.ShapeDtypeStruct((2, RHS, LEAVES * R), f32),
        in_specs=[VMEM] * 3 + [SMEM] * 2 + [VMEM] * 4,
        out_specs=VMEM,
        scratch_shapes=[
            pltpu.VMEM((2, 3 * ROWS, RHS, 2 * R), bf16),
            pltpu.VMEM((LOCAL, 2 * RHS, R), f32),
            pltpu.VMEM((LEAVES, 2 * RHS, R), f32),
        ],
        compiler_params=pltpu.CompilerParams(vmem_limit_bytes=24 * 2**20),
        cost_estimate=pl.CostEstimate(
            flops=10**8, bytes_accessed=2 * 10**7, transcendentals=0
        ),
        name="local",
    )(own, before, after, coupling_source, near_source, coupling, near, transfer, basis)


def final_kernel(got, fold, leafs, base, out):
    leaf = lax.axis_index("leaf")
    parts = []
    for step in range(DEPTH):
        total = None
        for i in range(1 << step, 2 << step):
            v = got[jnp.bitwise_xor(leaf, i), 0].astype(f32)
            total = v if total is None else total + v
        parts.append(total.astype(bf16))
    total = got[0, 1].astype(f32)
    for i in range(1, N_LEAF):
        total = total + got[i, 1].astype(f32)
    parts.append(total.astype(bf16))
    target = dot_nt(jnp.concatenate(parts, axis=1), fold[...]).astype(bf16)
    far = dot_nt(target, leafs[...])
    width = LEAVES * R
    for g in range(2):
        out[g] = base[g] + far[:, g * width : (g + 1) * width]


def final_call(got, fold, leafs, base):
    return pl.pallas_call(
        final_kernel,
        out_shape=jax.ShapeDtypeStruct((2, RHS, LEAVES * R), f32),
        in_specs=[VMEM] * 4,
        out_specs=VMEM,
        compiler_params=pltpu.CompilerParams(vmem_limit_bytes=8 * 2**20),
        name="final",
    )(got, fold, leafs, base)


def per_device(
    values,
    leaf_basis,
    transfer,
    local_coupling,
    coupling_source,
    near_field,
    near_source,
    upper_transfer,
    upper_coupling,
    top_coupling,
):
    rows, chain, fan = up_call(values, leaf_basis, transfer, upper_transfer)
    roots = lax.all_to_all(fan, "branch", 0, 0, tiled=True)
    last = N_BRANCH * N_LEAF - 1
    ring = ("branch", "leaf")
    before = lax.ppermute(rows, ring, [(i, i + 1) for i in range(last)])
    after = lax.ppermute(rows, ring, [(i + 1, i) for i in range(last)])
    over, fold, leafs = prep_call(
        upper_transfer, upper_coupling, top_coupling, leaf_basis, transfer
    )
    sent = mid_call(roots, over, chain)
    got = lax.all_to_all(sent, "leaf", 0, 0, tiled=True)
    base = local_call(
        rows, before, after, coupling_source, near_source, local_coupling, near_field,
        transfer, leaf_basis,
    )
    return final_call(got, fold, leafs, base)


def solution(mesh):
    in_specs = (
        P(None, None, ("branch", "leaf")),
        P(("branch", "leaf"), None, None),
        P(("branch", "leaf"), None, None),
        P(None, ("branch", "leaf"), None, None, None),
        P(("branch", "leaf"), None),
        P(None, ("branch", "leaf"), None, None, None),
        P(("branch", "leaf"), None),
        P("branch", None, None, None),
        P(None, "branch", None, None, None),
        P(None, "branch", None, None, None),
    )
    out_specs = P(None, None, ("branch", "leaf"))
    return jax.shard_map(
        per_device, mesh=mesh, in_specs=in_specs, out_specs=out_specs, check_vma=False
    )
```

```python
import functools

import jax
import jax.numpy as jnp
from jax import lax
from jax.experimental import pallas as pl
from jax.experimental.pallas import tpu as pltpu
from jax.sharding import PartitionSpec as P

f32 = jnp.float32
bf16 = jnp.bfloat16
R = 64
RHS = 16
LEAVES = 8
LOCAL = 14
ROWS = 22
DEPTH = 5
N_LEAF = 32
N_BRANCH = 8
LINKS = 12
ANY = pl.BlockSpec(memory_space=pl.ANY)
VMEM = pl.BlockSpec(memory_space=pltpu.VMEM)
MB = 2**20


def hbm(*arrays):
    return [pltpu.with_memory_space_constraint(a, pltpu.HBM) for a in arrays]


def dot(a, b):
    return jnp.dot(a, b, preferred_element_type=f32)


def dot_nt(a, b):
    return lax.dot_general(a, b, (((1,), (1,)), ((), ())), preferred_element_type=f32)


def turned(v):
    return jnp.concatenate([v[:, R:], v[:, :R]], axis=1)


def packed(c):
    return jnp.concatenate([c[:RHS], c[RHS:]], axis=1)


def upper_index(leaf, step):
    return 2 * N_LEAF - 2 * (N_LEAF >> step) + jnp.right_shift(leaf, step)


def up_kernel(values, basis, transfer, upper, rows, chain, fan, vals, bas, tra, upp, sem):
    leaf = lax.axis_index("leaf")
    copies = [
        pltpu.make_async_copy(values, vals, sem.at[0]),
        pltpu.make_async_copy(basis, bas, sem.at[1]),
        pltpu.make_async_copy(transfer, tra, sem.at[2]),
    ]
    for step in range(DEPTH):
        copies.append(
            pltpu.make_async_copy(
                upper.at[0, upper_index(leaf, step)], upp.at[step], sem.at[3 + step]
            )
        )
    for copy in copies:
        copy.start()
    copies[0].wait()
    left = lax.broadcasted_iota(jnp.int32, (RHS, 2 * R), 1) < R
    cells = []
    for pair in range(LEAVES // 2):
        x0 = vals[0, :, pl.ds(pair * 2 * R, 2 * R)]
        x1 = vals[1, :, pl.ds(pair * 2 * R, 2 * R)]
        y0, y1 = turned(x0), turned(x1)
        rows[2 * pair] = jnp.where(left, x0, y1)
        rows[2 * pair + 1] = jnp.where(left, y0, x1)
        cells.append(jnp.concatenate([x0[:, :R], x1[:, :R]], axis=0))
        cells.append(jnp.concatenate([y0[:, :R], y1[:, :R]], axis=0))
    copies[1].wait()
    coefs = [dot(cells[i], bas[i]).astype(bf16) for i in range(LEAVES)]
    copies[2].wait()
    begin, place = 0, LEAVES
    while len(coefs) > 1:
        for i, c in enumerate(coefs):
            rows[place + i] = packed(c)
        place += len(coefs)
        merged = [
            (
                dot(coefs[i], tra[begin + i]) + dot(coefs[i + 1], tra[begin + i + 1])
            ).astype(bf16)
            for i in range(0, len(coefs), 2)
        ]
        begin += len(coefs)
        coefs = merged
    coef = coefs[0]
    for step in range(DEPTH):
        chain[step] = packed(coef)
        copies[3 + step].wait()
        coef = dot(coef, upp[step]).astype(bf16)
    top = packed(coef)
    for b in range(N_BRANCH):
        fan[b] = top


def up_call(values, basis, transfer, upper):
    return pl.pallas_call(
        up_kernel,
        out_shape=[
            pltpu.VMEM((ROWS, RHS, 2 * R), bf16),
            pltpu.VMEM((DEPTH, RHS, 2 * R), bf16),
            pltpu.VMEM((N_BRANCH, RHS, 2 * R), bf16),
        ],
        in_specs=[ANY] * 4,
        out_specs=[VMEM] * 3,
        scratch_shapes=[
            pltpu.VMEM((2, RHS, LEAVES * R), bf16),
            pltpu.VMEM((LEAVES, R, R), bf16),
            pltpu.VMEM((LOCAL, R, R), bf16),
            pltpu.VMEM((DEPTH, R, R), bf16),
            pltpu.SemaphoreType.DMA((3 + DEPTH,)),
        ],
        compiler_params=pltpu.CompilerParams(vmem_limit_bytes=8 * MB),
        name="up",
    )(*hbm(values, basis, transfer, upper))


def prep_kernel(
    upper, couple, top, basis, transfer, over, fold, leafs, upp, cou, tops, bas, tra, sem
):
    leaf = lax.axis_index("leaf")
    copies = []
    for step in range(DEPTH):
        index = upper_index(leaf, step)
        copies.append(pltpu.make_async_copy(upper.at[0, index], upp.at[step], sem.at[step]))
        copies.append(
            pltpu.make_async_copy(couple.at[:, 0, index], cou.at[step], sem.at[DEPTH + step])
        )
    last = pltpu.make_async_copy(top, tops, sem.at[2 * DEPTH])
    first = [
        pltpu.make_async_copy(transfer, tra, sem.at[2 * DEPTH + 1]),
        pltpu.make_async_copy(basis, bas, sem.at[2 * DEPTH + 2]),
    ]
    for copy in first + copies + [last]:
        copy.start()
    zero = jnp.zeros((R, R), bf16)
    for copy in first:
        copy.wait()
    tops2 = [tra[12 + t] for t in range(2)]
    tops1 = [dot(tra[8 + t], tops2[t // 2]).astype(bf16) for t in range(4)]
    tops0 = [dot(tra[t], tops1[t // 2]).astype(bf16) for t in range(8)]
    for t in range(LEAVES):
        full = dot(bas[t], tops0[t]).astype(bf16)
        leafs[pl.ds(t * R, R), :] = jnp.concatenate([full, zero], axis=1)
        leafs[pl.ds((LEAVES + t) * R, R), :] = jnp.concatenate([zero, full], axis=1)
    for copy in copies:
        copy.wait()
    down = None
    for step in range(DEPTH + 1):
        lanes = pl.ds(step * 2 * R, 2 * R)
        for g in range(2):
            if step == DEPTH:
                mat = down
            elif step == 0:
                mat = cou[step, g]
            else:
                mat = dot(down, cou[step, g]).astype(bf16)
            pair = [mat, zero] if g == 0 else [zero, mat]
            fold[pl.ds(g * R, R), lanes] = jnp.concatenate(pair, axis=1)
        if step < DEPTH:
            down = upp[0] if step == 0 else dot(down, upp[step]).astype(bf16)
    last.wait()
    for i in range(N_BRANCH - 1):
        lanes = pl.ds(i * 2 * R, 2 * R)
        over[pl.ds(0, R), lanes] = jnp.concatenate([tops[0, 0, i], zero], axis=1)
        over[pl.ds(R, R), lanes] = jnp.concatenate([zero, tops[1, 0, i]], axis=1)


def prep_call(upper, couple, top, basis, transfer):
    return pl.pallas_call(
        prep_kernel,
        out_shape=[
            pltpu.VMEM((2 * R, (N_BRANCH - 1) * 2 * R), bf16),
            pltpu.VMEM((2 * R, (DEPTH + 1) * 2 * R), bf16),
            pltpu.VMEM((2 * LEAVES * R, 2 * R), bf16),
        ],
        in_specs=[ANY] * 5,
        out_specs=[VMEM] * 3,
        scratch_shapes=[
            pltpu.VMEM((DEPTH, R, R), bf16),
            pltpu.VMEM((DEPTH, 2, R, R), bf16),
            pltpu.VMEM((2, 1, N_BRANCH - 1, R, R), bf16),
            pltpu.VMEM((LEAVES, R, R), bf16),
            pltpu.VMEM((LOCAL, R, R), bf16),
            pltpu.SemaphoreType.DMA((2 * DEPTH + 3,)),
        ],
        compiler_params=pltpu.CompilerParams(vmem_limit_bytes=8 * MB),
        cost_estimate=pl.CostEstimate(
            flops=10**8, bytes_accessed=4 * 10**6, transcendentals=0
        ),
        name="prep",
    )(*hbm(upper, couple, top, basis, transfer))


def mid_kernel(roots, over, chain, out):
    leaf = lax.axis_index("leaf")
    branch = lax.axis_index("branch")
    others = [roots[(branch + 1 + i) % N_BRANCH] for i in range(N_BRANCH - 1)]
    part = dot_nt(jnp.concatenate(others, axis=1), over[...]).astype(bf16)
    for i in range(N_LEAF):
        to = jnp.bitwise_xor(leaf, i)
        out[to, 0] = chain[max(i.bit_length() - 1, 0)]
        out[to, 1] = part


def mid_call(roots, over, chain):
    return pl.pallas_call(
        mid_kernel,
        out_shape=pltpu.VMEM((N_LEAF, 2, RHS, 2 * R), bf16),
        in_specs=[VMEM] * 3,
        out_specs=VMEM,
        compiler_params=pltpu.CompilerParams(vmem_limit_bytes=8 * MB),
        name="mid",
    )(roots, over, chain)


def local_kernel(
    own, before, after, coupling, near, coupling_source, near_source, transfer, basis,
    base, wide, sums, cells, nea, cosrc, nesrc, tra, bas, sem,
):
    fields = [pltpu.make_async_copy(near.at[g], nea.at[g], sem.at[4 + g]) for g in range(2)]
    copies = [
        pltpu.make_async_copy(near_source, nesrc, sem.at[0]),
        pltpu.make_async_copy(coupling_source, cosrc, sem.at[1]),
        pltpu.make_async_copy(transfer, tra, sem.at[2]),
        pltpu.make_async_copy(basis, bas, sem.at[3]),
    ]
    for copy in copies + fields:
        copy.start()
    left = lax.broadcasted_iota(jnp.int32, (RHS, 2 * R), 1) < R
    for part, ref in enumerate((before, own, after)):
        for row in range(ROWS):
            v = ref[row]
            s = turned(v)
            wide[0, part * ROWS + row] = jnp.where(left, v, s)
            wide[1, part * ROWS + row] = jnp.where(left, s, v)

    def block(picked, mats):
        result = []
        for g in range(2):
            acc = jnp.zeros((RHS, R), f32)
            for j in range(0, LINKS, 4):
                v = jnp.concatenate(
                    [
                        jnp.where(left, wide[g, picked[j]], wide[g, picked[j + 1]]),
                        jnp.where(left, wide[g, picked[j + 2]], wide[g, picked[j + 3]]),
                    ],
                    axis=1,
                )
                m = jnp.concatenate([mats(g, j + n) for n in range(4)], axis=1)
                acc += dot_nt(v, m)
            result.append(acc)
        return jnp.concatenate(result, axis=0)

    for copy in copies:
        copy.wait()

    def far_body(log, start, t, carry):
        r = start + t
        picked = []
        for j in range(LINKS):
            s = cosrc[r, j]
            picked.append(
                jnp.right_shift(s, log) * ROWS
                + LEAVES
                + start
                + jnp.bitwise_and(s, (1 << log) - 1)
            )
        sums[r] = block(picked, lambda g, j: coupling[g, r, j])
        return carry

    for log, start in ((1, 12), (2, 8), (3, 0)):
        lax.fori_loop(0, 1 << log, functools.partial(far_body, log, start), 0)

    def near_body(t, carry):
        picked = []
        for j in range(LINKS):
            s = nesrc[t, j]
            picked.append(jnp.right_shift(s, 3) * ROWS + jnp.bitwise_and(s, 7))
        cells[t] = block(picked, lambda g, j: nea[g, t, j])
        return carry

    for field in fields:
        field.wait()
    lax.fori_loop(0, LEAVES, near_body, 0)
    up2 = [sums[12 + t].astype(bf16) for t in range(2)]
    up1 = [
        (sums[8 + t] + dot_nt(up2[t // 2], tra[8 + t])).astype(bf16) for t in range(4)
    ]
    up0 = [(sums[t] + dot_nt(up1[t // 2], tra[t])).astype(bf16) for t in range(8)]
    full = [cells[t] + dot_nt(up0[t], bas[t]) for t in range(8)]
    for pair in range(LEAVES // 2):
        both = jnp.concatenate([full[2 * pair], full[2 * pair + 1]], axis=1)
        for g in range(2):
            base[g, :, pl.ds(pair * 2 * R, 2 * R)] = both[g * RHS : (g + 1) * RHS]


def local_call(own, before, after, coupling_source, near_source, coupling, near, transfer, basis):
    return pl.pallas_call(
        local_kernel,
        out_shape=pltpu.VMEM((2, RHS, LEAVES * R), f32),
        in_specs=[VMEM] * 4 + [ANY] * 5,
        out_specs=VMEM,
        scratch_shapes=[
            pltpu.VMEM((2, 3 * ROWS, RHS, 2 * R), bf16),
            pltpu.VMEM((LOCAL, 2 * RHS, R), f32),
            pltpu.VMEM((LEAVES, 2 * RHS, R), f32),
            pltpu.VMEM((2, LEAVES, LINKS, R, R), bf16),
            pltpu.SMEM((LOCAL, LINKS), jnp.int32),
            pltpu.SMEM((LEAVES, LINKS), jnp.int32),
            pltpu.VMEM((LOCAL, R, R), bf16),
            pltpu.VMEM((LEAVES, R, R), bf16),
            pltpu.SemaphoreType.DMA((6,)),
        ],
        compiler_params=pltpu.CompilerParams(vmem_limit_bytes=24 * MB),
        cost_estimate=pl.CostEstimate(
            flops=10**8, bytes_accessed=2 * 10**7, transcendentals=0
        ),
        name="local",
    )(
        own, before, after, coupling,
        *hbm(near, coupling_source, near_source, transfer, basis),
    )


def final_kernel(got, fold, leafs, base, out):
    leaf = lax.axis_index("leaf")
    parts = []
    for step in range(DEPTH):
        total = None
        for i in range(1 << step, 2 << step):
            v = got[jnp.bitwise_xor(leaf, i), 0].astype(f32)
            total = v if total is None else total + v
        parts.append(total.astype(bf16))
    total = got[0, 1].astype(f32)
    for i in range(1, N_LEAF):
        total = total + got[i, 1].astype(f32)
    parts.append(total.astype(bf16))
    target = dot_nt(jnp.concatenate(parts, axis=1), fold[...]).astype(bf16)
    far = dot_nt(target, leafs[...])
    width = LEAVES * R
    for g in range(2):
        out[g] = base[g] + far[:, g * width : (g + 1) * width]


def final_call(got, fold, leafs, base):
    return pl.pallas_call(
        final_kernel,
        out_shape=jax.ShapeDtypeStruct((2, RHS, LEAVES * R), f32),
        in_specs=[VMEM] * 4,
        out_specs=VMEM,
        compiler_params=pltpu.CompilerParams(vmem_limit_bytes=8 * MB),
        name="final",
    )(got, fold, leafs, base)


def per_device(
    values,
    leaf_basis,
    transfer,
    local_coupling,
    coupling_source,
    near_field,
    near_source,
    upper_transfer,
    upper_coupling,
    top_coupling,
):
    rows, chain, fan = up_call(values, leaf_basis, transfer, upper_transfer)
    roots = lax.all_to_all(fan, "branch", 0, 0, tiled=True)
    last = N_BRANCH * N_LEAF - 1
    ring = ("branch", "leaf")
    before = lax.ppermute(rows, ring, [(i, i + 1) for i in range(last)])
    after = lax.ppermute(rows, ring, [(i + 1, i) for i in range(last)])
    over, fold, leafs = prep_call(
        upper_transfer, upper_coupling, top_coupling, leaf_basis, transfer
    )
    roots, before, after = lax.optimization_barrier((roots, before, after))
    sent = mid_call(roots, over, chain)
    got = lax.all_to_all(sent, "leaf", 0, 0, tiled=True)
    base = local_call(
        rows, before, after, coupling_source, near_source, local_coupling, near_field,
        transfer, leaf_basis,
    )
    return final_call(got, fold, leafs, base)


def solution(mesh):
    in_specs = (
        P(None, None, ("branch", "leaf")),
        P(("branch", "leaf"), None, None),
        P(("branch", "leaf"), None, None),
        P(None, ("branch", "leaf"), None, None, None),
        P(("branch", "leaf"), None),
        P(None, ("branch", "leaf"), None, None, None),
        P(("branch", "leaf"), None),
        P("branch", None, None, None),
        P(None, "branch", None, None, None),
        P(None, "branch", None, None, None),
    )
    out_specs = P(None, None, ("branch", "leaf"))
    return jax.shard_map(
        per_device, mesh=mesh, in_specs=in_specs, out_specs=out_specs, check_vma=False
    )
```

```python
import functools

import jax
import jax.numpy as jnp
from jax import lax
from jax.experimental import pallas as pl
from jax.experimental.pallas import tpu as pltpu
from jax.sharding import PartitionSpec as P

f32 = jnp.float32
bf16 = jnp.bfloat16
R = 64
RHS = 16
LEAVES = 8
LOCAL = 14
ROWS = 22
DEPTH = 5
N_LEAF = 32
N_BRANCH = 8
LINKS = 12
UNROLL = 4
ANY = pl.BlockSpec(memory_space=pl.ANY)
VMEM = pl.BlockSpec(memory_space=pltpu.VMEM)
MB = 2**20


def hbm(*arrays):
    return [pltpu.with_memory_space_constraint(a, pltpu.HBM) for a in arrays]


def dot(a, b):
    return jnp.dot(a, b, preferred_element_type=f32)


def dot_nt(a, b):
    return lax.dot_general(a, b, (((1,), (1,)), ((), ())), preferred_element_type=f32)


def turned(v):
    return jnp.concatenate([v[:, R:], v[:, :R]], axis=1)


def packed(c):
    return jnp.concatenate([c[:RHS], c[RHS:]], axis=1)


def upper_index(leaf, step):
    return 2 * N_LEAF - 2 * (N_LEAF >> step) + jnp.right_shift(leaf, step)


def up_kernel(values, basis, transfer, upper, rows, chain, fan, vals, bas, tra, upp, sem):
    leaf = lax.axis_index("leaf")
    copies = [
        pltpu.make_async_copy(values, vals, sem.at[0]),
        pltpu.make_async_copy(basis, bas, sem.at[1]),
        pltpu.make_async_copy(transfer, tra, sem.at[2]),
    ]
    for step in range(DEPTH):
        copies.append(
            pltpu.make_async_copy(
                upper.at[0, upper_index(leaf, step)], upp.at[step], sem.at[3 + step]
            )
        )
    for copy in copies:
        copy.start()
    copies[0].wait()
    left = lax.broadcasted_iota(jnp.int32, (RHS, 2 * R), 1) < R
    cells = []
    for pair in range(LEAVES // 2):
        x0 = vals[0, :, pl.ds(pair * 2 * R, 2 * R)]
        x1 = vals[1, :, pl.ds(pair * 2 * R, 2 * R)]
        y0, y1 = turned(x0), turned(x1)
        rows[2 * pair] = jnp.where(left, x0, y1)
        rows[2 * pair + 1] = jnp.where(left, y0, x1)
        cells.append(jnp.concatenate([x0[:, :R], x1[:, :R]], axis=0))
        cells.append(jnp.concatenate([y0[:, :R], y1[:, :R]], axis=0))
    copies[1].wait()
    coefs = [dot(cells[i], bas[i]).astype(bf16) for i in range(LEAVES)]
    copies[2].wait()
    begin, place = 0, LEAVES
    while len(coefs) > 1:
        for i, c in enumerate(coefs):
            rows[place + i] = packed(c)
        place += len(coefs)
        merged = [
            (
                dot(coefs[i], tra[begin + i]) + dot(coefs[i + 1], tra[begin + i + 1])
            ).astype(bf16)
            for i in range(0, len(coefs), 2)
        ]
        begin += len(coefs)
        coefs = merged
    coef = coefs[0]
    for step in range(DEPTH):
        chain[step] = packed(coef)
        copies[3 + step].wait()
        coef = dot(coef, upp[step]).astype(bf16)
    top = packed(coef)
    for b in range(N_BRANCH):
        fan[b] = top


def up_call(values, basis, transfer, upper):
    return pl.pallas_call(
        up_kernel,
        out_shape=[
            pltpu.VMEM((ROWS, RHS, 2 * R), bf16),
            pltpu.VMEM((DEPTH, RHS, 2 * R), bf16),
            pltpu.VMEM((N_BRANCH, RHS, 2 * R), bf16),
        ],
        in_specs=[ANY] * 4,
        out_specs=[VMEM] * 3,
        scratch_shapes=[
            pltpu.VMEM((2, RHS, LEAVES * R), bf16),
            pltpu.VMEM((LEAVES, R, R), bf16),
            pltpu.VMEM((LOCAL, R, R), bf16),
            pltpu.VMEM((DEPTH, R, R), bf16),
            pltpu.SemaphoreType.DMA((3 + DEPTH,)),
        ],
        compiler_params=pltpu.CompilerParams(vmem_limit_bytes=8 * MB),
        name="up",
    )(*hbm(values, basis, transfer, upper))


def prep_kernel(
    upper, couple, top, basis, transfer, over, fold, leafs, upp, cou, tops, bas, tra, sem
):
    leaf = lax.axis_index("leaf")
    copies = []
    for step in range(DEPTH):
        index = upper_index(leaf, step)
        copies.append(pltpu.make_async_copy(upper.at[0, index], upp.at[step], sem.at[step]))
        copies.append(
            pltpu.make_async_copy(couple.at[:, 0, index], cou.at[step], sem.at[DEPTH + step])
        )
    last = pltpu.make_async_copy(top, tops, sem.at[2 * DEPTH])
    first = [
        pltpu.make_async_copy(transfer, tra, sem.at[2 * DEPTH + 1]),
        pltpu.make_async_copy(basis, bas, sem.at[2 * DEPTH + 2]),
    ]
    for copy in first + copies + [last]:
        copy.start()
    zero = jnp.zeros((R, R), bf16)
    for copy in first:
        copy.wait()
    tops2 = [tra[12 + t] for t in range(2)]
    tops1 = [dot(tra[8 + t], tops2[t // 2]).astype(bf16) for t in range(4)]
    tops0 = [dot(tra[t], tops1[t // 2]).astype(bf16) for t in range(8)]
    for t in range(LEAVES):
        full = dot(bas[t], tops0[t]).astype(bf16)
        leafs[pl.ds(t * R, R), :] = jnp.concatenate([full, zero], axis=1)
        leafs[pl.ds((LEAVES + t) * R, R), :] = jnp.concatenate([zero, full], axis=1)
    for copy in copies:
        copy.wait()
    down = None
    for step in range(DEPTH + 1):
        lanes = pl.ds(step * 2 * R, 2 * R)
        for g in range(2):
            if step == DEPTH:
                mat = down
            elif step == 0:
                mat = cou[step, g]
            else:
                mat = dot(down, cou[step, g]).astype(bf16)
            pair = [mat, zero] if g == 0 else [zero, mat]
            fold[pl.ds(g * R, R), lanes] = jnp.concatenate(pair, axis=1)
        if step < DEPTH:
            down = upp[0] if step == 0 else dot(down, upp[step]).astype(bf16)
    last.wait()
    for i in range(N_BRANCH - 1):
        lanes = pl.ds(i * 2 * R, 2 * R)
        over[pl.ds(0, R), lanes] = jnp.concatenate([tops[0, 0, i], zero], axis=1)
        over[pl.ds(R, R), lanes] = jnp.concatenate([zero, tops[1, 0, i]], axis=1)


def prep_call(upper, couple, top, basis, transfer):
    return pl.pallas_call(
        prep_kernel,
        out_shape=[
            pltpu.VMEM((2 * R, (N_BRANCH - 1) * 2 * R), bf16),
            pltpu.VMEM((2 * R, (DEPTH + 1) * 2 * R), bf16),
            pltpu.VMEM((2 * LEAVES * R, 2 * R), bf16),
        ],
        in_specs=[ANY] * 5,
        out_specs=[VMEM] * 3,
        scratch_shapes=[
            pltpu.VMEM((DEPTH, R, R), bf16),
            pltpu.VMEM((DEPTH, 2, R, R), bf16),
            pltpu.VMEM((2, 1, N_BRANCH - 1, R, R), bf16),
            pltpu.VMEM((LEAVES, R, R), bf16),
            pltpu.VMEM((LOCAL, R, R), bf16),
            pltpu.SemaphoreType.DMA((2 * DEPTH + 3,)),
        ],
        compiler_params=pltpu.CompilerParams(vmem_limit_bytes=8 * MB),
        cost_estimate=pl.CostEstimate(
            flops=10**8, bytes_accessed=4 * 10**6, transcendentals=0
        ),
        name="prep",
    )(*hbm(upper, couple, top, basis, transfer))


def mid_kernel(roots, over, chain, out):
    leaf = lax.axis_index("leaf")
    branch = lax.axis_index("branch")
    others = [roots[(branch + 1 + i) % N_BRANCH] for i in range(N_BRANCH - 1)]
    part = dot_nt(jnp.concatenate(others, axis=1), over[...]).astype(bf16)
    for i in range(N_LEAF):
        to = jnp.bitwise_xor(leaf, i)
        out[to, 0] = chain[max(i.bit_length() - 1, 0)]
        out[to, 1] = part


def mid_call(roots, over, chain):
    return pl.pallas_call(
        mid_kernel,
        out_shape=pltpu.VMEM((N_LEAF, 2, RHS, 2 * R), bf16),
        in_specs=[VMEM] * 3,
        out_specs=VMEM,
        compiler_params=pltpu.CompilerParams(vmem_limit_bytes=8 * MB),
        name="mid",
    )(roots, over, chain)


def local_kernel(
    own, before, after, coupling, near, coupling_source, near_source, transfer, basis,
    base, wide, sums, cells, cou, nea, cosrc, nesrc, tra, bas, sem,
):
    smalls = [
        pltpu.make_async_copy(coupling_source, cosrc, sem.at[0]),
        pltpu.make_async_copy(near_source, nesrc, sem.at[1]),
        pltpu.make_async_copy(transfer, tra, sem.at[2]),
        pltpu.make_async_copy(basis, bas, sem.at[3]),
    ]
    bigs = []
    for n, (source, into, start, count) in enumerate(
        ((coupling, cou, 8, 6), (coupling, cou, 0, 4), (coupling, cou, 4, 4),
         (near, nea, 0, 4), (near, nea, 4, 4))
    ):
        span = pl.ds(start, count)
        bigs.append(pltpu.make_async_copy(source.at[:, span], into.at[:, span], sem.at[4 + n]))
    for copy in smalls[:2] + bigs + smalls[2:]:
        copy.start()
    left = lax.broadcasted_iota(jnp.int32, (RHS, 2 * R), 1) < R
    for part, ref in enumerate((before, own, after)):
        for row in range(ROWS):
            v = ref[row]
            s = turned(v)
            wide[0, part * ROWS + row] = jnp.where(left, v, s)
            wide[1, part * ROWS + row] = jnp.where(left, s, v)

    def block(picked, mats):
        result = []
        for g in range(2):
            acc = None
            for j in range(0, LINKS, 4):
                v = jnp.concatenate(
                    [
                        jnp.where(left, wide[g, picked[j]], wide[g, picked[j + 1]]),
                        jnp.where(left, wide[g, picked[j + 2]], wide[g, picked[j + 3]]),
                    ],
                    axis=1,
                )
                m = jnp.concatenate([mats(g, j + n) for n in range(4)], axis=1)
                part = dot_nt(v, m)
                acc = part if acc is None else acc + part
            result.append(acc)
        return jnp.concatenate(result, axis=0)

    def far_body(log, start, t):
        r = start + t
        picked = []
        for j in range(LINKS):
            s = cosrc[r, j]
            picked.append(
                jnp.right_shift(s, log) * ROWS
                + LEAVES
                + start
                + jnp.bitwise_and(s, (1 << log) - 1)
            )
        sums[r] = block(picked, lambda g, j: cou[g, r, j])

    def near_body(t):
        picked = []
        for j in range(LINKS):
            s = nesrc[t, j]
            picked.append(jnp.right_shift(s, 3) * ROWS + jnp.bitwise_and(s, 7))
        cells[t] = block(picked, lambda g, j: nea[g, t, j])

    def each(body, first, count):
        def step(i, carry):
            body(first + i)
            return carry

        lax.fori_loop(0, count, step, 0, unroll=min(UNROLL, count))

    for copy in smalls[:2]:
        copy.wait()
    bigs[0].wait()
    each(functools.partial(far_body, 1, 12), 0, 2)
    each(functools.partial(far_body, 2, 8), 0, 4)
    bigs[1].wait()
    each(functools.partial(far_body, 3, 0), 0, 4)
    bigs[2].wait()
    each(functools.partial(far_body, 3, 0), 4, 4)
    bigs[3].wait()
    each(near_body, 0, 4)
    bigs[4].wait()
    each(near_body, 4, 4)
    for copy in smalls[2:]:
        copy.wait()
    up2 = [sums[12 + t].astype(bf16) for t in range(2)]
    up1 = [
        (sums[8 + t] + dot_nt(up2[t // 2], tra[8 + t])).astype(bf16) for t in range(4)
    ]
    up0 = [(sums[t] + dot_nt(up1[t // 2], tra[t])).astype(bf16) for t in range(8)]
    full = [cells[t] + dot_nt(up0[t], bas[t]) for t in range(8)]
    for pair in range(LEAVES // 2):
        both = jnp.concatenate([full[2 * pair], full[2 * pair + 1]], axis=1)
        for g in range(2):
            base[g, :, pl.ds(pair * 2 * R, 2 * R)] = both[g * RHS : (g + 1) * RHS]


def local_call(own, before, after, coupling_source, near_source, coupling, near, transfer, basis):
    return pl.pallas_call(
        local_kernel,
        out_shape=pltpu.VMEM((2, RHS, LEAVES * R), f32),
        in_specs=[VMEM] * 3 + [ANY] * 6,
        out_specs=VMEM,
        scratch_shapes=[
            pltpu.VMEM((2, 3 * ROWS, RHS, 2 * R), bf16),
            pltpu.VMEM((LOCAL, 2 * RHS, R), f32),
            pltpu.VMEM((LEAVES, 2 * RHS, R), f32),
            pltpu.VMEM((2, LOCAL, LINKS, R, R), bf16),
            pltpu.VMEM((2, LEAVES, LINKS, R, R), bf16),
            pltpu.SMEM((LOCAL, LINKS), jnp.int32),
            pltpu.SMEM((LEAVES, LINKS), jnp.int32),
            pltpu.VMEM((LOCAL, R, R), bf16),
            pltpu.VMEM((LEAVES, R, R), bf16),
            pltpu.SemaphoreType.DMA((9,)),
        ],
        compiler_params=pltpu.CompilerParams(vmem_limit_bytes=24 * MB),
        cost_estimate=pl.CostEstimate(
            flops=10**8, bytes_accessed=2 * 10**7, transcendentals=0
        ),
        name="local",
    )(
        own, before, after,
        *hbm(coupling, near, coupling_source, near_source, transfer, basis),
    )


def final_kernel(got, fold, leafs, base, out):
    leaf = lax.axis_index("leaf")
    parts = []
    for step in range(DEPTH):
        total = None
        for i in range(1 << step, 2 << step):
            v = got[jnp.bitwise_xor(leaf, i), 0].astype(f32)
            total = v if total is None else total + v
        parts.append(total.astype(bf16))
    total = got[0, 1].astype(f32)
    for i in range(1, N_LEAF):
        total = total + got[i, 1].astype(f32)
    parts.append(total.astype(bf16))
    target = dot_nt(jnp.concatenate(parts, axis=1), fold[...]).astype(bf16)
    far = dot_nt(target, leafs[...])
    width = LEAVES * R
    for g in range(2):
        out[g] = base[g] + far[:, g * width : (g + 1) * width]


def final_call(got, fold, leafs, base):
    return pl.pallas_call(
        final_kernel,
        out_shape=jax.ShapeDtypeStruct((2, RHS, LEAVES * R), f32),
        in_specs=[VMEM] * 4,
        out_specs=VMEM,
        compiler_params=pltpu.CompilerParams(vmem_limit_bytes=8 * MB),
        name="final",
    )(got, fold, leafs, base)


def per_device(
    values,
    leaf_basis,
    transfer,
    local_coupling,
    coupling_source,
    near_field,
    near_source,
    upper_transfer,
    upper_coupling,
    top_coupling,
):
    rows, chain, fan = up_call(values, leaf_basis, transfer, upper_transfer)
    roots = lax.all_to_all(fan, "branch", 0, 0, tiled=True)
    last = N_BRANCH * N_LEAF - 1
    ring = ("branch", "leaf")
    before = lax.ppermute(rows, ring, [(i, i + 1) for i in range(last)])
    after = lax.ppermute(rows, ring, [(i + 1, i) for i in range(last)])
    over, fold, leafs = prep_call(
        upper_transfer, upper_coupling, top_coupling, leaf_basis, transfer
    )
    sent = mid_call(roots, over, chain)
    sent, before, after = lax.optimization_barrier((sent, before, after))
    got = lax.all_to_all(sent, "leaf", 0, 0, tiled=True)
    base = local_call(
        rows, before, after, coupling_source, near_source, local_coupling, near_field,
        transfer, leaf_basis,
    )
    return final_call(got, fold, leafs, base)


def solution(mesh):
    in_specs = (
        P(None, None, ("branch", "leaf")),
        P(("branch", "leaf"), None, None),
        P(("branch", "leaf"), None, None),
        P(None, ("branch", "leaf"), None, None, None),
        P(("branch", "leaf"), None),
        P(None, ("branch", "leaf"), None, None, None),
        P(("branch", "leaf"), None),
        P("branch", None, None, None),
        P(None, "branch", None, None, None),
        P(None, "branch", None, None, None),
    )
    out_specs = P(None, None, ("branch", "leaf"))
    return jax.shard_map(
        per_device, mesh=mesh, in_specs=in_specs, out_specs=out_specs, check_vma=False
    )
```

```python
import functools

import jax
import jax.numpy as jnp
from jax import lax
from jax.experimental import pallas as pl
from jax.experimental.pallas import tpu as pltpu
from jax.sharding import PartitionSpec as P

f32 = jnp.float32
bf16 = jnp.bfloat16
R = 64
RHS = 16
LEAVES = 8
LOCAL = 14
ROWS = 22
DEPTH = 5
N_LEAF = 32
N_BRANCH = 8
LINKS = 12
UNROLL = 4
ANY = pl.BlockSpec(memory_space=pl.ANY)
VMEM = pl.BlockSpec(memory_space=pltpu.VMEM)
MB = 2**20


def hbm(*arrays):
    return [pltpu.with_memory_space_constraint(a, pltpu.HBM) for a in arrays]


def dot(a, b):
    return jnp.dot(a, b, preferred_element_type=f32)


def dot_nt(a, b):
    return lax.dot_general(a, b, (((1,), (1,)), ((), ())), preferred_element_type=f32)


def turned(v):
    return jnp.concatenate([v[:, R:], v[:, :R]], axis=1)


def packed(c):
    return jnp.concatenate([c[:RHS], c[RHS:]], axis=1)


def upper_index(leaf, step):
    return 2 * N_LEAF - 2 * (N_LEAF >> step) + jnp.right_shift(leaf, step)


def up_kernel(
    values, basis, transfer, upper, top, vals, coefs, chain, fan, downs, tops, bas, tra, upp, sem
):
    leaf = lax.axis_index("leaf")
    firsts = [
        pltpu.make_async_copy(
            upper.at[0, upper_index(leaf, step)], upp.at[step], sem.at[4 + step]
        )
        for step in range(DEPTH)
    ]
    firsts += [
        pltpu.make_async_copy(values, vals, sem.at[0]),
        pltpu.make_async_copy(basis, bas, sem.at[1]),
        pltpu.make_async_copy(transfer, tra, sem.at[2]),
    ]
    last = pltpu.make_async_copy(top, tops, sem.at[3])
    for copy in firsts + [last]:
        copy.start()
    for copy in firsts:
        copy.wait()
    down = upp[0]
    downs[0] = down
    for step in range(1, DEPTH):
        down = dot(down, upp[step]).astype(bf16)
        downs[step] = down
    level = []
    for pair in range(LEAVES // 2):
        x0 = vals[0, :, pl.ds(pair * 2 * R, 2 * R)]
        x1 = vals[1, :, pl.ds(pair * 2 * R, 2 * R)]
        for half in range(2):
            lanes = slice(half * R, (half + 1) * R)
            cell = jnp.concatenate([x0[:, lanes], x1[:, lanes]], axis=0)
            level.append(dot(cell, bas[2 * pair + half]).astype(bf16))
    begin = 0
    while len(level) > 1:
        for i, c in enumerate(level):
            coefs[begin + i] = c
        merged = [
            (dot(level[i], tra[begin + i]) + dot(level[i + 1], tra[begin + i + 1])).astype(bf16)
            for i in range(0, len(level), 2)
        ]
        begin += len(level)
        level = merged
    root = level[0]
    chain[0] = packed(root)
    for step in range(1, DEPTH + 1):
        part = packed(dot(root, downs[step - 1]).astype(bf16))
        if step < DEPTH:
            chain[step] = part
        else:
            for b in range(N_BRANCH):
                fan[b] = part
    last.wait()


def up_call(values, basis, transfer, upper, top):
    return pl.pallas_call(
        up_kernel,
        out_shape=[
            pltpu.VMEM((2, RHS, LEAVES * R), bf16),
            pltpu.VMEM((LOCAL, 2 * RHS, R), bf16),
            pltpu.VMEM((DEPTH, RHS, 2 * R), bf16),
            pltpu.VMEM((N_BRANCH, RHS, 2 * R), bf16),
            pltpu.VMEM((DEPTH, R, R), bf16),
            pltpu.VMEM((2, 1, N_BRANCH - 1, R, R), bf16),
        ],
        in_specs=[ANY] * 5,
        out_specs=[VMEM] * 6,
        scratch_shapes=[
            pltpu.VMEM((LEAVES, R, R), bf16),
            pltpu.VMEM((LOCAL, R, R), bf16),
            pltpu.VMEM((DEPTH, R, R), bf16),
            pltpu.SemaphoreType.DMA((4 + DEPTH,)),
        ],
        compiler_params=pltpu.CompilerParams(vmem_limit_bytes=8 * MB),
        name="up",
    )(*hbm(values, basis, transfer, upper, top))


def pack_kernel(vals, coefs, rows):
    left = lax.broadcasted_iota(jnp.int32, (RHS, 2 * R), 1) < R
    for pair in range(LEAVES // 2):
        x0 = vals[0, :, pl.ds(pair * 2 * R, 2 * R)]
        x1 = vals[1, :, pl.ds(pair * 2 * R, 2 * R)]
        rows[2 * pair] = jnp.where(left, x0, turned(x1))
        rows[2 * pair + 1] = jnp.where(left, turned(x0), x1)
    for i in range(LOCAL):
        rows[LEAVES + i] = packed(coefs[i])


def pack_call(vals, coefs):
    return pl.pallas_call(
        pack_kernel,
        out_shape=pltpu.VMEM((ROWS, RHS, 2 * R), bf16),
        in_specs=[VMEM] * 2,
        out_specs=VMEM,
        compiler_params=pltpu.CompilerParams(vmem_limit_bytes=8 * MB),
        cost_estimate=pl.CostEstimate(
            flops=10**8, bytes_accessed=4 * 10**6, transcendentals=0
        ),
        name="pack",
    )(vals, coefs)


def prep_kernel(couple, downs, basis, transfer, fold, leafs, cou, bas, tra, sem):
    leaf = lax.axis_index("leaf")
    copies = [
        pltpu.make_async_copy(transfer, tra, sem.at[DEPTH]),
        pltpu.make_async_copy(basis, bas, sem.at[DEPTH + 1]),
    ]
    for step in range(DEPTH):
        copies.append(
            pltpu.make_async_copy(
                couple.at[:, 0, upper_index(leaf, step)], cou.at[step], sem.at[step]
            )
        )
    for copy in copies:
        copy.start()
    for copy in copies:
        copy.wait()
    zero = jnp.zeros((R, R), bf16)
    tops2 = [tra[12 + t] for t in range(2)]
    tops1 = [dot(tra[8 + t], tops2[t // 2]).astype(bf16) for t in range(4)]
    tops0 = [dot(tra[t], tops1[t // 2]).astype(bf16) for t in range(8)]
    for t in range(LEAVES):
        full = dot(bas[t], tops0[t]).astype(bf16)
        leafs[pl.ds(t * R, R), :] = jnp.concatenate([full, zero], axis=1)
        leafs[pl.ds((LEAVES + t) * R, R), :] = jnp.concatenate([zero, full], axis=1)
    for step in range(DEPTH + 1):
        lanes = pl.ds(step * 2 * R, 2 * R)
        for g in range(2):
            if step == DEPTH:
                mat = downs[DEPTH - 1]
            elif step == 0:
                mat = cou[step, g]
            else:
                mat = dot(downs[step - 1], cou[step, g]).astype(bf16)
            pair = [mat, zero] if g == 0 else [zero, mat]
            fold[pl.ds(g * R, R), lanes] = jnp.concatenate(pair, axis=1)


def prep_call(couple, downs, basis, transfer):
    couple, basis, transfer = hbm(couple, basis, transfer)
    return pl.pallas_call(
        prep_kernel,
        out_shape=[
            pltpu.VMEM((2 * R, (DEPTH + 1) * 2 * R), bf16),
            pltpu.VMEM((2 * LEAVES * R, 2 * R), bf16),
        ],
        in_specs=[ANY, VMEM, ANY, ANY],
        out_specs=[VMEM] * 2,
        scratch_shapes=[
            pltpu.VMEM((DEPTH, 2, R, R), bf16),
            pltpu.VMEM((LEAVES, R, R), bf16),
            pltpu.VMEM((LOCAL, R, R), bf16),
            pltpu.SemaphoreType.DMA((DEPTH + 2,)),
        ],
        compiler_params=pltpu.CompilerParams(vmem_limit_bytes=8 * MB),
        cost_estimate=pl.CostEstimate(
            flops=10**8, bytes_accessed=4 * 10**6, transcendentals=0
        ),
        name="prep",
    )(couple, downs, basis, transfer)


def mid_kernel(roots, tops, chain, out):
    leaf = lax.axis_index("leaf")
    branch = lax.axis_index("branch")
    others = [roots[(branch + 1 + i) % N_BRANCH] for i in range(N_BRANCH - 1)]
    parts = []
    for g in range(2):
        lanes = slice(g * R, (g + 1) * R)
        v = jnp.concatenate([other[:, lanes] for other in others], axis=1)
        m = jnp.concatenate([tops[g, 0, i] for i in range(N_BRANCH - 1)], axis=1)
        parts.append(dot_nt(v, m))
    part = jnp.concatenate(parts, axis=1).astype(bf16)
    for i in range(N_LEAF):
        to = jnp.bitwise_xor(leaf, i)
        out[to, 0] = chain[max(i.bit_length() - 1, 0)]
        out[to, 1] = part


def mid_call(roots, tops, chain):
    return pl.pallas_call(
        mid_kernel,
        out_shape=pltpu.VMEM((N_LEAF, 2, RHS, 2 * R), bf16),
        in_specs=[VMEM] * 3,
        out_specs=VMEM,
        compiler_params=pltpu.CompilerParams(vmem_limit_bytes=8 * MB),
        name="mid",
    )(roots, tops, chain)


def local_kernel(
    own, before, after, coupling, near, coupling_source, near_source, transfer, basis,
    base, wide, sums, cells, cou, nea, cosrc, nesrc, tra, bas, sem,
):
    smalls = [
        pltpu.make_async_copy(coupling_source, cosrc, sem.at[0]),
        pltpu.make_async_copy(near_source, nesrc, sem.at[1]),
        pltpu.make_async_copy(transfer, tra, sem.at[2]),
        pltpu.make_async_copy(basis, bas, sem.at[3]),
    ]
    bigs = []
    for n, (source, into, start, count) in enumerate(
        ((coupling, cou, 8, 6), (coupling, cou, 0, 4), (coupling, cou, 4, 4),
         (near, nea, 0, 4), (near, nea, 4, 4))
    ):
        span = pl.ds(start, count)
        bigs.append(pltpu.make_async_copy(source.at[:, span], into.at[:, span], sem.at[4 + n]))
    for copy in smalls[:2] + bigs + smalls[2:]:
        copy.start()
    left = lax.broadcasted_iota(jnp.int32, (RHS, 2 * R), 1) < R
    for part, ref in enumerate((before, own, after)):
        for row in range(ROWS):
            v = ref[row]
            s = turned(v)
            wide[0, part * ROWS + row] = jnp.where(left, v, s)
            wide[1, part * ROWS + row] = jnp.where(left, s, v)

    def block(picked, mats):
        result = []
        for g in range(2):
            acc = None
            for j in range(0, LINKS, 4):
                v = jnp.concatenate(
                    [
                        jnp.where(left, wide[g, picked[j]], wide[g, picked[j + 1]]),
                        jnp.where(left, wide[g, picked[j + 2]], wide[g, picked[j + 3]]),
                    ],
                    axis=1,
                )
                m = jnp.concatenate([mats(g, j + n) for n in range(4)], axis=1)
                part = dot_nt(v, m)
                acc = part if acc is None else acc + part
            result.append(acc)
        return jnp.concatenate(result, axis=0)

    def far_body(log, start, t):
        r = start + t
        picked = []
        for j in range(LINKS):
            s = cosrc[r, j]
            picked.append(
                jnp.right_shift(s, log) * ROWS
                + LEAVES
                + start
                + jnp.bitwise_and(s, (1 << log) - 1)
            )
        sums[r] = block(picked, lambda g, j: cou[g, r, j])

    def near_body(t):
        picked = []
        for j in range(LINKS):
            s = nesrc[t, j]
            picked.append(jnp.right_shift(s, 3) * ROWS + jnp.bitwise_and(s, 7))
        cells[t] = block(picked, lambda g, j: nea[g, t, j])

    def each(body, first, count):
        def step(i, carry):
            body(first + i)
            return carry

        lax.fori_loop(0, count, step, 0, unroll=min(UNROLL, count))

    for copy in smalls[:2]:
        copy.wait()
    bigs[0].wait()
    each(functools.partial(far_body, 1, 12), 0, 2)
    each(functools.partial(far_body, 2, 8), 0, 4)
    bigs[1].wait()
    each(functools.partial(far_body, 3, 0), 0, 4)
    bigs[2].wait()
    each(functools.partial(far_body, 3, 0), 4, 4)
    bigs[3].wait()
    each(near_body, 0, 4)
    bigs[4].wait()
    each(near_body, 4, 4)
    for copy in smalls[2:]:
        copy.wait()
    up2 = [sums[12 + t].astype(bf16) for t in range(2)]
    up1 = [
        (sums[8 + t] + dot_nt(up2[t // 2], tra[8 + t])).astype(bf16) for t in range(4)
    ]
    up0 = [(sums[t] + dot_nt(up1[t // 2], tra[t])).astype(bf16) for t in range(8)]
    full = [cells[t] + dot_nt(up0[t], bas[t]) for t in range(8)]
    for pair in range(LEAVES // 2):
        both = jnp.concatenate([full[2 * pair], full[2 * pair + 1]], axis=1)
        for g in range(2):
            base[g, :, pl.ds(pair * 2 * R, 2 * R)] = both[g * RHS : (g + 1) * RHS]


def local_call(own, before, after, coupling_source, near_source, coupling, near, transfer, basis):
    return pl.pallas_call(
        local_kernel,
        out_shape=pltpu.VMEM((2, RHS, LEAVES * R), f32),
        in_specs=[VMEM] * 3 + [ANY] * 6,
        out_specs=VMEM,
        scratch_shapes=[
            pltpu.VMEM((2, 3 * ROWS, RHS, 2 * R), bf16),
            pltpu.VMEM((LOCAL, 2 * RHS, R), f32),
            pltpu.VMEM((LEAVES, 2 * RHS, R), f32),
            pltpu.VMEM((2, LOCAL, LINKS, R, R), bf16),
            pltpu.VMEM((2, LEAVES, LINKS, R, R), bf16),
            pltpu.SMEM((LOCAL, LINKS), jnp.int32),
            pltpu.SMEM((LEAVES, LINKS), jnp.int32),
            pltpu.VMEM((LOCAL, R, R), bf16),
            pltpu.VMEM((LEAVES, R, R), bf16),
            pltpu.SemaphoreType.DMA((9,)),
        ],
        compiler_params=pltpu.CompilerParams(vmem_limit_bytes=24 * MB),
        cost_estimate=pl.CostEstimate(
            flops=10**8, bytes_accessed=2 * 10**7, transcendentals=0
        ),
        name="local",
    )(
        own, before, after,
        *hbm(coupling, near, coupling_source, near_source, transfer, basis),
    )


def final_kernel(got, fold, leafs, base, out):
    leaf = lax.axis_index("leaf")
    parts = []
    for step in range(DEPTH):
        total = None
        for i in range(1 << step, 2 << step):
            v = got[jnp.bitwise_xor(leaf, i), 0].astype(f32)
            total = v if total is None else total + v
        parts.append(total.astype(bf16))
    total = got[0, 1].astype(f32)
    for i in range(1, N_LEAF):
        total = total + got[i, 1].astype(f32)
    parts.append(total.astype(bf16))
    target = dot_nt(jnp.concatenate(parts, axis=1), fold[...]).astype(bf16)
    far = dot_nt(target, leafs[...])
    width = LEAVES * R
    for g in range(2):
        out[g] = base[g] + far[:, g * width : (g + 1) * width]


def final_call(got, fold, leafs, base):
    return pl.pallas_call(
        final_kernel,
        out_shape=jax.ShapeDtypeStruct((2, RHS, LEAVES * R), f32),
        in_specs=[VMEM] * 4,
        out_specs=VMEM,
        compiler_params=pltpu.CompilerParams(vmem_limit_bytes=8 * MB),
        name="final",
    )(got, fold, leafs, base)


def per_device(
    values,
    leaf_basis,
    transfer,
    local_coupling,
    coupling_source,
    near_field,
    near_source,
    upper_transfer,
    upper_coupling,
    top_coupling,
):
    vals, coefs, chain, fan, downs, tops = up_call(
        values, leaf_basis, transfer, upper_transfer, top_coupling
    )
    roots = lax.all_to_all(fan, "branch", 0, 0, tiled=True)
    rows = pack_call(vals, coefs)
    last = N_BRANCH * N_LEAF - 1
    ring = ("branch", "leaf")
    before = lax.ppermute(rows, ring, [(i, i + 1) for i in range(last)])
    after = lax.ppermute(rows, ring, [(i + 1, i) for i in range(last)])
    sent = mid_call(roots, tops, chain)
    sent, before, after = lax.optimization_barrier((sent, before, after))
    got = lax.all_to_all(sent, "leaf", 0, 0, tiled=True)
    fold, leafs = prep_call(upper_coupling, downs, leaf_basis, transfer)
    base = local_call(
        rows, before, after, coupling_source, near_source, local_coupling, near_field,
        transfer, leaf_basis,
    )
    return final_call(got, fold, leafs, base)


def solution(mesh):
    in_specs = (
        P(None, None, ("branch", "leaf")),
        P(("branch", "leaf"), None, None),
        P(("branch", "leaf"), None, None),
        P(None, ("branch", "leaf"), None, None, None),
        P(("branch", "leaf"), None),
        P(None, ("branch", "leaf"), None, None, None),
        P(("branch", "leaf"), None),
        P("branch", None, None, None),
        P(None, "branch", None, None, None),
        P(None, "branch", None, None, None),
    )
    out_specs = P(None, None, ("branch", "leaf"))
    return jax.shard_map(
        per_device, mesh=mesh, in_specs=in_specs, out_specs=out_specs, check_vma=False
    )
```

```python
import functools

import jax
import jax.numpy as jnp
from jax import lax
from jax.experimental import pallas as pl
from jax.experimental.pallas import tpu as pltpu
from jax.sharding import PartitionSpec as P

f32 = jnp.float32
bf16 = jnp.bfloat16
R = 64
RHS = 16
LEAVES = 8
LOCAL = 14
ROWS = 22
DEPTH = 5
N_LEAF = 32
N_BRANCH = 8
LINKS = 12
UNROLL = 4
ANY = pl.BlockSpec(memory_space=pl.ANY)
VMEM = pl.BlockSpec(memory_space=pltpu.VMEM)
MB = 2**20


def hbm(*arrays):
    return [pltpu.with_memory_space_constraint(a, pltpu.HBM) for a in arrays]


def dot(a, b):
    return jnp.dot(a, b, preferred_element_type=f32)


def dot_nt(a, b):
    return lax.dot_general(a, b, (((1,), (1,)), ((), ())), preferred_element_type=f32)


def turned(v):
    return jnp.concatenate([v[:, R:], v[:, :R]], axis=1)


def packed(c):
    return jnp.concatenate([c[:RHS], c[RHS:]], axis=1)


def upper_index(leaf, step):
    return 2 * N_LEAF - 2 * (N_LEAF >> step) + jnp.right_shift(leaf, step)


def up_kernel(
    values, basis, transfer, upper, top, vals, coefs, chain, fan, downs, tops, bas, tra, upp, sem
):
    leaf = lax.axis_index("leaf")
    firsts = [
        pltpu.make_async_copy(
            upper.at[0, upper_index(leaf, step)], upp.at[step], sem.at[4 + step]
        )
        for step in range(DEPTH)
    ]
    firsts += [
        pltpu.make_async_copy(values, vals, sem.at[0]),
        pltpu.make_async_copy(basis, bas, sem.at[1]),
        pltpu.make_async_copy(transfer, tra, sem.at[2]),
    ]
    last = pltpu.make_async_copy(top, tops, sem.at[3])
    for copy in firsts + [last]:
        copy.start()
    for copy in firsts:
        copy.wait()
    down = upp[0]
    downs[0] = down
    for step in range(1, DEPTH):
        down = dot(down, upp[step]).astype(bf16)
        downs[step] = down
    level = []
    for pair in range(LEAVES // 2):
        x0 = vals[0, :, pl.ds(pair * 2 * R, 2 * R)]
        x1 = vals[1, :, pl.ds(pair * 2 * R, 2 * R)]
        for half in range(2):
            lanes = slice(half * R, (half + 1) * R)
            cell = jnp.concatenate([x0[:, lanes], x1[:, lanes]], axis=0)
            level.append(dot(cell, bas[2 * pair + half]).astype(bf16))
    begin = 0
    while len(level) > 1:
        for i, c in enumerate(level):
            coefs[begin + i] = c
        merged = [
            (dot(level[i], tra[begin + i]) + dot(level[i + 1], tra[begin + i + 1])).astype(bf16)
            for i in range(0, len(level), 2)
        ]
        begin += len(level)
        level = merged
    root = level[0]
    chain[0] = packed(root)
    for step in range(1, DEPTH + 1):
        part = packed(dot(root, downs[step - 1]).astype(bf16))
        if step < DEPTH:
            chain[step] = part
        else:
            for b in range(N_BRANCH):
                fan[b] = part
    last.wait()


def up_call(values, basis, transfer, upper, top):
    return pl.pallas_call(
        up_kernel,
        out_shape=[
            pltpu.VMEM((2, RHS, LEAVES * R), bf16),
            pltpu.VMEM((LOCAL, 2 * RHS, R), bf16),
            pltpu.VMEM((DEPTH, RHS, 2 * R), bf16),
            pltpu.VMEM((N_BRANCH, RHS, 2 * R), bf16),
            pltpu.VMEM((DEPTH, R, R), bf16),
            pltpu.VMEM((2, 1, N_BRANCH - 1, R, R), bf16),
        ],
        in_specs=[ANY] * 5,
        out_specs=[VMEM] * 6,
        scratch_shapes=[
            pltpu.VMEM((LEAVES, R, R), bf16),
            pltpu.VMEM((LOCAL, R, R), bf16),
            pltpu.VMEM((DEPTH, R, R), bf16),
            pltpu.SemaphoreType.DMA((4 + DEPTH,)),
        ],
        compiler_params=pltpu.CompilerParams(vmem_limit_bytes=8 * MB),
        name="up",
    )(*hbm(values, basis, transfer, upper, top))


def pack_kernel(vals, coefs, rows):
    left = lax.broadcasted_iota(jnp.int32, (RHS, 2 * R), 1) < R
    for pair in range(LEAVES // 2):
        x0 = vals[0, :, pl.ds(pair * 2 * R, 2 * R)]
        x1 = vals[1, :, pl.ds(pair * 2 * R, 2 * R)]
        rows[2 * pair] = jnp.where(left, x0, turned(x1))
        rows[2 * pair + 1] = jnp.where(left, turned(x0), x1)
    for i in range(LOCAL):
        rows[LEAVES + i] = packed(coefs[i])


def pack_call(vals, coefs):
    return pl.pallas_call(
        pack_kernel,
        out_shape=pltpu.VMEM((ROWS, RHS, 2 * R), bf16),
        in_specs=[VMEM] * 2,
        out_specs=VMEM,
        compiler_params=pltpu.CompilerParams(vmem_limit_bytes=8 * MB),
        cost_estimate=pl.CostEstimate(
            flops=10**8, bytes_accessed=4 * 10**6, transcendentals=0
        ),
        name="pack",
    )(vals, coefs)


def prep_kernel(couple, downs, basis, transfer, fold, leafs, cou, bas, tra, sem):
    leaf = lax.axis_index("leaf")
    copies = [
        pltpu.make_async_copy(transfer, tra, sem.at[DEPTH]),
        pltpu.make_async_copy(basis, bas, sem.at[DEPTH + 1]),
    ]
    for step in range(DEPTH):
        copies.append(
            pltpu.make_async_copy(
                couple.at[:, 0, upper_index(leaf, step)], cou.at[step], sem.at[step]
            )
        )
    for copy in copies:
        copy.start()
    for copy in copies:
        copy.wait()
    zero = jnp.zeros((R, R), bf16)
    tops2 = [tra[12 + t] for t in range(2)]
    tops1 = [dot(tra[8 + t], tops2[t // 2]).astype(bf16) for t in range(4)]
    tops0 = [dot(tra[t], tops1[t // 2]).astype(bf16) for t in range(8)]
    for t in range(LEAVES):
        full = dot(bas[t], tops0[t]).astype(bf16)
        leafs[pl.ds(t * R, R), :] = jnp.concatenate([full, zero], axis=1)
        leafs[pl.ds((LEAVES + t) * R, R), :] = jnp.concatenate([zero, full], axis=1)
    for step in range(DEPTH + 1):
        lanes = pl.ds(step * 2 * R, 2 * R)
        for g in range(2):
            if step == DEPTH:
                mat = downs[DEPTH - 1]
            elif step == 0:
                mat = cou[step, g]
            else:
                mat = dot(downs[step - 1], cou[step, g]).astype(bf16)
            pair = [mat, zero] if g == 0 else [zero, mat]
            fold[pl.ds(g * R, R), lanes] = jnp.concatenate(pair, axis=1)


def prep_call(couple, downs, basis, transfer):
    couple, basis, transfer = hbm(couple, basis, transfer)
    return pl.pallas_call(
        prep_kernel,
        out_shape=[
            pltpu.VMEM((2 * R, (DEPTH + 1) * 2 * R), bf16),
            pltpu.VMEM((2 * LEAVES * R, 2 * R), bf16),
        ],
        in_specs=[ANY, VMEM, ANY, ANY],
        out_specs=[VMEM] * 2,
        scratch_shapes=[
            pltpu.VMEM((DEPTH, 2, R, R), bf16),
            pltpu.VMEM((LEAVES, R, R), bf16),
            pltpu.VMEM((LOCAL, R, R), bf16),
            pltpu.SemaphoreType.DMA((DEPTH + 2,)),
        ],
        compiler_params=pltpu.CompilerParams(vmem_limit_bytes=8 * MB),
        cost_estimate=pl.CostEstimate(
            flops=10**8, bytes_accessed=4 * 10**6, transcendentals=0
        ),
        name="prep",
    )(couple, downs, basis, transfer)


def mid_kernel(roots, tops, chain, out):
    leaf = lax.axis_index("leaf")
    branch = lax.axis_index("branch")
    others = [roots[(branch + 1 + i) % N_BRANCH] for i in range(N_BRANCH - 1)]
    parts = []
    for g in range(2):
        lanes = slice(g * R, (g + 1) * R)
        v = jnp.concatenate([other[:, lanes] for other in others], axis=1)
        m = jnp.concatenate([tops[g, 0, i] for i in range(N_BRANCH - 1)], axis=1)
        parts.append(dot_nt(v, m))
    part = jnp.concatenate(parts, axis=1).astype(bf16)
    for i in range(N_LEAF):
        to = jnp.bitwise_xor(leaf, i)
        out[to, 0] = chain[max(i.bit_length() - 1, 0)]
        out[to, 1] = part


def mid_call(roots, tops, chain):
    return pl.pallas_call(
        mid_kernel,
        out_shape=pltpu.VMEM((N_LEAF, 2, RHS, 2 * R), bf16),
        in_specs=[VMEM] * 3,
        out_specs=VMEM,
        compiler_params=pltpu.CompilerParams(vmem_limit_bytes=8 * MB),
        name="mid",
    )(roots, tops, chain)


def local_kernel(
    own, even, odd, coupling, near, coupling_source, near_source, transfer, basis,
    base, wide, sums, cells, cou, nea, cosrc, nesrc, tra, bas, sem,
):
    smalls = [
        pltpu.make_async_copy(coupling_source, cosrc, sem.at[0]),
        pltpu.make_async_copy(near_source, nesrc, sem.at[1]),
        pltpu.make_async_copy(transfer, tra, sem.at[2]),
        pltpu.make_async_copy(basis, bas, sem.at[3]),
    ]
    bigs = []
    for n, (source, into, start, count) in enumerate(
        ((coupling, cou, 8, 6), (coupling, cou, 0, 4), (coupling, cou, 4, 4),
         (near, nea, 0, 4), (near, nea, 4, 4))
    ):
        span = pl.ds(start, count)
        bigs.append(pltpu.make_async_copy(source.at[:, span], into.at[:, span], sem.at[4 + n]))
    for copy in smalls[:2] + bigs + smalls[2:]:
        copy.start()
    left = lax.broadcasted_iota(jnp.int32, (RHS, 2 * R), 1) < R
    here = jnp.bitwise_and(lax.axis_index("leaf"), 1)
    for part, ref in ((1, own), (2 - 2 * here, even), (2 * here, odd)):
        for row in range(ROWS):
            v = ref[row]
            s = turned(v)
            wide[0, part * ROWS + row] = jnp.where(left, v, s)
            wide[1, part * ROWS + row] = jnp.where(left, s, v)

    def block(picked, mats):
        result = []
        for g in range(2):
            acc = None
            for j in range(0, LINKS, 4):
                v = jnp.concatenate(
                    [
                        jnp.where(left, wide[g, picked[j]], wide[g, picked[j + 1]]),
                        jnp.where(left, wide[g, picked[j + 2]], wide[g, picked[j + 3]]),
                    ],
                    axis=1,
                )
                m = jnp.concatenate([mats(g, j + n) for n in range(4)], axis=1)
                part = dot_nt(v, m)
                acc = part if acc is None else acc + part
            result.append(acc)
        return jnp.concatenate(result, axis=0)

    def far_body(log, start, t):
        r = start + t
        picked = []
        for j in range(LINKS):
            s = cosrc[r, j]
            picked.append(
                jnp.right_shift(s, log) * ROWS
                + LEAVES
                + start
                + jnp.bitwise_and(s, (1 << log) - 1)
            )
        sums[r] = block(picked, lambda g, j: cou[g, r, j])

    def near_body(t):
        picked = []
        for j in range(LINKS):
            s = nesrc[t, j]
            picked.append(jnp.right_shift(s, 3) * ROWS + jnp.bitwise_and(s, 7))
        cells[t] = block(picked, lambda g, j: nea[g, t, j])

    def each(body, first, count):
        def step(i, carry):
            body(first + i)
            return carry

        lax.fori_loop(0, count, step, 0, unroll=min(UNROLL, count))

    for copy in smalls[:2]:
        copy.wait()
    bigs[0].wait()
    each(functools.partial(far_body, 1, 12), 0, 2)
    each(functools.partial(far_body, 2, 8), 0, 4)
    bigs[1].wait()
    each(functools.partial(far_body, 3, 0), 0, 4)
    bigs[2].wait()
    each(functools.partial(far_body, 3, 0), 4, 4)
    bigs[3].wait()
    each(near_body, 0, 4)
    bigs[4].wait()
    each(near_body, 4, 4)
    for copy in smalls[2:]:
        copy.wait()
    up2 = [sums[12 + t].astype(bf16) for t in range(2)]
    up1 = [
        (sums[8 + t] + dot_nt(up2[t // 2], tra[8 + t])).astype(bf16) for t in range(4)
    ]
    up0 = [(sums[t] + dot_nt(up1[t // 2], tra[t])).astype(bf16) for t in range(8)]
    full = [cells[t] + dot_nt(up0[t], bas[t]) for t in range(8)]
    for pair in range(LEAVES // 2):
        both = jnp.concatenate([full[2 * pair], full[2 * pair + 1]], axis=1)
        for g in range(2):
            base[g, :, pl.ds(pair * 2 * R, 2 * R)] = both[g * RHS : (g + 1) * RHS]


def local_call(own, even, odd, coupling_source, near_source, coupling, near, transfer, basis):
    return pl.pallas_call(
        local_kernel,
        out_shape=pltpu.VMEM((2, RHS, LEAVES * R), f32),
        in_specs=[VMEM] * 3 + [ANY] * 6,
        out_specs=VMEM,
        scratch_shapes=[
            pltpu.VMEM((2, 3 * ROWS, RHS, 2 * R), bf16),
            pltpu.VMEM((LOCAL, 2 * RHS, R), f32),
            pltpu.VMEM((LEAVES, 2 * RHS, R), f32),
            pltpu.VMEM((2, LOCAL, LINKS, R, R), bf16),
            pltpu.VMEM((2, LEAVES, LINKS, R, R), bf16),
            pltpu.SMEM((LOCAL, LINKS), jnp.int32),
            pltpu.SMEM((LEAVES, LINKS), jnp.int32),
            pltpu.VMEM((LOCAL, R, R), bf16),
            pltpu.VMEM((LEAVES, R, R), bf16),
            pltpu.SemaphoreType.DMA((9,)),
        ],
        compiler_params=pltpu.CompilerParams(vmem_limit_bytes=24 * MB),
        cost_estimate=pl.CostEstimate(
            flops=10**8, bytes_accessed=2 * 10**7, transcendentals=0
        ),
        name="local",
    )(
        own, even, odd,
        *hbm(coupling, near, coupling_source, near_source, transfer, basis),
    )


def final_kernel(got, fold, leafs, base, out):
    leaf = lax.axis_index("leaf")
    parts = []
    for step in range(DEPTH):
        total = None
        for i in range(1 << step, 2 << step):
            v = got[jnp.bitwise_xor(leaf, i), 0].astype(f32)
            total = v if total is None else total + v
        parts.append(total.astype(bf16))
    total = got[0, 1].astype(f32)
    for i in range(1, N_LEAF):
        total = total + got[i, 1].astype(f32)
    parts.append(total.astype(bf16))
    target = dot_nt(jnp.concatenate(parts, axis=1), fold[...]).astype(bf16)
    far = dot_nt(target, leafs[...])
    width = LEAVES * R
    for g in range(2):
        out[g] = base[g] + far[:, g * width : (g + 1) * width]


def final_call(got, fold, leafs, base):
    return pl.pallas_call(
        final_kernel,
        out_shape=jax.ShapeDtypeStruct((2, RHS, LEAVES * R), f32),
        in_specs=[VMEM] * 4,
        out_specs=VMEM,
        compiler_params=pltpu.CompilerParams(vmem_limit_bytes=8 * MB),
        name="final",
    )(got, fold, leafs, base)


def per_device(
    values,
    leaf_basis,
    transfer,
    local_coupling,
    coupling_source,
    near_field,
    near_source,
    upper_transfer,
    upper_coupling,
    top_coupling,
):
    vals, coefs, chain, fan, downs, tops = up_call(
        values, leaf_basis, transfer, upper_transfer, top_coupling
    )
    roots = lax.all_to_all(fan, "branch", 0, 0, tiled=True)
    fold, leafs = prep_call(upper_coupling, downs, leaf_basis, transfer)
    rows = pack_call(vals, coefs)
    count = N_BRANCH * N_LEAF
    ring = ("branch", "leaf")
    even = lax.ppermute(rows, ring, [(i, i ^ 1) for i in range(count)])
    odd = lax.ppermute(
        rows, ring, [(i, ((i + 1) ^ 1) - 1) for i in range(1, count - 1)]
    )
    roots, fold, leafs = lax.optimization_barrier((roots, fold, leafs))
    sent = mid_call(roots, tops, chain)
    sent, even, odd = lax.optimization_barrier((sent, even, odd))
    got = lax.all_to_all(sent, "leaf", 0, 0, tiled=True)
    base = local_call(
        rows, even, odd, coupling_source, near_source, local_coupling, near_field,
        transfer, leaf_basis,
    )
    return final_call(got, fold, leafs, base)


def solution(mesh):
    in_specs = (
        P(None, None, ("branch", "leaf")),
        P(("branch", "leaf"), None, None),
        P(("branch", "leaf"), None, None),
        P(None, ("branch", "leaf"), None, None, None),
        P(("branch", "leaf"), None),
        P(None, ("branch", "leaf"), None, None, None),
        P(("branch", "leaf"), None),
        P("branch", None, None, None),
        P(None, "branch", None, None, None),
        P(None, "branch", None, None, None),
    )
    out_specs = P(None, None, ("branch", "leaf"))
    return jax.shard_map(
        per_device, mesh=mesh, in_specs=in_specs, out_specs=out_specs, check_vma=False
    )
```

```python
import functools

import jax
import jax.numpy as jnp
from jax import lax
from jax.experimental import pallas as pl
from jax.experimental.pallas import tpu as pltpu
from jax.sharding import PartitionSpec as P

f32 = jnp.float32
bf16 = jnp.bfloat16
R = 64
RHS = 16
LEAVES = 8
LOCAL = 14
ROWS = 22
DEPTH = 5
N_LEAF = 32
N_BRANCH = 8
LINKS = 12
UNROLL = 4
ANY = pl.BlockSpec(memory_space=pl.ANY)
VMEM = pl.BlockSpec(memory_space=pltpu.VMEM)
MB = 2**20


def hbm(*arrays):
    return [pltpu.with_memory_space_constraint(a, pltpu.HBM) for a in arrays]


def dot(a, b):
    return jnp.dot(a, b, preferred_element_type=f32)


def dot_nt(a, b):
    return lax.dot_general(a, b, (((1,), (1,)), ((), ())), preferred_element_type=f32)


def turned(v):
    return jnp.concatenate([v[:, R:], v[:, :R]], axis=1)


def packed(c):
    return jnp.concatenate([c[:RHS], c[RHS:]], axis=1)


def upper_index(leaf, step):
    return 2 * N_LEAF - 2 * (N_LEAF >> step) + jnp.right_shift(leaf, step)


def up_kernel(
    values, basis, transfer, upper, top, vals, coefs, chain, fan, downs, tops, bas, tra, upp, sem
):
    leaf = lax.axis_index("leaf")
    firsts = [
        pltpu.make_async_copy(
            upper.at[0, upper_index(leaf, step)], upp.at[step], sem.at[4 + step]
        )
        for step in range(DEPTH)
    ]
    firsts += [
        pltpu.make_async_copy(values, vals, sem.at[0]),
        pltpu.make_async_copy(basis, bas, sem.at[1]),
        pltpu.make_async_copy(transfer, tra, sem.at[2]),
    ]
    last = pltpu.make_async_copy(top, tops, sem.at[3])
    for copy in firsts + [last]:
        copy.start()
    for copy in firsts:
        copy.wait()
    down = upp[0]
    downs[0] = down
    for step in range(1, DEPTH):
        down = dot(down, upp[step]).astype(bf16)
        downs[step] = down
    level = []
    for pair in range(LEAVES // 2):
        x0 = vals[0, :, pl.ds(pair * 2 * R, 2 * R)]
        x1 = vals[1, :, pl.ds(pair * 2 * R, 2 * R)]
        for half in range(2):
            lanes = slice(half * R, (half + 1) * R)
            cell = jnp.concatenate([x0[:, lanes], x1[:, lanes]], axis=0)
            level.append(dot(cell, bas[2 * pair + half]).astype(bf16))
    begin = 0
    while len(level) > 1:
        for i, c in enumerate(level):
            coefs[begin + i] = c
        merged = [
            (dot(level[i], tra[begin + i]) + dot(level[i + 1], tra[begin + i + 1])).astype(bf16)
            for i in range(0, len(level), 2)
        ]
        begin += len(level)
        level = merged
    root = level[0]
    chain[0] = packed(root)
    for step in range(1, DEPTH + 1):
        part = packed(dot(root, downs[step - 1]).astype(bf16))
        if step < DEPTH:
            chain[step] = part
        else:
            for b in range(N_BRANCH):
                fan[b] = part
    last.wait()


def up_call(values, basis, transfer, upper, top):
    return pl.pallas_call(
        up_kernel,
        out_shape=[
            pltpu.VMEM((2, RHS, LEAVES * R), bf16),
            pltpu.VMEM((LOCAL, 2 * RHS, R), bf16),
            pltpu.VMEM((DEPTH, RHS, 2 * R), bf16),
            pltpu.VMEM((N_BRANCH, RHS, 2 * R), bf16),
            pltpu.VMEM((DEPTH, R, R), bf16),
            pltpu.VMEM((2, 1, N_BRANCH - 1, R, R), bf16),
        ],
        in_specs=[ANY] * 5,
        out_specs=[VMEM] * 6,
        scratch_shapes=[
            pltpu.VMEM((LEAVES, R, R), bf16),
            pltpu.VMEM((LOCAL, R, R), bf16),
            pltpu.VMEM((DEPTH, R, R), bf16),
            pltpu.SemaphoreType.DMA((4 + DEPTH,)),
        ],
        compiler_params=pltpu.CompilerParams(vmem_limit_bytes=8 * MB),
        name="up",
    )(*hbm(values, basis, transfer, upper, top))


def pack_kernel(vals, coefs, rows):
    left = lax.broadcasted_iota(jnp.int32, (RHS, 2 * R), 1) < R
    for pair in range(LEAVES // 2):
        x0 = vals[0, :, pl.ds(pair * 2 * R, 2 * R)]
        x1 = vals[1, :, pl.ds(pair * 2 * R, 2 * R)]
        rows[2 * pair] = jnp.where(left, x0, turned(x1))
        rows[2 * pair + 1] = jnp.where(left, turned(x0), x1)
    for i in range(LOCAL):
        rows[LEAVES + i] = packed(coefs[i])


def pack_call(vals, coefs):
    return pl.pallas_call(
        pack_kernel,
        out_shape=pltpu.VMEM((ROWS, RHS, 2 * R), bf16),
        in_specs=[VMEM] * 2,
        out_specs=VMEM,
        compiler_params=pltpu.CompilerParams(vmem_limit_bytes=8 * MB),
        cost_estimate=pl.CostEstimate(
            flops=10**8, bytes_accessed=4 * 10**6, transcendentals=0
        ),
        name="pack",
    )(vals, coefs)


def cast_kernel(upper, couple, chain, pushed, carry, own, sib, cou, sem):
    leaf = lax.axis_index("leaf")
    copies = []
    for step in range(DEPTH):
        here = upper_index(leaf, step)
        there = jnp.bitwise_xor(here, 1)
        copies += [
            pltpu.make_async_copy(upper.at[0, here], own.at[step], sem.at[3 * step]),
            pltpu.make_async_copy(upper.at[0, there], sib.at[step], sem.at[3 * step + 1]),
            pltpu.make_async_copy(couple.at[:, 0, there], cou.at[step], sem.at[3 * step + 2]),
        ]
    for copy in copies:
        copy.start()
    for copy in copies:
        copy.wait()
    zero = jnp.zeros((R, R), bf16)

    def place(step, mat):
        carry[pl.ds(2 * step * R, R), :] = jnp.concatenate([mat, zero], axis=1)
        carry[pl.ds((2 * step + 1) * R, R), :] = jnp.concatenate([zero, mat], axis=1)

    path = own[DEPTH - 1]
    place(DEPTH - 1, sib[DEPTH - 1])
    for step in range(DEPTH - 2, -1, -1):
        place(step, dot(sib[step], path).astype(bf16))
        path = dot(own[step], path).astype(bf16)
    place(DEPTH, path)
    for step in range(DEPTH):
        v = chain[step]
        pushed[step] = jnp.concatenate(
            [dot_nt(v[:, g * R : (g + 1) * R], cou[step, g]) for g in range(2)], axis=1
        )


def cast_call(upper, couple, chain):
    return pl.pallas_call(
        cast_kernel,
        out_shape=[
            pltpu.VMEM((DEPTH, RHS, 2 * R), f32),
            pltpu.VMEM(((DEPTH + 1) * 2 * R, 2 * R), bf16),
        ],
        in_specs=[ANY, ANY, VMEM],
        out_specs=[VMEM] * 2,
        scratch_shapes=[
            pltpu.VMEM((DEPTH, R, R), bf16),
            pltpu.VMEM((DEPTH, R, R), bf16),
            pltpu.VMEM((DEPTH, 2, R, R), bf16),
            pltpu.SemaphoreType.DMA((3 * DEPTH,)),
        ],
        compiler_params=pltpu.CompilerParams(vmem_limit_bytes=8 * MB),
        cost_estimate=pl.CostEstimate(
            flops=10**8, bytes_accessed=4 * 10**6, transcendentals=0
        ),
        name="cast",
    )(*hbm(upper, couple), chain)


def prep_kernel(downs, basis, transfer, fold, leafs, bas, tra, sem):
    copies = [
        pltpu.make_async_copy(transfer, tra, sem.at[0]),
        pltpu.make_async_copy(basis, bas, sem.at[1]),
    ]
    for copy in copies:
        copy.start()
    zero = jnp.zeros((R, R), bf16)
    for step in range(DEPTH - 1):
        lanes = pl.ds(step * 2 * R, 2 * R)
        mat = downs[step]
        fold[pl.ds(0, R), lanes] = jnp.concatenate([mat, zero], axis=1)
        fold[pl.ds(R, R), lanes] = jnp.concatenate([zero, mat], axis=1)
    for copy in copies:
        copy.wait()
    tops2 = [tra[12 + t] for t in range(2)]
    tops1 = [dot(tra[8 + t], tops2[t // 2]).astype(bf16) for t in range(4)]
    tops0 = [dot(tra[t], tops1[t // 2]).astype(bf16) for t in range(8)]
    for t in range(LEAVES):
        full = dot(bas[t], tops0[t]).astype(bf16)
        leafs[pl.ds(t * R, R), :] = jnp.concatenate([full, zero], axis=1)
        leafs[pl.ds((LEAVES + t) * R, R), :] = jnp.concatenate([zero, full], axis=1)


def prep_call(downs, basis, transfer):
    basis, transfer = hbm(basis, transfer)
    return pl.pallas_call(
        prep_kernel,
        out_shape=[
            pltpu.VMEM((2 * R, (DEPTH - 1) * 2 * R), bf16),
            pltpu.VMEM((2 * LEAVES * R, 2 * R), bf16),
        ],
        in_specs=[VMEM, ANY, ANY],
        out_specs=[VMEM] * 2,
        scratch_shapes=[
            pltpu.VMEM((LEAVES, R, R), bf16),
            pltpu.VMEM((LOCAL, R, R), bf16),
            pltpu.SemaphoreType.DMA((2,)),
        ],
        compiler_params=pltpu.CompilerParams(vmem_limit_bytes=8 * MB),
        cost_estimate=pl.CostEstimate(
            flops=10**8, bytes_accessed=4 * 10**6, transcendentals=0
        ),
        name="prep",
    )(downs, basis, transfer)


def mid_kernel(roots, tops, pushed, carry, out):
    leaf = lax.axis_index("leaf")
    branch = lax.axis_index("branch")
    others = [roots[(branch + 1 + i) % N_BRANCH] for i in range(N_BRANCH - 1)]
    parts = []
    for g in range(2):
        lanes = slice(g * R, (g + 1) * R)
        v = jnp.concatenate([other[:, lanes] for other in others], axis=1)
        m = jnp.concatenate([tops[g, 0, i] for i in range(N_BRANCH - 1)], axis=1)
        parts.append(dot_nt(v, m))
    part = jnp.concatenate(parts, axis=1).astype(bf16)
    far = dot_nt(part, carry[...])
    pieces = [far[:, k * 2 * R : (k + 1) * 2 * R] for k in range(DEPTH + 1)]
    given = [(pieces[k] + pushed[k]).astype(bf16) for k in range(DEPTH)]
    out[leaf] = pieces[DEPTH].astype(bf16)
    for i in range(1, N_LEAF):
        out[jnp.bitwise_xor(leaf, i)] = given[i.bit_length() - 1]


def mid_call(roots, tops, pushed, carry):
    return pl.pallas_call(
        mid_kernel,
        out_shape=pltpu.VMEM((N_LEAF, RHS, 2 * R), bf16),
        in_specs=[VMEM] * 4,
        out_specs=VMEM,
        compiler_params=pltpu.CompilerParams(vmem_limit_bytes=8 * MB),
        name="mid",
    )(roots, tops, pushed, carry)


def local_kernel(
    own, even, odd, coupling, near, coupling_source, near_source, transfer, basis,
    base, wide, sums, cells, cou, nea, cosrc, nesrc, tra, bas, sem,
):
    smalls = [
        pltpu.make_async_copy(coupling_source, cosrc, sem.at[0]),
        pltpu.make_async_copy(near_source, nesrc, sem.at[1]),
        pltpu.make_async_copy(transfer, tra, sem.at[2]),
        pltpu.make_async_copy(basis, bas, sem.at[3]),
    ]
    bigs = []
    for n, (source, into, start, count) in enumerate(
        ((coupling, cou, 8, 6), (coupling, cou, 0, 4), (coupling, cou, 4, 4),
         (near, nea, 0, 4), (near, nea, 4, 4))
    ):
        span = pl.ds(start, count)
        bigs.append(pltpu.make_async_copy(source.at[:, span], into.at[:, span], sem.at[4 + n]))
    for copy in smalls[:2] + bigs + smalls[2:]:
        copy.start()
    left = lax.broadcasted_iota(jnp.int32, (RHS, 2 * R), 1) < R
    here = jnp.bitwise_and(lax.axis_index("leaf"), 1)
    for part, ref in ((1, own), (2 - 2 * here, even), (2 * here, odd)):
        for row in range(ROWS):
            v = ref[row]
            s = turned(v)
            wide[0, part * ROWS + row] = jnp.where(left, v, s)
            wide[1, part * ROWS + row] = jnp.where(left, s, v)

    def block(picked, mats):
        result = []
        for g in range(2):
            acc = None
            for j in range(0, LINKS, 4):
                v = jnp.concatenate(
                    [
                        jnp.where(left, wide[g, picked[j]], wide[g, picked[j + 1]]),
                        jnp.where(left, wide[g, picked[j + 2]], wide[g, picked[j + 3]]),
                    ],
                    axis=1,
                )
                m = jnp.concatenate([mats(g, j + n) for n in range(4)], axis=1)
                part = dot_nt(v, m)
                acc = part if acc is None else acc + part
            result.append(acc)
        return jnp.concatenate(result, axis=0)

    def far_body(log, start, t):
        r = start + t
        picked = []
        for j in range(LINKS):
            s = cosrc[r, j]
            picked.append(
                jnp.right_shift(s, log) * ROWS
                + LEAVES
                + start
                + jnp.bitwise_and(s, (1 << log) - 1)
            )
        sums[r] = block(picked, lambda g, j: cou[g, r, j])

    def near_body(t):
        picked = []
        for j in range(LINKS):
            s = nesrc[t, j]
            picked.append(jnp.right_shift(s, 3) * ROWS + jnp.bitwise_and(s, 7))
        cells[t] = block(picked, lambda g, j: nea[g, t, j])

    def each(body, first, count):
        def step(i, carry):
            body(first + i)
            return carry

        lax.fori_loop(0, count, step, 0, unroll=min(UNROLL, count))

    for copy in smalls[:2]:
        copy.wait()
    bigs[0].wait()
    each(functools.partial(far_body, 1, 12), 0, 2)
    each(functools.partial(far_body, 2, 8), 0, 4)
    bigs[1].wait()
    each(functools.partial(far_body, 3, 0), 0, 4)
    bigs[2].wait()
    each(functools.partial(far_body, 3, 0), 4, 4)
    bigs[3].wait()
    each(near_body, 0, 4)
    bigs[4].wait()
    each(near_body, 4, 4)
    for copy in smalls[2:]:
        copy.wait()
    up2 = [sums[12 + t].astype(bf16) for t in range(2)]
    up1 = [
        (sums[8 + t] + dot_nt(up2[t // 2], tra[8 + t])).astype(bf16) for t in range(4)
    ]
    up0 = [(sums[t] + dot_nt(up1[t // 2], tra[t])).astype(bf16) for t in range(8)]
    full = [cells[t] + dot_nt(up0[t], bas[t]) for t in range(8)]
    for pair in range(LEAVES // 2):
        both = jnp.concatenate([full[2 * pair], full[2 * pair + 1]], axis=1)
        for g in range(2):
            base[g, :, pl.ds(pair * 2 * R, 2 * R)] = both[g * RHS : (g + 1) * RHS]


def local_call(own, even, odd, coupling_source, near_source, coupling, near, transfer, basis):
    return pl.pallas_call(
        local_kernel,
        out_shape=pltpu.VMEM((2, RHS, LEAVES * R), f32),
        in_specs=[VMEM] * 3 + [ANY] * 6,
        out_specs=VMEM,
        scratch_shapes=[
            pltpu.VMEM((2, 3 * ROWS, RHS, 2 * R), bf16),
            pltpu.VMEM((LOCAL, 2 * RHS, R), f32),
            pltpu.VMEM((LEAVES, 2 * RHS, R), f32),
            pltpu.VMEM((2, LOCAL, LINKS, R, R), bf16),
            pltpu.VMEM((2, LEAVES, LINKS, R, R), bf16),
            pltpu.SMEM((LOCAL, LINKS), jnp.int32),
            pltpu.SMEM((LEAVES, LINKS), jnp.int32),
            pltpu.VMEM((LOCAL, R, R), bf16),
            pltpu.VMEM((LEAVES, R, R), bf16),
            pltpu.SemaphoreType.DMA((9,)),
        ],
        compiler_params=pltpu.CompilerParams(vmem_limit_bytes=24 * MB),
        cost_estimate=pl.CostEstimate(
            flops=10**8, bytes_accessed=2 * 10**7, transcendentals=0
        ),
        name="local",
    )(
        own, even, odd,
        *hbm(coupling, near, coupling_source, near_source, transfer, basis),
    )


def final_kernel(got, fold, leafs, base, out):
    leaf = lax.axis_index("leaf")
    near = got[leaf].astype(f32) + got[jnp.bitwise_xor(leaf, 1)].astype(f32)
    parts = []
    for step in range(1, DEPTH):
        total = None
        for i in range(1 << step, 2 << step):
            v = got[jnp.bitwise_xor(leaf, i)].astype(f32)
            total = v if total is None else total + v
        parts.append(total.astype(bf16))
    target = (near + dot_nt(jnp.concatenate(parts, axis=1), fold[...])).astype(bf16)
    far = dot_nt(target, leafs[...])
    width = LEAVES * R
    for g in range(2):
        out[g] = base[g] + far[:, g * width : (g + 1) * width]


def final_call(got, fold, leafs, base):
    return pl.pallas_call(
        final_kernel,
        out_shape=jax.ShapeDtypeStruct((2, RHS, LEAVES * R), f32),
        in_specs=[VMEM] * 4,
        out_specs=VMEM,
        compiler_params=pltpu.CompilerParams(vmem_limit_bytes=8 * MB),
        name="final",
    )(got, fold, leafs, base)


def per_device(
    values,
    leaf_basis,
    transfer,
    local_coupling,
    coupling_source,
    near_field,
    near_source,
    upper_transfer,
    upper_coupling,
    top_coupling,
):
    vals, coefs, chain, fan, downs, tops = up_call(
        values, leaf_basis, transfer, upper_transfer, top_coupling
    )
    roots = lax.all_to_all(fan, "branch", 0, 0, tiled=True)
    pushed, carry = cast_call(upper_transfer, upper_coupling, chain)
    rows = pack_call(vals, coefs)
    count = N_BRANCH * N_LEAF
    ring = ("branch", "leaf")
    even = lax.ppermute(rows, ring, [(i, i ^ 1) for i in range(count)])
    odd = lax.ppermute(
        rows, ring, [(i, ((i + 1) ^ 1) - 1) for i in range(1, count - 1)]
    )
    roots, pushed, carry = lax.optimization_barrier((roots, pushed, carry))
    sent = mid_call(roots, tops, pushed, carry)
    sent, even, odd = lax.optimization_barrier((sent, even, odd))
    got = lax.all_to_all(sent, "leaf", 0, 0, tiled=True)
    fold, leafs = prep_call(downs, leaf_basis, transfer)
    base = local_call(
        rows, even, odd, coupling_source, near_source, local_coupling, near_field,
        transfer, leaf_basis,
    )
    return final_call(got, fold, leafs, base)


def solution(mesh):
    in_specs = (
        P(None, None, ("branch", "leaf")),
        P(("branch", "leaf"), None, None),
        P(("branch", "leaf"), None, None),
        P(None, ("branch", "leaf"), None, None, None),
        P(("branch", "leaf"), None),
        P(None, ("branch", "leaf"), None, None, None),
        P(("branch", "leaf"), None),
        P("branch", None, None, None),
        P(None, "branch", None, None, None),
        P(None, "branch", None, None, None),
    )
    out_specs = P(None, None, ("branch", "leaf"))
    return jax.shard_map(
        per_device, mesh=mesh, in_specs=in_specs, out_specs=out_specs, check_vma=False
    )
```

```python
import functools

import jax
import jax.numpy as jnp
from jax import lax
from jax.experimental import pallas as pl
from jax.experimental.pallas import tpu as pltpu
from jax.sharding import PartitionSpec as P

f32 = jnp.float32
bf16 = jnp.bfloat16
R = 64
RHS = 16
LEAVES = 8
LOCAL = 14
ROWS = 22
DEPTH = 5
N_LEAF = 32
N_BRANCH = 8
LINKS = 12
UNROLL = 4
ANY = pl.BlockSpec(memory_space=pl.ANY)
VMEM = pl.BlockSpec(memory_space=pltpu.VMEM)
MB = 2**20


def hbm(*arrays):
    return [pltpu.with_memory_space_constraint(a, pltpu.HBM) for a in arrays]


def dot(a, b):
    return jnp.dot(a, b, preferred_element_type=f32)


def dot_nt(a, b):
    return lax.dot_general(a, b, (((1,), (1,)), ((), ())), preferred_element_type=f32)


def turned(v):
    return jnp.concatenate([v[:, R:], v[:, :R]], axis=1)


def packed(c):
    return jnp.concatenate([c[:RHS], c[RHS:]], axis=1)


def upper_index(leaf, step):
    return 2 * N_LEAF - 2 * (N_LEAF >> step) + jnp.right_shift(leaf, step)


def up_kernel(
    values, basis, transfer, upper, couple, top,
    vals, coefs, sent, summit, downs, upp, sib, cou, tops, bas, tra, sem,
):
    leaf = lax.axis_index("leaf")
    here = [upper_index(leaf, step) for step in range(DEPTH)]
    firsts = [
        pltpu.make_async_copy(values, vals, sem.at[0]),
        pltpu.make_async_copy(basis, bas, sem.at[1]),
        pltpu.make_async_copy(transfer, tra, sem.at[2]),
    ]
    lasts = [pltpu.make_async_copy(top, tops, sem.at[3])]
    for k in range(DEPTH):
        there = jnp.bitwise_xor(here[k], 1)
        firsts.append(pltpu.make_async_copy(upper.at[0, here[k]], upp.at[k], sem.at[4 + 3 * k]))
        lasts.append(pltpu.make_async_copy(upper.at[0, there], sib.at[k], sem.at[5 + 3 * k]))
        lasts.append(
            pltpu.make_async_copy(couple.at[:, 0, here[k]], cou.at[k], sem.at[6 + 3 * k])
        )
    for copy in firsts + lasts:
        copy.start()
    for copy in firsts:
        copy.wait()
    down = upp[0]
    downs[0] = down
    for step in range(1, DEPTH):
        down = dot(down, upp[step]).astype(bf16)
        downs[step] = down
    level = []
    for pair in range(LEAVES // 2):
        x0 = vals[0, :, pl.ds(pair * 2 * R, 2 * R)]
        x1 = vals[1, :, pl.ds(pair * 2 * R, 2 * R)]
        for half in range(2):
            lanes = slice(half * R, (half + 1) * R)
            cell = jnp.concatenate([x0[:, lanes], x1[:, lanes]], axis=0)
            level.append(dot(cell, bas[2 * pair + half]).astype(bf16))
    begin = 0
    while len(level) > 1:
        for i, c in enumerate(level):
            coefs[begin + i] = c
        merged = [
            (dot(level[i], tra[begin + i]) + dot(level[i + 1], tra[begin + i + 1])).astype(bf16)
            for i in range(0, len(level), 2)
        ]
        begin += len(level)
        level = merged
    root = level[0]
    chain = [packed(root)]
    for step in range(DEPTH):
        chain.append(packed(dot(root, downs[step]).astype(bf16)))
    summit[...] = chain[DEPTH]
    sent[leaf] = chain[0]
    for i in range(1, N_LEAF):
        sent[jnp.bitwise_xor(leaf, i)] = chain[i.bit_length() - 1]
    for copy in lasts:
        copy.wait()


def up_call(values, basis, transfer, upper, couple, top):
    return pl.pallas_call(
        up_kernel,
        out_shape=[
            pltpu.VMEM((2, RHS, LEAVES * R), bf16),
            pltpu.VMEM((LOCAL, 2 * RHS, R), bf16),
            pltpu.VMEM((N_LEAF, RHS, 2 * R), bf16),
            pltpu.VMEM((RHS, 2 * R), bf16),
            pltpu.VMEM((DEPTH, R, R), bf16),
            pltpu.VMEM((DEPTH, R, R), bf16),
            pltpu.VMEM((DEPTH, R, R), bf16),
            pltpu.VMEM((DEPTH, 2, R, R), bf16),
            pltpu.VMEM((2, 1, N_BRANCH - 1, R, R), bf16),
            pltpu.VMEM((LEAVES, R, R), bf16),
            pltpu.VMEM((LOCAL, R, R), bf16),
        ],
        in_specs=[ANY] * 6,
        out_specs=[VMEM] * 11,
        scratch_shapes=[pltpu.SemaphoreType.DMA((4 + 3 * DEPTH,))],
        compiler_params=pltpu.CompilerParams(vmem_limit_bytes=8 * MB),
        name="up",
    )(*hbm(values, basis, transfer, upper, couple, top))


def pack_kernel(vals, coefs, rows):
    left = lax.broadcasted_iota(jnp.int32, (RHS, 2 * R), 1) < R
    for pair in range(LEAVES // 2):
        x0 = vals[0, :, pl.ds(pair * 2 * R, 2 * R)]
        x1 = vals[1, :, pl.ds(pair * 2 * R, 2 * R)]
        rows[2 * pair] = jnp.where(left, x0, turned(x1))
        rows[2 * pair + 1] = jnp.where(left, turned(x0), x1)
    for i in range(LOCAL):
        rows[LEAVES + i] = packed(coefs[i])


def pack_call(vals, coefs):
    return pl.pallas_call(
        pack_kernel,
        out_shape=pltpu.VMEM((ROWS, RHS, 2 * R), bf16),
        in_specs=[VMEM] * 2,
        out_specs=VMEM,
        compiler_params=pltpu.CompilerParams(vmem_limit_bytes=8 * MB),
        cost_estimate=pl.CostEstimate(
            flops=10**8, bytes_accessed=4 * 10**6, transcendentals=0
        ),
        name="pack",
    )(vals, coefs)


def cast_kernel(own, sib, lift):
    zero = jnp.zeros((R, R), bf16)

    def place(step, mat):
        lift[pl.ds(2 * step * R, R), :] = jnp.concatenate([mat, zero], axis=1)
        lift[pl.ds((2 * step + 1) * R, R), :] = jnp.concatenate([zero, mat], axis=1)

    path = own[DEPTH - 1]
    place(DEPTH - 1, sib[DEPTH - 1])
    for step in range(DEPTH - 2, -1, -1):
        place(step, dot(sib[step], path).astype(bf16))
        if step:
            path = dot(own[step], path).astype(bf16)


def cast_call(own, sib):
    return pl.pallas_call(
        cast_kernel,
        out_shape=pltpu.VMEM((DEPTH * 2 * R, 2 * R), bf16),
        in_specs=[VMEM] * 2,
        out_specs=VMEM,
        compiler_params=pltpu.CompilerParams(vmem_limit_bytes=8 * MB),
        cost_estimate=pl.CostEstimate(
            flops=10**8, bytes_accessed=4 * 10**6, transcendentals=0
        ),
        name="cast",
    )(own, sib)


def prep_kernel(cou, tops, downs, bas, tra, fold, leafs):
    zero = jnp.zeros((R, R), bf16)
    tops2 = [tra[12 + t] for t in range(2)]
    tops1 = [dot(tra[8 + t], tops2[t // 2]).astype(bf16) for t in range(4)]
    tops0 = [dot(tra[t], tops1[t // 2]).astype(bf16) for t in range(8)]
    for t in range(LEAVES):
        full = dot(bas[t], tops0[t]).astype(bf16)
        leafs[pl.ds(t * R, R), :] = jnp.concatenate([full, zero], axis=1)
        leafs[pl.ds((LEAVES + t) * R, R), :] = jnp.concatenate([zero, full], axis=1)
    for step in range(DEPTH + N_BRANCH - 1):
        lanes = pl.ds(step * 2 * R, 2 * R)
        for g in range(2):
            if step == 0:
                mat = cou[step, g]
            elif step < DEPTH:
                mat = dot(downs[step - 1], cou[step, g]).astype(bf16)
            else:
                mat = dot(downs[DEPTH - 1], tops[g, 0, step - DEPTH]).astype(bf16)
            pair = [mat, zero] if g == 0 else [zero, mat]
            fold[pl.ds(g * R, R), lanes] = jnp.concatenate(pair, axis=1)


def prep_call(cou, tops, downs, bas, tra):
    return pl.pallas_call(
        prep_kernel,
        out_shape=[
            pltpu.VMEM((2 * R, (DEPTH + N_BRANCH - 1) * 2 * R), bf16),
            pltpu.VMEM((2 * LEAVES * R, 2 * R), bf16),
        ],
        in_specs=[VMEM] * 5,
        out_specs=[VMEM] * 2,
        compiler_params=pltpu.CompilerParams(vmem_limit_bytes=8 * MB),
        cost_estimate=pl.CostEstimate(
            flops=10**8, bytes_accessed=4 * 10**6, transcendentals=0
        ),
        name="prep",
    )(cou, tops, downs, bas, tra)


def mid_kernel(got, summit, lift, parts, fan):
    leaf = lax.axis_index("leaf")
    for step in range(DEPTH):
        total = None
        for i in range(1 << step, 2 << step):
            v = got[jnp.bitwise_xor(leaf, i)].astype(f32)
            total = v if total is None else total + v
        parts[:, pl.ds(step * 2 * R, 2 * R)] = total.astype(bf16)
    root = (dot(parts[...], lift[...]) + summit[...].astype(f32)).astype(bf16)
    for b in range(N_BRANCH):
        fan[b] = root


def mid_call(got, summit, lift):
    return pl.pallas_call(
        mid_kernel,
        out_shape=[
            pltpu.VMEM((RHS, DEPTH * 2 * R), bf16),
            pltpu.VMEM((N_BRANCH, RHS, 2 * R), bf16),
        ],
        in_specs=[VMEM] * 3,
        out_specs=[VMEM] * 2,
        compiler_params=pltpu.CompilerParams(vmem_limit_bytes=8 * MB),
        name="mid",
    )(got, summit, lift)


def local_kernel(
    own, even, odd, coupling, near, coupling_source, near_source, transfer, basis,
    base, wide, sums, cells, cou, nea, cosrc, nesrc, tra, bas, sem,
):
    smalls = [
        pltpu.make_async_copy(coupling_source, cosrc, sem.at[0]),
        pltpu.make_async_copy(near_source, nesrc, sem.at[1]),
        pltpu.make_async_copy(transfer, tra, sem.at[2]),
        pltpu.make_async_copy(basis, bas, sem.at[3]),
    ]
    bigs = []
    for n, (source, into, start, count) in enumerate(
        ((coupling, cou, 8, 6), (coupling, cou, 0, 4), (coupling, cou, 4, 4),
         (near, nea, 0, 4), (near, nea, 4, 4))
    ):
        span = pl.ds(start, count)
        bigs.append(pltpu.make_async_copy(source.at[:, span], into.at[:, span], sem.at[4 + n]))
    for copy in smalls[:2] + bigs + smalls[2:]:
        copy.start()
    left = lax.broadcasted_iota(jnp.int32, (RHS, 2 * R), 1) < R
    here = jnp.bitwise_and(lax.axis_index("leaf"), 1)
    for part, ref in ((1, own), (2 - 2 * here, even), (2 * here, odd)):
        for row in range(ROWS):
            v = ref[row]
            s = turned(v)
            wide[0, part * ROWS + row] = jnp.where(left, v, s)
            wide[1, part * ROWS + row] = jnp.where(left, s, v)

    def block(picked, mats):
        result = []
        for g in range(2):
            acc = None
            for j in range(0, LINKS, 4):
                v = jnp.concatenate(
                    [
                        jnp.where(left, wide[g, picked[j]], wide[g, picked[j + 1]]),
                        jnp.where(left, wide[g, picked[j + 2]], wide[g, picked[j + 3]]),
                    ],
                    axis=1,
                )
                m = jnp.concatenate([mats(g, j + n) for n in range(4)], axis=1)
                part = dot_nt(v, m)
                acc = part if acc is None else acc + part
            result.append(acc)
        return jnp.concatenate(result, axis=0)

    def far_body(log, start, t):
        r = start + t
        picked = []
        for j in range(LINKS):
            s = cosrc[r, j]
            picked.append(
                jnp.right_shift(s, log) * ROWS
                + LEAVES
                + start
                + jnp.bitwise_and(s, (1 << log) - 1)
            )
        sums[r] = block(picked, lambda g, j: cou[g, r, j])

    def near_body(t):
        picked = []
        for j in range(LINKS):
            s = nesrc[t, j]
            picked.append(jnp.right_shift(s, 3) * ROWS + jnp.bitwise_and(s, 7))
        cells[t] = block(picked, lambda g, j: nea[g, t, j])

    def each(body, first, count):
        def step(i, carry):
            body(first + i)
            return carry

        lax.fori_loop(0, count, step, 0, unroll=min(UNROLL, count))

    for copy in smalls[:2]:
        copy.wait()
    bigs[0].wait()
    each(functools.partial(far_body, 1, 12), 0, 2)
    each(functools.partial(far_body, 2, 8), 0, 4)
    bigs[1].wait()
    each(functools.partial(far_body, 3, 0), 0, 4)
    bigs[2].wait()
    each(functools.partial(far_body, 3, 0), 4, 4)
    bigs[3].wait()
    each(near_body, 0, 4)
    bigs[4].wait()
    each(near_body, 4, 4)
    for copy in smalls[2:]:
        copy.wait()
    up2 = [sums[12 + t].astype(bf16) for t in range(2)]
    up1 = [
        (sums[8 + t] + dot_nt(up2[t // 2], tra[8 + t])).astype(bf16) for t in range(4)
    ]
    up0 = [(sums[t] + dot_nt(up1[t // 2], tra[t])).astype(bf16) for t in range(8)]
    full = [cells[t] + dot_nt(up0[t], bas[t]) for t in range(8)]
    for pair in range(LEAVES // 2):
        both = jnp.concatenate([full[2 * pair], full[2 * pair + 1]], axis=1)
        for g in range(2):
            base[g, :, pl.ds(pair * 2 * R, 2 * R)] = both[g * RHS : (g + 1) * RHS]


def local_call(own, even, odd, coupling_source, near_source, coupling, near, transfer, basis):
    return pl.pallas_call(
        local_kernel,
        out_shape=pltpu.VMEM((2, RHS, LEAVES * R), f32),
        in_specs=[VMEM] * 3 + [ANY] * 6,
        out_specs=VMEM,
        scratch_shapes=[
            pltpu.VMEM((2, 3 * ROWS, RHS, 2 * R), bf16),
            pltpu.VMEM((LOCAL, 2 * RHS, R), f32),
            pltpu.VMEM((LEAVES, 2 * RHS, R), f32),
            pltpu.VMEM((2, LOCAL, LINKS, R, R), bf16),
            pltpu.VMEM((2, LEAVES, LINKS, R, R), bf16),
            pltpu.SMEM((LOCAL, LINKS), jnp.int32),
            pltpu.SMEM((LEAVES, LINKS), jnp.int32),
            pltpu.VMEM((LOCAL, R, R), bf16),
            pltpu.VMEM((LEAVES, R, R), bf16),
            pltpu.SemaphoreType.DMA((9,)),
        ],
        compiler_params=pltpu.CompilerParams(vmem_limit_bytes=24 * MB),
        cost_estimate=pl.CostEstimate(
            flops=10**8, bytes_accessed=2 * 10**7, transcendentals=0
        ),
        name="local",
    )(
        own, even, odd,
        *hbm(coupling, near, coupling_source, near_source, transfer, basis),
    )


def final_kernel(parts, roots, fold, leafs, base, out):
    branch = lax.axis_index("branch")
    others = [roots[(branch + 1 + i) % N_BRANCH] for i in range(N_BRANCH - 1)]
    row = jnp.concatenate([parts[...]] + others, axis=1)
    target = dot_nt(row, fold[...]).astype(bf16)
    far = dot_nt(target, leafs[...])
    width = LEAVES * R
    for g in range(2):
        out[g] = base[g] + far[:, g * width : (g + 1) * width]


def final_call(parts, roots, fold, leafs, base):
    return pl.pallas_call(
        final_kernel,
        out_shape=jax.ShapeDtypeStruct((2, RHS, LEAVES * R), f32),
        in_specs=[VMEM] * 5,
        out_specs=VMEM,
        compiler_params=pltpu.CompilerParams(vmem_limit_bytes=8 * MB),
        name="final",
    )(parts, roots, fold, leafs, base)


def per_device(
    values,
    leaf_basis,
    transfer,
    local_coupling,
    coupling_source,
    near_field,
    near_source,
    upper_transfer,
    upper_coupling,
    top_coupling,
):
    vals, coefs, sent, summit, downs, own, sib, cou, tops, bas, tra = up_call(
        values, leaf_basis, transfer, upper_transfer, upper_coupling, top_coupling
    )
    got = lax.all_to_all(sent, "leaf", 0, 0, tiled=True)
    lift = cast_call(own, sib)
    fold, leafs = prep_call(cou, tops, downs, bas, tra)
    rows = pack_call(vals, coefs)
    count = N_BRANCH * N_LEAF
    ring = ("branch", "leaf")
    even = lax.ppermute(rows, ring, [(i, i ^ 1) for i in range(count)])
    odd = lax.ppermute(
        rows, ring, [(i, ((i + 1) ^ 1) - 1) for i in range(1, count - 1)]
    )
    parts, fan = mid_call(got, summit, lift)
    parts, fan, even, odd, fold, leafs = lax.optimization_barrier(
        (parts, fan, even, odd, fold, leafs)
    )
    roots = lax.all_to_all(fan, "branch", 0, 0, tiled=True)
    base = local_call(
        rows, even, odd, coupling_source, near_source, local_coupling, near_field,
        transfer, leaf_basis,
    )
    return final_call(parts, roots, fold, leafs, base)


def solution(mesh):
    in_specs = (
        P(None, None, ("branch", "leaf")),
        P(("branch", "leaf"), None, None),
        P(("branch", "leaf"), None, None),
        P(None, ("branch", "leaf"), None, None, None),
        P(("branch", "leaf"), None),
        P(None, ("branch", "leaf"), None, None, None),
        P(("branch", "leaf"), None),
        P("branch", None, None, None),
        P(None, "branch", None, None, None),
        P(None, "branch", None, None, None),
    )
    out_specs = P(None, None, ("branch", "leaf"))
    return jax.shard_map(
        per_device, mesh=mesh, in_specs=in_specs, out_specs=out_specs, check_vma=False
    )
```

```python
import functools

import jax
import jax.numpy as jnp
from jax import lax
from jax.experimental import pallas as pl
from jax.experimental.pallas import tpu as pltpu
from jax.sharding import PartitionSpec as P

f32 = jnp.float32
bf16 = jnp.bfloat16
R = 64
RHS = 16
LEAVES = 8
LOCAL = 14
ROWS = 22
DEPTH = 5
N_LEAF = 32
N_BRANCH = 8
LINKS = 12
UNROLL = 4
ANY = pl.BlockSpec(memory_space=pl.ANY)
VMEM = pl.BlockSpec(memory_space=pltpu.VMEM)
MB = 2**20


def hbm(*arrays):
    return [pltpu.with_memory_space_constraint(a, pltpu.HBM) for a in arrays]


def dot(a, b):
    return jnp.dot(a, b, preferred_element_type=f32)


def dot_nt(a, b):
    return lax.dot_general(a, b, (((1,), (1,)), ((), ())), preferred_element_type=f32)


def turned(v):
    return jnp.concatenate([v[:, R:], v[:, :R]], axis=1)


def packed(c):
    return jnp.concatenate([c[:RHS], c[RHS:]], axis=1)


def upper_index(leaf, step):
    return 2 * N_LEAF - 2 * (N_LEAF >> step) + jnp.right_shift(leaf, step)


def up_kernel(
    values, basis, transfer, upper, couple, top,
    vals, coefs, sent, summit, downs, upp, sib, cou, tops, bas, tra, sem,
):
    leaf = lax.axis_index("leaf")
    here = [upper_index(leaf, step) for step in range(DEPTH)]
    firsts = [
        pltpu.make_async_copy(values, vals, sem.at[0]),
        pltpu.make_async_copy(basis, bas, sem.at[1]),
        pltpu.make_async_copy(transfer, tra, sem.at[2]),
    ]
    lasts = [pltpu.make_async_copy(top, tops, sem.at[3])]
    for k in range(DEPTH):
        there = jnp.bitwise_xor(here[k], 1)
        firsts.append(pltpu.make_async_copy(upper.at[0, here[k]], upp.at[k], sem.at[4 + 3 * k]))
        lasts.append(pltpu.make_async_copy(upper.at[0, there], sib.at[k], sem.at[5 + 3 * k]))
        lasts.append(
            pltpu.make_async_copy(couple.at[:, 0, here[k]], cou.at[k], sem.at[6 + 3 * k])
        )
    for copy in firsts + lasts:
        copy.start()
    for copy in firsts:
        copy.wait()
    down = upp[0]
    downs[0] = down
    for step in range(1, DEPTH):
        down = dot(down, upp[step]).astype(bf16)
        downs[step] = down
    level = []
    for pair in range(LEAVES // 2):
        x0 = vals[0, :, pl.ds(pair * 2 * R, 2 * R)]
        x1 = vals[1, :, pl.ds(pair * 2 * R, 2 * R)]
        for half in range(2):
            lanes = slice(half * R, (half + 1) * R)
            cell = jnp.concatenate([x0[:, lanes], x1[:, lanes]], axis=0)
            level.append(dot(cell, bas[2 * pair + half]).astype(bf16))
    begin = 0
    while len(level) > 1:
        for i, c in enumerate(level):
            coefs[begin + i] = c
        merged = [
            (dot(level[i], tra[begin + i]) + dot(level[i + 1], tra[begin + i + 1])).astype(bf16)
            for i in range(0, len(level), 2)
        ]
        begin += len(level)
        level = merged
    root = level[0]
    chain = [packed(root)]
    for step in range(DEPTH):
        chain.append(packed(dot(root, downs[step]).astype(bf16)))
    summit[...] = chain[DEPTH]
    sent[leaf] = chain[0]
    for i in range(1, N_LEAF):
        sent[jnp.bitwise_xor(leaf, i)] = chain[i.bit_length() - 1]
    for copy in lasts:
        copy.wait()


def up_call(values, basis, transfer, upper, couple, top):
    return pl.pallas_call(
        up_kernel,
        out_shape=[
            pltpu.VMEM((2, RHS, LEAVES * R), bf16),
            pltpu.VMEM((LOCAL, 2 * RHS, R), bf16),
            pltpu.VMEM((N_LEAF, RHS, 2 * R), bf16),
            pltpu.VMEM((RHS, 2 * R), bf16),
            pltpu.VMEM((DEPTH, R, R), bf16),
            pltpu.VMEM((DEPTH, R, R), bf16),
            pltpu.VMEM((DEPTH, R, R), bf16),
            pltpu.VMEM((DEPTH, 2, R, R), bf16),
            pltpu.VMEM((2, 1, N_BRANCH - 1, R, R), bf16),
            pltpu.VMEM((LEAVES, R, R), bf16),
            pltpu.VMEM((LOCAL, R, R), bf16),
        ],
        in_specs=[ANY] * 6,
        out_specs=[VMEM] * 11,
        scratch_shapes=[pltpu.SemaphoreType.DMA((4 + 3 * DEPTH,))],
        compiler_params=pltpu.CompilerParams(vmem_limit_bytes=8 * MB),
        name="up",
    )(*hbm(values, basis, transfer, upper, couple, top))


def pack_kernel(vals, coefs, rows):
    left = lax.broadcasted_iota(jnp.int32, (RHS, 2 * R), 1) < R
    for pair in range(LEAVES // 2):
        x0 = vals[0, :, pl.ds(pair * 2 * R, 2 * R)]
        x1 = vals[1, :, pl.ds(pair * 2 * R, 2 * R)]
        rows[2 * pair] = jnp.where(left, x0, turned(x1))
        rows[2 * pair + 1] = jnp.where(left, turned(x0), x1)
    for i in range(LOCAL):
        rows[LEAVES + i] = packed(coefs[i])


def pack_call(vals, coefs):
    return pl.pallas_call(
        pack_kernel,
        out_shape=pltpu.VMEM((ROWS, RHS, 2 * R), bf16),
        in_specs=[VMEM] * 2,
        out_specs=VMEM,
        compiler_params=pltpu.CompilerParams(vmem_limit_bytes=8 * MB),
        cost_estimate=pl.CostEstimate(
            flops=10**8, bytes_accessed=4 * 10**6, transcendentals=0
        ),
        name="pack",
    )(vals, coefs)


def cast_kernel(own, sib, lift):
    zero = jnp.zeros((R, R), bf16)

    def place(step, mat):
        lift[pl.ds(2 * step * R, R), :] = jnp.concatenate([mat, zero], axis=1)
        lift[pl.ds((2 * step + 1) * R, R), :] = jnp.concatenate([zero, mat], axis=1)

    path = own[DEPTH - 1]
    place(DEPTH - 1, sib[DEPTH - 1])
    for step in range(DEPTH - 2, -1, -1):
        place(step, dot(sib[step], path).astype(bf16))
        if step:
            path = dot(own[step], path).astype(bf16)


def cast_call(own, sib):
    return pl.pallas_call(
        cast_kernel,
        out_shape=pltpu.VMEM((DEPTH * 2 * R, 2 * R), bf16),
        in_specs=[VMEM] * 2,
        out_specs=VMEM,
        compiler_params=pltpu.CompilerParams(vmem_limit_bytes=8 * MB),
        cost_estimate=pl.CostEstimate(
            flops=10**8, bytes_accessed=4 * 10**6, transcendentals=0
        ),
        name="cast",
    )(own, sib)


def prep_kernel(cou, tops, downs, bas, tra, fold, leafs):
    zero = jnp.zeros((R, R), bf16)
    tops2 = [tra[12 + t] for t in range(2)]
    tops1 = [dot(tra[8 + t], tops2[t // 2]).astype(bf16) for t in range(4)]
    tops0 = [dot(tra[t], tops1[t // 2]).astype(bf16) for t in range(8)]
    for t in range(LEAVES):
        full = dot(bas[t], tops0[t]).astype(bf16)
        leafs[pl.ds(t * R, R), :] = jnp.concatenate([full, zero], axis=1)
        leafs[pl.ds((LEAVES + t) * R, R), :] = jnp.concatenate([zero, full], axis=1)
    for step in range(DEPTH + N_BRANCH - 1):
        lanes = pl.ds(step * 2 * R, 2 * R)
        for g in range(2):
            if step == 0:
                mat = cou[step, g]
            elif step < DEPTH:
                mat = dot(downs[step - 1], cou[step, g]).astype(bf16)
            else:
                mat = dot(downs[DEPTH - 1], tops[g, 0, step - DEPTH]).astype(bf16)
            pair = [mat, zero] if g == 0 else [zero, mat]
            fold[pl.ds(g * R, R), lanes] = jnp.concatenate(pair, axis=1)


def prep_call(cou, tops, downs, bas, tra):
    return pl.pallas_call(
        prep_kernel,
        out_shape=[
            pltpu.VMEM((2 * R, (DEPTH + N_BRANCH - 1) * 2 * R), bf16),
            pltpu.VMEM((2 * LEAVES * R, 2 * R), bf16),
        ],
        in_specs=[VMEM] * 5,
        out_specs=[VMEM] * 2,
        compiler_params=pltpu.CompilerParams(vmem_limit_bytes=8 * MB),
        cost_estimate=pl.CostEstimate(
            flops=10**8, bytes_accessed=4 * 10**6, transcendentals=0
        ),
        name="prep",
    )(cou, tops, downs, bas, tra)


def mid_kernel(got, summit, lift, parts, fan):
    leaf = lax.axis_index("leaf")
    for step in range(DEPTH):
        total = None
        for i in range(1 << step, 2 << step):
            v = got[jnp.bitwise_xor(leaf, i)].astype(f32)
            total = v if total is None else total + v
        parts[:, pl.ds(step * 2 * R, 2 * R)] = total.astype(bf16)
    root = (dot(parts[...], lift[...]) + summit[...].astype(f32)).astype(bf16)
    for b in range(N_BRANCH):
        fan[b] = root


def mid_call(got, summit, lift):
    return pl.pallas_call(
        mid_kernel,
        out_shape=[
            pltpu.VMEM((RHS, DEPTH * 2 * R), bf16),
            pltpu.VMEM((N_BRANCH, RHS, 2 * R), bf16),
        ],
        in_specs=[VMEM] * 3,
        out_specs=[VMEM] * 2,
        compiler_params=pltpu.CompilerParams(vmem_limit_bytes=8 * MB),
        name="mid",
    )(got, summit, lift)


def local_kernel(
    own, even, odd, coupling, near, coupling_source, near_source, transfer, basis,
    base, wide, sums, cells, cou, nea, cosrc, nesrc, tra, bas, sem,
):
    smalls = [
        pltpu.make_async_copy(coupling_source, cosrc, sem.at[0]),
        pltpu.make_async_copy(near_source, nesrc, sem.at[1]),
        pltpu.make_async_copy(transfer, tra, sem.at[2]),
        pltpu.make_async_copy(basis, bas, sem.at[3]),
    ]
    bigs = []
    for n, (source, into, start, count) in enumerate(
        ((coupling, cou, 8, 6), (coupling, cou, 0, 4), (coupling, cou, 4, 4),
         (near, nea, 0, 4), (near, nea, 4, 4))
    ):
        span = pl.ds(start, count)
        bigs.append(pltpu.make_async_copy(source.at[:, span], into.at[:, span], sem.at[4 + n]))
    for copy in smalls[:2] + bigs + smalls[2:]:
        copy.start()
    left = lax.broadcasted_iota(jnp.int32, (RHS, 2 * R), 1) < R
    here = jnp.bitwise_and(lax.axis_index("leaf"), 1)
    for part, ref in ((1, own), (2 - 2 * here, even), (2 * here, odd)):
        for row in range(ROWS):
            v = ref[row]
            s = turned(v)
            wide[0, part * ROWS + row] = jnp.where(left, v, s)
            wide[1, part * ROWS + row] = jnp.where(left, s, v)

    def block(picked, mats):
        result = []
        for g in range(2):
            acc = None
            for j in range(0, LINKS, 4):
                v = jnp.concatenate(
                    [
                        jnp.where(left, wide[g, picked[j]], wide[g, picked[j + 1]]),
                        jnp.where(left, wide[g, picked[j + 2]], wide[g, picked[j + 3]]),
                    ],
                    axis=1,
                )
                m = jnp.concatenate([mats(g, j + n) for n in range(4)], axis=1)
                part = dot_nt(v, m)
                acc = part if acc is None else acc + part
            result.append(acc)
        return jnp.concatenate(result, axis=0)

    def far_body(log, start, t):
        r = start + t
        picked = []
        for j in range(LINKS):
            s = cosrc[r, j]
            picked.append(
                jnp.right_shift(s, log) * ROWS
                + LEAVES
                + start
                + jnp.bitwise_and(s, (1 << log) - 1)
            )
        sums[r] = block(picked, lambda g, j: cou[g, r, j])

    def near_body(t):
        picked = []
        for j in range(LINKS):
            s = nesrc[t, j]
            picked.append(jnp.right_shift(s, 3) * ROWS + jnp.bitwise_and(s, 7))
        cells[t] = block(picked, lambda g, j: nea[g, t, j])

    def each(body, first, count):
        def step(i, carry):
            body(first + i)
            return carry

        lax.fori_loop(0, count, step, 0, unroll=min(UNROLL, count))

    for copy in smalls[:2]:
        copy.wait()
    bigs[0].wait()
    each(functools.partial(far_body, 1, 12), 0, 2)
    each(functools.partial(far_body, 2, 8), 0, 4)
    bigs[1].wait()
    each(functools.partial(far_body, 3, 0), 0, 4)
    bigs[2].wait()
    each(functools.partial(far_body, 3, 0), 4, 4)
    bigs[3].wait()
    each(near_body, 0, 4)
    bigs[4].wait()
    each(near_body, 4, 4)
    for copy in smalls[2:]:
        copy.wait()
    up2 = [sums[12 + t].astype(bf16) for t in range(2)]
    up1 = [
        (sums[8 + t] + dot_nt(up2[t // 2], tra[8 + t])).astype(bf16) for t in range(4)
    ]
    up0 = [(sums[t] + dot_nt(up1[t // 2], tra[t])).astype(bf16) for t in range(8)]
    full = [cells[t] + dot_nt(up0[t], bas[t]) for t in range(8)]
    for pair in range(LEAVES // 2):
        both = jnp.concatenate([full[2 * pair], full[2 * pair + 1]], axis=1)
        for g in range(2):
            base[g, :, pl.ds(pair * 2 * R, 2 * R)] = both[g * RHS : (g + 1) * RHS]


def local_call(own, even, odd, coupling_source, near_source, coupling, near, transfer, basis):
    return pl.pallas_call(
        local_kernel,
        out_shape=pltpu.VMEM((2, RHS, LEAVES * R), f32),
        in_specs=[VMEM] * 3 + [ANY] * 6,
        out_specs=VMEM,
        scratch_shapes=[
            pltpu.VMEM((2, 3 * ROWS, RHS, 2 * R), bf16),
            pltpu.VMEM((LOCAL, 2 * RHS, R), f32),
            pltpu.VMEM((LEAVES, 2 * RHS, R), f32),
            pltpu.VMEM((2, LOCAL, LINKS, R, R), bf16),
            pltpu.VMEM((2, LEAVES, LINKS, R, R), bf16),
            pltpu.SMEM((LOCAL, LINKS), jnp.int32),
            pltpu.SMEM((LEAVES, LINKS), jnp.int32),
            pltpu.VMEM((LOCAL, R, R), bf16),
            pltpu.VMEM((LEAVES, R, R), bf16),
            pltpu.SemaphoreType.DMA((9,)),
        ],
        compiler_params=pltpu.CompilerParams(vmem_limit_bytes=24 * MB),
        cost_estimate=pl.CostEstimate(
            flops=10**8, bytes_accessed=2 * 10**7, transcendentals=0
        ),
        name="local",
    )(
        own, even, odd,
        *hbm(coupling, near, coupling_source, near_source, transfer, basis),
    )


def final_kernel(parts, roots, fold, leafs, base, out):
    branch = lax.axis_index("branch")
    others = [roots[(branch + 1 + i) % N_BRANCH] for i in range(N_BRANCH - 1)]
    row = jnp.concatenate([parts[...]] + others, axis=1)
    target = dot_nt(row, fold[...]).astype(bf16)
    far = dot_nt(target, leafs[...])
    width = LEAVES * R
    for g in range(2):
        out[g] = base[g] + far[:, g * width : (g + 1) * width]


def final_call(parts, roots, fold, leafs, base):
    return pl.pallas_call(
        final_kernel,
        out_shape=jax.ShapeDtypeStruct((2, RHS, LEAVES * R), f32),
        in_specs=[VMEM] * 5,
        out_specs=VMEM,
        compiler_params=pltpu.CompilerParams(vmem_limit_bytes=8 * MB),
        name="final",
    )(parts, roots, fold, leafs, base)


def per_device(
    values,
    leaf_basis,
    transfer,
    local_coupling,
    coupling_source,
    near_field,
    near_source,
    upper_transfer,
    upper_coupling,
    top_coupling,
):
    vals, coefs, sent, summit, downs, own, sib, cou, tops, bas, tra = up_call(
        values, leaf_basis, transfer, upper_transfer, upper_coupling, top_coupling
    )
    got = lax.all_to_all(sent, "leaf", 0, 0, tiled=True)
    lift = cast_call(own, sib)
    fold, leafs = prep_call(cou, tops, downs, bas, tra)
    rows = pack_call(vals, coefs)
    count = N_BRANCH * N_LEAF
    ring = ("branch", "leaf")
    even = lax.ppermute(rows, ring, [(i, i ^ 1) for i in range(count)])
    odd = lax.ppermute(
        rows, ring, [(i, ((i + 1) ^ 1) - 1) for i in range(1, count - 1)]
    )
    parts, fan = mid_call(got, summit, lift)
    parts, fan, even, fold, leafs = lax.optimization_barrier((parts, fan, even, fold, leafs))
    roots = lax.all_to_all(fan, "branch", 0, 0, tiled=True)
    base = local_call(
        rows, even, odd, coupling_source, near_source, local_coupling, near_field,
        transfer, leaf_basis,
    )
    return final_call(parts, roots, fold, leafs, base)


def solution(mesh):
    in_specs = (
        P(None, None, ("branch", "leaf")),
        P(("branch", "leaf"), None, None),
        P(("branch", "leaf"), None, None),
        P(None, ("branch", "leaf"), None, None, None),
        P(("branch", "leaf"), None),
        P(None, ("branch", "leaf"), None, None, None),
        P(("branch", "leaf"), None),
        P("branch", None, None, None),
        P(None, "branch", None, None, None),
        P(None, "branch", None, None, None),
    )
    out_specs = P(None, None, ("branch", "leaf"))
    return jax.shard_map(
        per_device, mesh=mesh, in_specs=in_specs, out_specs=out_specs, check_vma=False
    )
```

```python
import functools

import jax
import jax.numpy as jnp
from jax import lax
from jax.experimental import pallas as pl
from jax.experimental.pallas import tpu as pltpu
from jax.sharding import PartitionSpec as P

f32 = jnp.float32
bf16 = jnp.bfloat16
R = 64
RHS = 16
LEAVES = 8
LOCAL = 14
ROWS = 22
DEPTH = 5
N_LEAF = 32
N_BRANCH = 8
LINKS = 12
UNROLL = 4
ANY = pl.BlockSpec(memory_space=pl.ANY)
VMEM = pl.BlockSpec(memory_space=pltpu.VMEM)
MB = 2**20


def hbm(*arrays):
    return [pltpu.with_memory_space_constraint(a, pltpu.HBM) for a in arrays]


def dot(a, b):
    return jnp.dot(a, b, preferred_element_type=f32)


def dot_nt(a, b):
    return lax.dot_general(a, b, (((1,), (1,)), ((), ())), preferred_element_type=f32)


def turned(v):
    return jnp.concatenate([v[:, R:], v[:, :R]], axis=1)


def packed(c):
    return jnp.concatenate([c[:RHS], c[RHS:]], axis=1)


def upper_index(leaf, step):
    return 2 * N_LEAF - 2 * (N_LEAF >> step) + jnp.right_shift(leaf, step)


def seat(leaf):
    return N_LEAF - 1 - leaf


def up_kernel(
    values, basis, transfer, upper, couple, top,
    vals, coefs, sent, summit, downs, upp, sib, cou, tops, bas, tra, sem,
):
    leaf = lax.axis_index("leaf")
    here = [upper_index(leaf, step) for step in range(DEPTH)]
    firsts = [
        pltpu.make_async_copy(values, vals, sem.at[0]),
        pltpu.make_async_copy(basis, bas, sem.at[1]),
        pltpu.make_async_copy(transfer, tra, sem.at[2]),
    ]
    lasts = [pltpu.make_async_copy(top, tops, sem.at[3])]
    for k in range(DEPTH):
        there = jnp.bitwise_xor(here[k], 1)
        firsts.append(pltpu.make_async_copy(upper.at[0, here[k]], upp.at[k], sem.at[4 + 3 * k]))
        lasts.append(pltpu.make_async_copy(upper.at[0, there], sib.at[k], sem.at[5 + 3 * k]))
        lasts.append(
            pltpu.make_async_copy(couple.at[:, 0, here[k]], cou.at[k], sem.at[6 + 3 * k])
        )
    for copy in firsts + lasts:
        copy.start()
    for copy in firsts:
        copy.wait()
    down = upp[0]
    downs[0] = down
    for step in range(1, DEPTH):
        down = dot(down, upp[step]).astype(bf16)
        downs[step] = down
    level = []
    for pair in range(LEAVES // 2):
        x0 = vals[0, :, pl.ds(pair * 2 * R, 2 * R)]
        x1 = vals[1, :, pl.ds(pair * 2 * R, 2 * R)]
        for half in range(2):
            lanes = slice(half * R, (half + 1) * R)
            cell = jnp.concatenate([x0[:, lanes], x1[:, lanes]], axis=0)
            level.append(dot(cell, bas[2 * pair + half]).astype(bf16))
    begin = 0
    while len(level) > 1:
        for i, c in enumerate(level):
            coefs[begin + i] = c
        merged = [
            (dot(level[i], tra[begin + i]) + dot(level[i + 1], tra[begin + i + 1])).astype(bf16)
            for i in range(0, len(level), 2)
        ]
        begin += len(level)
        level = merged
    root = level[0]
    chain = [packed(root)]
    for step in range(DEPTH):
        chain.append(packed(dot(root, downs[step]).astype(bf16)))
    summit[...] = chain[DEPTH]
    sent[seat(leaf)] = chain[0]
    for i in range(1, N_LEAF):
        sent[seat(jnp.bitwise_xor(leaf, i))] = chain[i.bit_length() - 1]
    for copy in lasts:
        copy.wait()


def up_call(values, basis, transfer, upper, couple, top):
    return pl.pallas_call(
        up_kernel,
        out_shape=[
            pltpu.VMEM((2, RHS, LEAVES * R), bf16),
            pltpu.VMEM((LOCAL, 2 * RHS, R), bf16),
            pltpu.VMEM((N_LEAF, RHS, 2 * R), bf16),
            pltpu.VMEM((RHS, 2 * R), bf16),
            pltpu.VMEM((DEPTH, R, R), bf16),
            pltpu.VMEM((DEPTH, R, R), bf16),
            pltpu.VMEM((DEPTH, R, R), bf16),
            pltpu.VMEM((DEPTH, 2, R, R), bf16),
            pltpu.VMEM((2, 1, N_BRANCH - 1, R, R), bf16),
            pltpu.VMEM((LEAVES, R, R), bf16),
            pltpu.VMEM((LOCAL, R, R), bf16),
        ],
        in_specs=[ANY] * 6,
        out_specs=[VMEM] * 11,
        scratch_shapes=[pltpu.SemaphoreType.DMA((4 + 3 * DEPTH,))],
        compiler_params=pltpu.CompilerParams(vmem_limit_bytes=8 * MB),
        name="up",
    )(*hbm(values, basis, transfer, upper, couple, top))


def pack_kernel(vals, coefs, rows):
    left = lax.broadcasted_iota(jnp.int32, (RHS, 2 * R), 1) < R
    for pair in range(LEAVES // 2):
        x0 = vals[0, :, pl.ds(pair * 2 * R, 2 * R)]
        x1 = vals[1, :, pl.ds(pair * 2 * R, 2 * R)]
        rows[2 * pair] = jnp.where(left, x0, turned(x1))
        rows[2 * pair + 1] = jnp.where(left, turned(x0), x1)
    for i in range(LOCAL):
        rows[LEAVES + i] = packed(coefs[i])


def pack_call(vals, coefs):
    return pl.pallas_call(
        pack_kernel,
        out_shape=pltpu.VMEM((ROWS, RHS, 2 * R), bf16),
        in_specs=[VMEM] * 2,
        out_specs=VMEM,
        compiler_params=pltpu.CompilerParams(vmem_limit_bytes=8 * MB),
        cost_estimate=pl.CostEstimate(
            flops=10**8, bytes_accessed=4 * 10**6, transcendentals=0
        ),
        name="pack",
    )(vals, coefs)


def cast_kernel(own, sib, lift):
    zero = jnp.zeros((R, R), bf16)

    def place(step, mat):
        lift[pl.ds(2 * step * R, R), :] = jnp.concatenate([mat, zero], axis=1)
        lift[pl.ds((2 * step + 1) * R, R), :] = jnp.concatenate([zero, mat], axis=1)

    path = own[DEPTH - 1]
    place(DEPTH - 1, sib[DEPTH - 1])
    for step in range(DEPTH - 2, -1, -1):
        place(step, dot(sib[step], path).astype(bf16))
        if step:
            path = dot(own[step], path).astype(bf16)


def cast_call(own, sib):
    return pl.pallas_call(
        cast_kernel,
        out_shape=pltpu.VMEM((DEPTH * 2 * R, 2 * R), bf16),
        in_specs=[VMEM] * 2,
        out_specs=VMEM,
        compiler_params=pltpu.CompilerParams(vmem_limit_bytes=8 * MB),
        cost_estimate=pl.CostEstimate(
            flops=10**8, bytes_accessed=4 * 10**6, transcendentals=0
        ),
        name="cast",
    )(own, sib)


def prep_kernel(cou, tops, downs, bas, tra, fold, leafs):
    zero = jnp.zeros((R, R), bf16)
    tops2 = [tra[12 + t] for t in range(2)]
    tops1 = [dot(tra[8 + t], tops2[t // 2]).astype(bf16) for t in range(4)]
    tops0 = [dot(tra[t], tops1[t // 2]).astype(bf16) for t in range(8)]
    for t in range(LEAVES):
        full = dot(bas[t], tops0[t]).astype(bf16)
        leafs[pl.ds(t * R, R), :] = jnp.concatenate([full, zero], axis=1)
        leafs[pl.ds((LEAVES + t) * R, R), :] = jnp.concatenate([zero, full], axis=1)
    for step in range(DEPTH + N_BRANCH - 1):
        lanes = pl.ds(step * 2 * R, 2 * R)
        for g in range(2):
            if step == 0:
                mat = cou[step, g]
            elif step < DEPTH:
                mat = dot(downs[step - 1], cou[step, g]).astype(bf16)
            else:
                mat = dot(downs[DEPTH - 1], tops[g, 0, step - DEPTH]).astype(bf16)
            pair = [mat, zero] if g == 0 else [zero, mat]
            fold[pl.ds(g * R, R), lanes] = jnp.concatenate(pair, axis=1)


def prep_call(cou, tops, downs, bas, tra):
    return pl.pallas_call(
        prep_kernel,
        out_shape=[
            pltpu.VMEM((2 * R, (DEPTH + N_BRANCH - 1) * 2 * R), bf16),
            pltpu.VMEM((2 * LEAVES * R, 2 * R), bf16),
        ],
        in_specs=[VMEM] * 5,
        out_specs=[VMEM] * 2,
        compiler_params=pltpu.CompilerParams(vmem_limit_bytes=8 * MB),
        cost_estimate=pl.CostEstimate(
            flops=10**8, bytes_accessed=4 * 10**6, transcendentals=0
        ),
        name="prep",
    )(cou, tops, downs, bas, tra)


def mid_kernel(got, summit, lift, parts, fan):
    leaf = lax.axis_index("leaf")
    for step in range(DEPTH):
        total = None
        for i in range(1 << step, 2 << step):
            v = got[seat(jnp.bitwise_xor(leaf, i))].astype(f32)
            total = v if total is None else total + v
        parts[:, pl.ds(step * 2 * R, 2 * R)] = total.astype(bf16)
    root = (dot(parts[...], lift[...]) + summit[...].astype(f32)).astype(bf16)
    for b in range(N_BRANCH):
        fan[b] = root


def mid_call(got, summit, lift):
    return pl.pallas_call(
        mid_kernel,
        out_shape=[
            pltpu.VMEM((RHS, DEPTH * 2 * R), bf16),
            pltpu.VMEM((N_BRANCH, RHS, 2 * R), bf16),
        ],
        in_specs=[VMEM] * 3,
        out_specs=[VMEM] * 2,
        compiler_params=pltpu.CompilerParams(vmem_limit_bytes=8 * MB),
        name="mid",
    )(got, summit, lift)


def local_kernel(
    own, even, odd, coupling, near, coupling_source, near_source, transfer, basis,
    base, wide, sums, cells, cou, nea, cosrc, nesrc, tra, bas, sem,
):
    smalls = [
        pltpu.make_async_copy(coupling_source, cosrc, sem.at[0]),
        pltpu.make_async_copy(near_source, nesrc, sem.at[1]),
        pltpu.make_async_copy(transfer, tra, sem.at[2]),
        pltpu.make_async_copy(basis, bas, sem.at[3]),
    ]
    bigs = []
    for n, (source, into, start, count) in enumerate(
        ((coupling, cou, 8, 6), (coupling, cou, 0, 4), (coupling, cou, 4, 4),
         (near, nea, 0, 4), (near, nea, 4, 4))
    ):
        span = pl.ds(start, count)
        bigs.append(pltpu.make_async_copy(source.at[:, span], into.at[:, span], sem.at[4 + n]))
    for copy in smalls[:2] + bigs + smalls[2:]:
        copy.start()
    left = lax.broadcasted_iota(jnp.int32, (RHS, 2 * R), 1) < R
    here = jnp.bitwise_and(lax.axis_index("leaf"), 1)
    for part, ref in ((1, own), (2 - 2 * here, even), (2 * here, odd)):
        for row in range(ROWS):
            v = ref[row]
            s = turned(v)
            wide[0, part * ROWS + row] = jnp.where(left, v, s)
            wide[1, part * ROWS + row] = jnp.where(left, s, v)

    def block(picked, mats):
        result = []
        for g in range(2):
            acc = None
            for j in range(0, LINKS, 4):
                v = jnp.concatenate(
                    [
                        jnp.where(left, wide[g, picked[j]], wide[g, picked[j + 1]]),
                        jnp.where(left, wide[g, picked[j + 2]], wide[g, picked[j + 3]]),
                    ],
                    axis=1,
                )
                m = jnp.concatenate([mats(g, j + n) for n in range(4)], axis=1)
                part = dot_nt(v, m)
                acc = part if acc is None else acc + part
            result.append(acc)
        return jnp.concatenate(result, axis=0)

    def far_body(log, start, t):
        r = start + t
        picked = []
        for j in range(LINKS):
            s = cosrc[r, j]
            picked.append(
                jnp.right_shift(s, log) * ROWS
                + LEAVES
                + start
                + jnp.bitwise_and(s, (1 << log) - 1)
            )
        sums[r] = block(picked, lambda g, j: cou[g, r, j])

    def near_body(t):
        picked = []
        for j in range(LINKS):
            s = nesrc[t, j]
            picked.append(jnp.right_shift(s, 3) * ROWS + jnp.bitwise_and(s, 7))
        cells[t] = block(picked, lambda g, j: nea[g, t, j])

    def each(body, first, count):
        def step(i, carry):
            body(first + i)
            return carry

        lax.fori_loop(0, count, step, 0, unroll=min(UNROLL, count))

    for copy in smalls[:2]:
        copy.wait()
    bigs[0].wait()
    each(functools.partial(far_body, 1, 12), 0, 2)
    each(functools.partial(far_body, 2, 8), 0, 4)
    bigs[1].wait()
    each(functools.partial(far_body, 3, 0), 0, 4)
    bigs[2].wait()
    each(functools.partial(far_body, 3, 0), 4, 4)
    bigs[3].wait()
    each(near_body, 0, 4)
    bigs[4].wait()
    each(near_body, 4, 4)
    for copy in smalls[2:]:
        copy.wait()
    up2 = [sums[12 + t].astype(bf16) for t in range(2)]
    up1 = [
        (sums[8 + t] + dot_nt(up2[t // 2], tra[8 + t])).astype(bf16) for t in range(4)
    ]
    up0 = [(sums[t] + dot_nt(up1[t // 2], tra[t])).astype(bf16) for t in range(8)]
    full = [cells[t] + dot_nt(up0[t], bas[t]) for t in range(8)]
    for pair in range(LEAVES // 2):
        both = jnp.concatenate([full[2 * pair], full[2 * pair + 1]], axis=1)
        for g in range(2):
            base[g, :, pl.ds(pair * 2 * R, 2 * R)] = both[g * RHS : (g + 1) * RHS]


def local_call(own, even, odd, coupling_source, near_source, coupling, near, transfer, basis):
    return pl.pallas_call(
        local_kernel,
        out_shape=pltpu.VMEM((2, RHS, LEAVES * R), f32),
        in_specs=[VMEM] * 3 + [ANY] * 6,
        out_specs=VMEM,
        scratch_shapes=[
            pltpu.VMEM((2, 3 * ROWS, RHS, 2 * R), bf16),
            pltpu.VMEM((LOCAL, 2 * RHS, R), f32),
            pltpu.VMEM((LEAVES, 2 * RHS, R), f32),
            pltpu.VMEM((2, LOCAL, LINKS, R, R), bf16),
            pltpu.VMEM((2, LEAVES, LINKS, R, R), bf16),
            pltpu.SMEM((LOCAL, LINKS), jnp.int32),
            pltpu.SMEM((LEAVES, LINKS), jnp.int32),
            pltpu.VMEM((LOCAL, R, R), bf16),
            pltpu.VMEM((LEAVES, R, R), bf16),
            pltpu.SemaphoreType.DMA((9,)),
        ],
        compiler_params=pltpu.CompilerParams(vmem_limit_bytes=24 * MB),
        cost_estimate=pl.CostEstimate(
            flops=10**8, bytes_accessed=2 * 10**7, transcendentals=0
        ),
        name="local",
    )(
        own, even, odd,
        *hbm(coupling, near, coupling_source, near_source, transfer, basis),
    )


def final_kernel(parts, roots, fold, leafs, base, out):
    branch = lax.axis_index("branch")
    others = [roots[(branch + 1 + i) % N_BRANCH] for i in range(N_BRANCH - 1)]
    row = jnp.concatenate([parts[...]] + others, axis=1)
    target = dot_nt(row, fold[...]).astype(bf16)
    far = dot_nt(target, leafs[...])
    width = LEAVES * R
    for g in range(2):
        out[g] = base[g] + far[:, g * width : (g + 1) * width]


def final_call(parts, roots, fold, leafs, base):
    return pl.pallas_call(
        final_kernel,
        out_shape=jax.ShapeDtypeStruct((2, RHS, LEAVES * R), f32),
        in_specs=[VMEM] * 5,
        out_specs=VMEM,
        compiler_params=pltpu.CompilerParams(vmem_limit_bytes=8 * MB),
        name="final",
    )(parts, roots, fold, leafs, base)


def per_device(
    values,
    leaf_basis,
    transfer,
    local_coupling,
    coupling_source,
    near_field,
    near_source,
    upper_transfer,
    upper_coupling,
    top_coupling,
):
    vals, coefs, sent, summit, downs, own, sib, cou, tops, bas, tra = up_call(
        values, leaf_basis, transfer, upper_transfer, upper_coupling, top_coupling
    )
    got = lax.all_to_all(sent, "leaf", 0, 0, axis_index_groups=[list(range(N_LEAF - 1, -1, -1))], tiled=True)
    lift = cast_call(own, sib)
    fold, leafs = prep_call(cou, tops, downs, bas, tra)
    rows = pack_call(vals, coefs)
    count = N_BRANCH * N_LEAF
    ring = ("branch", "leaf")
    even = lax.ppermute(rows, ring, [(i, i ^ 1) for i in range(count)])
    odd = lax.ppermute(
        rows, ring, [(i, ((i + 1) ^ 1) - 1) for i in range(1, count - 1)]
    )
    parts, fan = mid_call(got, summit, lift)
    parts, fan, even, fold, leafs = lax.optimization_barrier((parts, fan, even, fold, leafs))
    roots = lax.all_to_all(fan, "branch", 0, 0, tiled=True)
    base = local_call(
        rows, even, odd, coupling_source, near_source, local_coupling, near_field,
        transfer, leaf_basis,
    )
    return final_call(parts, roots, fold, leafs, base)


def solution(mesh):
    in_specs = (
        P(None, None, ("branch", "leaf")),
        P(("branch", "leaf"), None, None),
        P(("branch", "leaf"), None, None),
        P(None, ("branch", "leaf"), None, None, None),
        P(("branch", "leaf"), None),
        P(None, ("branch", "leaf"), None, None, None),
        P(("branch", "leaf"), None),
        P("branch", None, None, None),
        P(None, "branch", None, None, None),
        P(None, "branch", None, None, None),
    )
    out_specs = P(None, None, ("branch", "leaf"))
    return jax.shard_map(
        per_device, mesh=mesh, in_specs=in_specs, out_specs=out_specs, check_vma=False
    )
```

```python
import functools

import jax
import jax.numpy as jnp
from jax import lax
from jax.experimental import pallas as pl
from jax.experimental.pallas import tpu as pltpu
from jax.sharding import PartitionSpec as P

f32 = jnp.float32
bf16 = jnp.bfloat16
R = 64
RHS = 16
LEAVES = 8
LOCAL = 14
ROWS = 22
DEPTH = 5
N_LEAF = 32
N_BRANCH = 8
LINKS = 12
UNROLL = 4
ANY = pl.BlockSpec(memory_space=pl.ANY)
VMEM = pl.BlockSpec(memory_space=pltpu.VMEM)
MB = 2**20


def hbm(*arrays):
    return [pltpu.with_memory_space_constraint(a, pltpu.HBM) for a in arrays]


def dot(a, b):
    return jnp.dot(a, b, preferred_element_type=f32)


def dot_nt(a, b):
    return lax.dot_general(a, b, (((1,), (1,)), ((), ())), preferred_element_type=f32)


def turned(v):
    return jnp.concatenate([v[:, R:], v[:, :R]], axis=1)


def packed(c):
    return jnp.concatenate([c[:RHS], c[RHS:]], axis=1)


def upper_index(leaf, step):
    return 2 * N_LEAF - 2 * (N_LEAF >> step) + jnp.right_shift(leaf, step)


def seat(leaf):
    return N_LEAF - 1 - leaf


def up_kernel(
    values, basis, transfer, upper, couple, top,
    vals, coefs, sent, summit, downs, upp, sib, cou, tops, bas, tra, sem,
):
    leaf = lax.axis_index("leaf")
    here = [upper_index(leaf, step) for step in range(DEPTH)]
    firsts = [
        pltpu.make_async_copy(values, vals, sem.at[0]),
        pltpu.make_async_copy(basis, bas, sem.at[1]),
        pltpu.make_async_copy(transfer, tra, sem.at[2]),
    ]
    lasts = [pltpu.make_async_copy(top, tops, sem.at[3])]
    for k in range(DEPTH):
        there = jnp.bitwise_xor(here[k], 1)
        firsts.append(pltpu.make_async_copy(upper.at[0, here[k]], upp.at[k], sem.at[4 + 3 * k]))
        lasts.append(pltpu.make_async_copy(upper.at[0, there], sib.at[k], sem.at[5 + 3 * k]))
        lasts.append(
            pltpu.make_async_copy(couple.at[:, 0, here[k]], cou.at[k], sem.at[6 + 3 * k])
        )
    for copy in firsts + lasts:
        copy.start()
    for copy in firsts:
        copy.wait()
    down = upp[0]
    downs[0] = down
    for step in range(1, DEPTH):
        down = dot(down, upp[step]).astype(bf16)
        downs[step] = down
    level = []
    for pair in range(LEAVES // 2):
        x0 = vals[0, :, pl.ds(pair * 2 * R, 2 * R)]
        x1 = vals[1, :, pl.ds(pair * 2 * R, 2 * R)]
        for half in range(2):
            lanes = slice(half * R, (half + 1) * R)
            cell = jnp.concatenate([x0[:, lanes], x1[:, lanes]], axis=0)
            level.append(dot(cell, bas[2 * pair + half]).astype(bf16))
    begin = 0
    while len(level) > 1:
        for i, c in enumerate(level):
            coefs[begin + i] = c
        merged = [
            (dot(level[i], tra[begin + i]) + dot(level[i + 1], tra[begin + i + 1])).astype(bf16)
            for i in range(0, len(level), 2)
        ]
        begin += len(level)
        level = merged
    root = level[0]
    chain = [packed(root)]
    for step in range(DEPTH):
        chain.append(packed(dot(root, downs[step]).astype(bf16)))
    summit[...] = chain[DEPTH]
    sent[seat(leaf)] = chain[0]
    for i in range(1, N_LEAF):
        sent[seat(jnp.bitwise_xor(leaf, i))] = chain[i.bit_length() - 1]
    for copy in lasts:
        copy.wait()


def up_call(values, basis, transfer, upper, couple, top):
    return pl.pallas_call(
        up_kernel,
        out_shape=[
            pltpu.VMEM((2, RHS, LEAVES * R), bf16),
            pltpu.VMEM((LOCAL, 2 * RHS, R), bf16),
            pltpu.VMEM((N_LEAF, RHS, 2 * R), bf16),
            pltpu.VMEM((RHS, 2 * R), bf16),
            pltpu.VMEM((DEPTH, R, R), bf16),
            pltpu.VMEM((DEPTH, R, R), bf16),
            pltpu.VMEM((DEPTH, R, R), bf16),
            pltpu.VMEM((DEPTH, 2, R, R), bf16),
            pltpu.VMEM((2, 1, N_BRANCH - 1, R, R), bf16),
            pltpu.VMEM((LEAVES, R, R), bf16),
            pltpu.VMEM((LOCAL, R, R), bf16),
        ],
        in_specs=[ANY] * 6,
        out_specs=[VMEM] * 11,
        scratch_shapes=[pltpu.SemaphoreType.DMA((4 + 3 * DEPTH,))],
        compiler_params=pltpu.CompilerParams(vmem_limit_bytes=8 * MB),
        name="up",
    )(*hbm(values, basis, transfer, upper, couple, top))


def pack_kernel(vals, coefs, rows):
    left = lax.broadcasted_iota(jnp.int32, (RHS, 2 * R), 1) < R
    for pair in range(LEAVES // 2):
        x0 = vals[0, :, pl.ds(pair * 2 * R, 2 * R)]
        x1 = vals[1, :, pl.ds(pair * 2 * R, 2 * R)]
        rows[2 * pair] = jnp.where(left, x0, turned(x1))
        rows[2 * pair + 1] = jnp.where(left, turned(x0), x1)
    for i in range(LOCAL):
        rows[LEAVES + i] = packed(coefs[i])


def pack_call(vals, coefs):
    return pl.pallas_call(
        pack_kernel,
        out_shape=pltpu.VMEM((ROWS, RHS, 2 * R), bf16),
        in_specs=[VMEM] * 2,
        out_specs=VMEM,
        compiler_params=pltpu.CompilerParams(vmem_limit_bytes=8 * MB),
        cost_estimate=pl.CostEstimate(
            flops=10**8, bytes_accessed=4 * 10**6, transcendentals=0
        ),
        name="pack",
    )(vals, coefs)


def cast_kernel(own, sib, lift):
    zero = jnp.zeros((R, R), bf16)

    def place(step, mat):
        lift[pl.ds(2 * step * R, R), :] = jnp.concatenate([mat, zero], axis=1)
        lift[pl.ds((2 * step + 1) * R, R), :] = jnp.concatenate([zero, mat], axis=1)

    path = own[DEPTH - 1]
    place(DEPTH - 1, sib[DEPTH - 1])
    for step in range(DEPTH - 2, -1, -1):
        place(step, dot(sib[step], path).astype(bf16))
        if step:
            path = dot(own[step], path).astype(bf16)


def cast_call(own, sib):
    return pl.pallas_call(
        cast_kernel,
        out_shape=pltpu.VMEM((DEPTH * 2 * R, 2 * R), bf16),
        in_specs=[VMEM] * 2,
        out_specs=VMEM,
        compiler_params=pltpu.CompilerParams(vmem_limit_bytes=8 * MB),
        cost_estimate=pl.CostEstimate(
            flops=10**8, bytes_accessed=4 * 10**6, transcendentals=0
        ),
        name="cast",
    )(own, sib)


def prep_kernel(cou, tops, downs, bas, tra, fold, leafs):
    zero = jnp.zeros((R, R), bf16)
    tops2 = [tra[12 + t] for t in range(2)]
    tops1 = [dot(tra[8 + t], tops2[t // 2]).astype(bf16) for t in range(4)]
    tops0 = [dot(tra[t], tops1[t // 2]).astype(bf16) for t in range(8)]
    for t in range(LEAVES):
        full = dot(bas[t], tops0[t]).astype(bf16)
        leafs[pl.ds(t * R, R), :] = jnp.concatenate([full, zero], axis=1)
        leafs[pl.ds((LEAVES + t) * R, R), :] = jnp.concatenate([zero, full], axis=1)
    for step in range(DEPTH + N_BRANCH - 1):
        lanes = pl.ds(step * 2 * R, 2 * R)
        for g in range(2):
            if step == 0:
                mat = cou[step, g]
            elif step < DEPTH:
                mat = dot(downs[step - 1], cou[step, g]).astype(bf16)
            else:
                mat = dot(downs[DEPTH - 1], tops[g, 0, step - DEPTH]).astype(bf16)
            pair = [mat, zero] if g == 0 else [zero, mat]
            fold[pl.ds(g * R, R), lanes] = jnp.concatenate(pair, axis=1)


def prep_call(cou, tops, downs, bas, tra):
    return pl.pallas_call(
        prep_kernel,
        out_shape=[
            pltpu.VMEM((2 * R, (DEPTH + N_BRANCH - 1) * 2 * R), bf16),
            pltpu.VMEM((2 * LEAVES * R, 2 * R), bf16),
        ],
        in_specs=[VMEM] * 5,
        out_specs=[VMEM] * 2,
        compiler_params=pltpu.CompilerParams(vmem_limit_bytes=8 * MB),
        cost_estimate=pl.CostEstimate(
            flops=10**8, bytes_accessed=4 * 10**6, transcendentals=0
        ),
        name="prep",
    )(cou, tops, downs, bas, tra)


def mid_kernel(got, summit, lift, parts, fan):
    leaf = lax.axis_index("leaf")
    for step in range(DEPTH):
        total = None
        for i in range(1 << step, 2 << step):
            v = got[seat(jnp.bitwise_xor(leaf, i))].astype(f32)
            total = v if total is None else total + v
        parts[:, pl.ds(step * 2 * R, 2 * R)] = total.astype(bf16)
    root = (dot(parts[...], lift[...]) + summit[...].astype(f32)).astype(bf16)
    for b in range(N_BRANCH):
        fan[b] = root


def mid_call(got, summit, lift):
    return pl.pallas_call(
        mid_kernel,
        out_shape=[
            pltpu.VMEM((RHS, DEPTH * 2 * R), bf16),
            pltpu.VMEM((N_BRANCH, RHS, 2 * R), bf16),
        ],
        in_specs=[VMEM] * 3,
        out_specs=[VMEM] * 2,
        compiler_params=pltpu.CompilerParams(vmem_limit_bytes=8 * MB),
        name="mid",
    )(got, summit, lift)


def local_kernel(
    own, even, odd, coupling, near, coupling_source, near_source, transfer, basis,
    base, wide, sums, cells, cou, nea, cosrc, nesrc, tra, bas, sem,
):
    smalls = [
        pltpu.make_async_copy(coupling_source, cosrc, sem.at[0]),
        pltpu.make_async_copy(near_source, nesrc, sem.at[1]),
        pltpu.make_async_copy(transfer, tra, sem.at[2]),
        pltpu.make_async_copy(basis, bas, sem.at[3]),
    ]
    bigs = []
    for n, (source, into, start, count) in enumerate(
        ((coupling, cou, 8, 6), (coupling, cou, 0, 4), (coupling, cou, 4, 4),
         (near, nea, 0, 4), (near, nea, 4, 2), (near, nea, 6, 2))
    ):
        span = pl.ds(start, count)
        bigs.append(pltpu.make_async_copy(source.at[:, span], into.at[:, span], sem.at[4 + n]))
    for copy in smalls + bigs:
        copy.start()
    left = lax.broadcasted_iota(jnp.int32, (RHS, 2 * R), 1) < R
    here = jnp.bitwise_and(lax.axis_index("leaf"), 1)
    for part, ref in ((1, own), (2 - 2 * here, even), (2 * here, odd)):
        for row in range(ROWS):
            v = ref[row]
            s = turned(v)
            wide[0, part * ROWS + row] = jnp.where(left, v, s)
            wide[1, part * ROWS + row] = jnp.where(left, s, v)

    def block(picked, mats):
        result = []
        for g in range(2):
            acc = None
            for j in range(0, LINKS, 4):
                v = jnp.concatenate(
                    [
                        jnp.where(left, wide[g, picked[j]], wide[g, picked[j + 1]]),
                        jnp.where(left, wide[g, picked[j + 2]], wide[g, picked[j + 3]]),
                    ],
                    axis=1,
                )
                m = jnp.concatenate([mats(g, j + n) for n in range(4)], axis=1)
                part = dot_nt(v, m)
                acc = part if acc is None else acc + part
            result.append(acc)
        return jnp.concatenate(result, axis=0)

    def far_body(log, start, t):
        r = start + t
        picked = []
        for j in range(LINKS):
            s = cosrc[r, j]
            picked.append(
                jnp.right_shift(s, log) * ROWS
                + LEAVES
                + start
                + jnp.bitwise_and(s, (1 << log) - 1)
            )
        sums[r] = block(picked, lambda g, j: cou[g, r, j])

    def near_body(t):
        picked = []
        for j in range(LINKS):
            s = nesrc[t, j]
            picked.append(jnp.right_shift(s, 3) * ROWS + jnp.bitwise_and(s, 7))
        cells[t] = block(picked, lambda g, j: nea[g, t, j])

    def each(body, first, count):
        def step(i, carry):
            body(first + i)
            return carry

        lax.fori_loop(0, count, step, 0, unroll=min(UNROLL, count))

    for copy in smalls[:2]:
        copy.wait()
    bigs[0].wait()
    each(functools.partial(far_body, 1, 12), 0, 2)
    each(functools.partial(far_body, 2, 8), 0, 4)
    bigs[1].wait()
    each(functools.partial(far_body, 3, 0), 0, 4)
    bigs[2].wait()
    each(functools.partial(far_body, 3, 0), 4, 4)
    for copy in smalls[2:]:
        copy.wait()
    up2 = [sums[12 + t].astype(bf16) for t in range(2)]
    up1 = [
        (sums[8 + t] + dot_nt(up2[t // 2], tra[8 + t])).astype(bf16) for t in range(4)
    ]
    up0 = [(sums[t] + dot_nt(up1[t // 2], tra[t])).astype(bf16) for t in range(8)]
    for t in range(LEAVES):
        sums[t] = dot_nt(up0[t], bas[t])
    bigs[3].wait()
    each(near_body, 0, 4)
    bigs[4].wait()
    each(near_body, 4, 2)
    bigs[5].wait()
    each(near_body, 6, 2)
    full = [cells[t] + sums[t] for t in range(LEAVES)]
    for pair in range(LEAVES // 2):
        both = jnp.concatenate([full[2 * pair], full[2 * pair + 1]], axis=1)
        for g in range(2):
            base[g, :, pl.ds(pair * 2 * R, 2 * R)] = both[g * RHS : (g + 1) * RHS]


def local_call(own, even, odd, coupling_source, near_source, coupling, near, transfer, basis):
    return pl.pallas_call(
        local_kernel,
        out_shape=pltpu.VMEM((2, RHS, LEAVES * R), f32),
        in_specs=[VMEM] * 3 + [ANY] * 6,
        out_specs=VMEM,
        scratch_shapes=[
            pltpu.VMEM((2, 3 * ROWS, RHS, 2 * R), bf16),
            pltpu.VMEM((LOCAL, 2 * RHS, R), f32),
            pltpu.VMEM((LEAVES, 2 * RHS, R), f32),
            pltpu.VMEM((2, LOCAL, LINKS, R, R), bf16),
            pltpu.VMEM((2, LEAVES, LINKS, R, R), bf16),
            pltpu.SMEM((LOCAL, LINKS), jnp.int32),
            pltpu.SMEM((LEAVES, LINKS), jnp.int32),
            pltpu.VMEM((LOCAL, R, R), bf16),
            pltpu.VMEM((LEAVES, R, R), bf16),
            pltpu.SemaphoreType.DMA((10,)),
        ],
        compiler_params=pltpu.CompilerParams(vmem_limit_bytes=24 * MB),
        cost_estimate=pl.CostEstimate(
            flops=10**8, bytes_accessed=2 * 10**7, transcendentals=0
        ),
        name="local",
    )(
        own, even, odd,
        *hbm(coupling, near, coupling_source, near_source, transfer, basis),
    )


def final_kernel(parts, roots, fold, leafs, base, out):
    branch = lax.axis_index("branch")
    others = [roots[(branch + 1 + i) % N_BRANCH] for i in range(N_BRANCH - 1)]
    row = jnp.concatenate([parts[...]] + others, axis=1)
    target = dot_nt(row, fold[...]).astype(bf16)
    far = dot_nt(target, leafs[...])
    width = LEAVES * R
    for g in range(2):
        out[g] = base[g] + far[:, g * width : (g + 1) * width]


def final_call(parts, roots, fold, leafs, base):
    return pl.pallas_call(
        final_kernel,
        out_shape=jax.ShapeDtypeStruct((2, RHS, LEAVES * R), f32),
        in_specs=[VMEM] * 5,
        out_specs=VMEM,
        compiler_params=pltpu.CompilerParams(vmem_limit_bytes=8 * MB),
        name="final",
    )(parts, roots, fold, leafs, base)


def per_device(
    values,
    leaf_basis,
    transfer,
    local_coupling,
    coupling_source,
    near_field,
    near_source,
    upper_transfer,
    upper_coupling,
    top_coupling,
):
    vals, coefs, sent, summit, downs, own, sib, cou, tops, bas, tra = up_call(
        values, leaf_basis, transfer, upper_transfer, upper_coupling, top_coupling
    )
    got = lax.all_to_all(sent, "leaf", 0, 0, axis_index_groups=[list(range(N_LEAF - 1, -1, -1))], tiled=True)
    lift = cast_call(own, sib)
    fold, leafs = prep_call(cou, tops, downs, bas, tra)
    rows = pack_call(vals, coefs)
    count = N_BRANCH * N_LEAF
    ring = ("branch", "leaf")
    even = lax.ppermute(rows, ring, [(i, i ^ 1) for i in range(count)])
    odd = lax.ppermute(
        rows, ring, [(i, ((i + 1) ^ 1) - 1) for i in range(1, count - 1)]
    )
    parts, fan = mid_call(got, summit, lift)
    parts, fan, even, fold, leafs = lax.optimization_barrier((parts, fan, even, fold, leafs))
    roots = lax.all_to_all(fan, "branch", 0, 0, tiled=True)
    base = local_call(
        rows, even, odd, coupling_source, near_source, local_coupling, near_field,
        transfer, leaf_basis,
    )
    return final_call(parts, roots, fold, leafs, base)


def solution(mesh):
    in_specs = (
        P(None, None, ("branch", "leaf")),
        P(("branch", "leaf"), None, None),
        P(("branch", "leaf"), None, None),
        P(None, ("branch", "leaf"), None, None, None),
        P(("branch", "leaf"), None),
        P(None, ("branch", "leaf"), None, None, None),
        P(("branch", "leaf"), None),
        P("branch", None, None, None),
        P(None, "branch", None, None, None),
        P(None, "branch", None, None, None),
    )
    out_specs = P(None, None, ("branch", "leaf"))
    return jax.shard_map(
        per_device, mesh=mesh, in_specs=in_specs, out_specs=out_specs, check_vma=False
    )
```

```python
import functools

import jax
import jax.numpy as jnp
from jax import lax
from jax.experimental import pallas as pl
from jax.experimental.pallas import tpu as pltpu
from jax.sharding import PartitionSpec as P

f32 = jnp.float32
bf16 = jnp.bfloat16
R = 64
RHS = 16
LEAVES = 8
LOCAL = 14
ROWS = 22
DEPTH = 5
N_LEAF = 32
N_BRANCH = 8
LINKS = 12
UNROLL = 4
ANY = pl.BlockSpec(memory_space=pl.ANY)
VMEM = pl.BlockSpec(memory_space=pltpu.VMEM)
MB = 2**20


def hbm(*arrays):
    return [pltpu.with_memory_space_constraint(a, pltpu.HBM) for a in arrays]


def dot(a, b):
    return jnp.dot(a, b, preferred_element_type=f32)


def dot_nt(a, b):
    return lax.dot_general(a, b, (((1,), (1,)), ((), ())), preferred_element_type=f32)


def turned(v):
    return jnp.concatenate([v[:, R:], v[:, :R]], axis=1)


def packed(c):
    return jnp.concatenate([c[:RHS], c[RHS:]], axis=1)


def upper_index(leaf, step):
    return 2 * N_LEAF - 2 * (N_LEAF >> step) + jnp.right_shift(leaf, step)


def seat(leaf):
    return N_LEAF - 1 - leaf


def up_kernel(
    values, basis, transfer, upper, couple, top,
    vals, coefs, sent, summit, downs, upp, sib, cou, tops, bas, tra, sem,
):
    leaf = lax.axis_index("leaf")
    here = [upper_index(leaf, step) for step in range(DEPTH)]
    firsts = [
        pltpu.make_async_copy(values, vals, sem.at[0]),
        pltpu.make_async_copy(basis, bas, sem.at[1]),
        pltpu.make_async_copy(transfer, tra, sem.at[2]),
    ]
    lasts = [pltpu.make_async_copy(top, tops, sem.at[3])]
    for k in range(DEPTH):
        there = jnp.bitwise_xor(here[k], 1)
        firsts.append(pltpu.make_async_copy(upper.at[0, here[k]], upp.at[k], sem.at[4 + 3 * k]))
        lasts.append(pltpu.make_async_copy(upper.at[0, there], sib.at[k], sem.at[5 + 3 * k]))
        lasts.append(
            pltpu.make_async_copy(couple.at[:, 0, here[k]], cou.at[k], sem.at[6 + 3 * k])
        )
    for copy in firsts + lasts:
        copy.start()
    for copy in firsts:
        copy.wait()
    down = upp[0]
    downs[0] = down
    for step in range(1, DEPTH):
        down = dot(down, upp[step]).astype(bf16)
        downs[step] = down
    level = []
    for pair in range(LEAVES // 2):
        x0 = vals[0, :, pl.ds(pair * 2 * R, 2 * R)]
        x1 = vals[1, :, pl.ds(pair * 2 * R, 2 * R)]
        for half in range(2):
            lanes = slice(half * R, (half + 1) * R)
            cell = jnp.concatenate([x0[:, lanes], x1[:, lanes]], axis=0)
            level.append(dot(cell, bas[2 * pair + half]).astype(bf16))
    begin = 0
    while len(level) > 1:
        for i, c in enumerate(level):
            coefs[begin + i] = c
        merged = [
            (dot(level[i], tra[begin + i]) + dot(level[i + 1], tra[begin + i + 1])).astype(bf16)
            for i in range(0, len(level), 2)
        ]
        begin += len(level)
        level = merged
    root = level[0]
    chain = [packed(root)]
    for step in range(DEPTH):
        chain.append(packed(dot(root, downs[step]).astype(bf16)))
    summit[...] = chain[DEPTH]
    sent[seat(leaf)] = chain[0]
    for i in range(1, N_LEAF):
        sent[seat(jnp.bitwise_xor(leaf, i))] = chain[i.bit_length() - 1]
    for copy in lasts:
        copy.wait()


def up_call(values, basis, transfer, upper, couple, top):
    return pl.pallas_call(
        up_kernel,
        out_shape=[
            pltpu.VMEM((2, RHS, LEAVES * R), bf16),
            pltpu.VMEM((LOCAL, 2 * RHS, R), bf16),
            pltpu.VMEM((N_LEAF, RHS, 2 * R), bf16),
            pltpu.VMEM((RHS, 2 * R), bf16),
            pltpu.VMEM((DEPTH, R, R), bf16),
            pltpu.VMEM((DEPTH, R, R), bf16),
            pltpu.VMEM((DEPTH, R, R), bf16),
            pltpu.VMEM((DEPTH, 2, R, R), bf16),
            pltpu.VMEM((2, 1, N_BRANCH - 1, R, R), bf16),
            pltpu.VMEM((LEAVES, R, R), bf16),
            pltpu.VMEM((LOCAL, R, R), bf16),
        ],
        in_specs=[ANY] * 6,
        out_specs=[VMEM] * 11,
        scratch_shapes=[pltpu.SemaphoreType.DMA((4 + 3 * DEPTH,))],
        compiler_params=pltpu.CompilerParams(vmem_limit_bytes=8 * MB),
        name="up",
    )(*hbm(values, basis, transfer, upper, couple, top))


def pack_kernel(vals, coefs, rows):
    left = lax.broadcasted_iota(jnp.int32, (RHS, 2 * R), 1) < R
    for pair in range(LEAVES // 2):
        x0 = vals[0, :, pl.ds(pair * 2 * R, 2 * R)]
        x1 = vals[1, :, pl.ds(pair * 2 * R, 2 * R)]
        rows[2 * pair] = jnp.where(left, x0, turned(x1))
        rows[2 * pair + 1] = jnp.where(left, turned(x0), x1)
    for i in range(LOCAL):
        rows[LEAVES + i] = packed(coefs[i])


def pack_call(vals, coefs):
    return pl.pallas_call(
        pack_kernel,
        out_shape=pltpu.VMEM((ROWS, RHS, 2 * R), bf16),
        in_specs=[VMEM] * 2,
        out_specs=VMEM,
        compiler_params=pltpu.CompilerParams(vmem_limit_bytes=8 * MB),
        cost_estimate=pl.CostEstimate(
            flops=10**8, bytes_accessed=4 * 10**6, transcendentals=0
        ),
        name="pack",
    )(vals, coefs)


def cast_kernel(own, sib, lift):
    zero = jnp.zeros((R, R), bf16)

    def place(step, mat):
        lift[pl.ds(2 * step * R, R), :] = jnp.concatenate([mat, zero], axis=1)
        lift[pl.ds((2 * step + 1) * R, R), :] = jnp.concatenate([zero, mat], axis=1)

    path = own[DEPTH - 1]
    place(DEPTH - 1, sib[DEPTH - 1])
    for step in range(DEPTH - 2, -1, -1):
        place(step, dot(sib[step], path).astype(bf16))
        if step:
            path = dot(own[step], path).astype(bf16)


def cast_call(own, sib):
    return pl.pallas_call(
        cast_kernel,
        out_shape=pltpu.VMEM((DEPTH * 2 * R, 2 * R), bf16),
        in_specs=[VMEM] * 2,
        out_specs=VMEM,
        compiler_params=pltpu.CompilerParams(vmem_limit_bytes=8 * MB),
        cost_estimate=pl.CostEstimate(
            flops=10**8, bytes_accessed=4 * 10**6, transcendentals=0
        ),
        name="cast",
    )(own, sib)


def prep_kernel(cou, tops, downs, bas, tra, fold, leafs):
    zero = jnp.zeros((R, R), bf16)
    tops2 = [tra[12 + t] for t in range(2)]
    tops1 = [dot(tra[8 + t], tops2[t // 2]).astype(bf16) for t in range(4)]
    tops0 = [dot(tra[t], tops1[t // 2]).astype(bf16) for t in range(8)]
    for t in range(LEAVES):
        full = dot(bas[t], tops0[t]).astype(bf16)
        leafs[pl.ds(t * R, R), :] = jnp.concatenate([full, zero], axis=1)
        leafs[pl.ds((LEAVES + t) * R, R), :] = jnp.concatenate([zero, full], axis=1)
    for step in range(DEPTH + N_BRANCH - 1):
        lanes = pl.ds(step * 2 * R, 2 * R)
        for g in range(2):
            if step == 0:
                mat = cou[step, g]
            elif step < DEPTH:
                mat = dot(downs[step - 1], cou[step, g]).astype(bf16)
            else:
                mat = dot(downs[DEPTH - 1], tops[g, 0, step - DEPTH]).astype(bf16)
            pair = [mat, zero] if g == 0 else [zero, mat]
            fold[pl.ds(g * R, R), lanes] = jnp.concatenate(pair, axis=1)


def prep_call(cou, tops, downs, bas, tra):
    return pl.pallas_call(
        prep_kernel,
        out_shape=[
            pltpu.VMEM((2 * R, (DEPTH + N_BRANCH - 1) * 2 * R), bf16),
            pltpu.VMEM((2 * LEAVES * R, 2 * R), bf16),
        ],
        in_specs=[VMEM] * 5,
        out_specs=[VMEM] * 2,
        compiler_params=pltpu.CompilerParams(vmem_limit_bytes=8 * MB),
        cost_estimate=pl.CostEstimate(
            flops=10**8, bytes_accessed=4 * 10**6, transcendentals=0
        ),
        name="prep",
    )(cou, tops, downs, bas, tra)


def mid_kernel(got, summit, lift, parts, fan):
    leaf = lax.axis_index("leaf")
    for step in range(DEPTH):
        total = None
        for i in range(1 << step, 2 << step):
            v = got[seat(jnp.bitwise_xor(leaf, i))].astype(f32)
            total = v if total is None else total + v
        parts[:, pl.ds(step * 2 * R, 2 * R)] = total.astype(bf16)
    root = (dot(parts[...], lift[...]) + summit[...].astype(f32)).astype(bf16)
    for b in range(N_BRANCH):
        fan[b] = root


def mid_call(got, summit, lift):
    return pl.pallas_call(
        mid_kernel,
        out_shape=[
            pltpu.VMEM((RHS, DEPTH * 2 * R), bf16),
            pltpu.VMEM((N_BRANCH, RHS, 2 * R), bf16),
        ],
        in_specs=[VMEM] * 3,
        out_specs=[VMEM] * 2,
        compiler_params=pltpu.CompilerParams(vmem_limit_bytes=8 * MB),
        name="mid",
    )(got, summit, lift)


def local_kernel(
    own, even, odd, coupling, near, coupling_source, near_source, transfer, basis,
    base, wide, sums, cells, cou, nea, cosrc, nesrc, tra, bas, sem,
):
    smalls = [
        pltpu.make_async_copy(coupling_source, cosrc, sem.at[0]),
        pltpu.make_async_copy(near_source, nesrc, sem.at[1]),
        pltpu.make_async_copy(transfer, tra, sem.at[2]),
        pltpu.make_async_copy(basis, bas, sem.at[3]),
    ]
    bigs = []
    for n, (source, into, start, count) in enumerate(
        ((coupling, cou, 8, 6), (coupling, cou, 0, 4), (coupling, cou, 4, 4),
         (near, nea, 0, 4), (near, nea, 4, 4))
    ):
        span = pl.ds(start, count)
        bigs.append(pltpu.make_async_copy(source.at[:, span], into.at[:, span], sem.at[4 + n]))
    for copy in smalls[:2] + bigs + smalls[2:]:
        copy.start()
    left = lax.broadcasted_iota(jnp.int32, (RHS, 2 * R), 1) < R
    here = jnp.bitwise_and(lax.axis_index("leaf"), 1)
    for part, ref in ((1, own), (2 - 2 * here, even), (2 * here, odd)):
        for row in range(ROWS):
            v = ref[row]
            s = turned(v)
            wide[0, part * ROWS + row] = jnp.where(left, v, s)
            wide[1, part * ROWS + row] = jnp.where(left, s, v)

    def block(picked, mats):
        result = []
        for g in range(2):
            acc = None
            for j in range(0, LINKS, 4):
                v = jnp.concatenate(
                    [
                        jnp.where(left, wide[g, picked[j]], wide[g, picked[j + 1]]),
                        jnp.where(left, wide[g, picked[j + 2]], wide[g, picked[j + 3]]),
                    ],
                    axis=1,
                )
                m = jnp.concatenate([mats(g, j + n) for n in range(4)], axis=1)
                part = dot_nt(v, m)
                acc = part if acc is None else acc + part
            result.append(acc)
        return jnp.concatenate(result, axis=0)

    def far_body(log, start, t):
        r = start + t
        picked = []
        for j in range(LINKS):
            s = cosrc[r, j]
            picked.append(
                jnp.right_shift(s, log) * ROWS
                + LEAVES
                + start
                + jnp.bitwise_and(s, (1 << log) - 1)
            )
        sums[r] = block(picked, lambda g, j: cou[g, r, j])

    def near_body(t):
        picked = []
        for j in range(LINKS):
            s = nesrc[t, j]
            picked.append(jnp.right_shift(s, 3) * ROWS + jnp.bitwise_and(s, 7))
        cells[t] = block(picked, lambda g, j: nea[g, t, j])

    def each(body, first, count):
        def step(i, carry):
            body(first + i)
            return carry

        lax.fori_loop(0, count, step, 0, unroll=min(UNROLL, count))

    for copy in smalls[:2]:
        copy.wait()
    bigs[0].wait()
    each(functools.partial(far_body, 1, 12), 0, 2)
    each(functools.partial(far_body, 2, 8), 0, 4)
    bigs[1].wait()
    each(functools.partial(far_body, 3, 0), 0, 4)
    bigs[2].wait()
    each(functools.partial(far_body, 3, 0), 4, 4)
    bigs[3].wait()
    each(near_body, 0, 4)
    for copy in smalls[2:]:
        copy.wait()
    up2 = [sums[12 + t].astype(bf16) for t in range(2)]
    up1 = [
        (sums[8 + t] + dot_nt(up2[t // 2], tra[8 + t])).astype(bf16) for t in range(4)
    ]
    up0 = [(sums[t] + dot_nt(up1[t // 2], tra[t])).astype(bf16) for t in range(8)]
    for t in range(LEAVES):
        sums[t] = dot_nt(up0[t], bas[t])
    bigs[4].wait()
    each(near_body, 4, 4)
    full = [cells[t] + sums[t] for t in range(LEAVES)]
    for pair in range(LEAVES // 2):
        both = jnp.concatenate([full[2 * pair], full[2 * pair + 1]], axis=1)
        for g in range(2):
            base[g, :, pl.ds(pair * 2 * R, 2 * R)] = both[g * RHS : (g + 1) * RHS]


def local_call(own, even, odd, coupling_source, near_source, coupling, near, transfer, basis):
    return pl.pallas_call(
        local_kernel,
        out_shape=pltpu.VMEM((2, RHS, LEAVES * R), f32),
        in_specs=[VMEM] * 3 + [ANY] * 6,
        out_specs=VMEM,
        scratch_shapes=[
            pltpu.VMEM((2, 3 * ROWS, RHS, 2 * R), bf16),
            pltpu.VMEM((LOCAL, 2 * RHS, R), f32),
            pltpu.VMEM((LEAVES, 2 * RHS, R), f32),
            pltpu.VMEM((2, LOCAL, LINKS, R, R), bf16),
            pltpu.VMEM((2, LEAVES, LINKS, R, R), bf16),
            pltpu.SMEM((LOCAL, LINKS), jnp.int32),
            pltpu.SMEM((LEAVES, LINKS), jnp.int32),
            pltpu.VMEM((LOCAL, R, R), bf16),
            pltpu.VMEM((LEAVES, R, R), bf16),
            pltpu.SemaphoreType.DMA((9,)),
        ],
        compiler_params=pltpu.CompilerParams(vmem_limit_bytes=24 * MB),
        cost_estimate=pl.CostEstimate(
            flops=10**8, bytes_accessed=2 * 10**7, transcendentals=0
        ),
        name="local",
    )(
        own, even, odd,
        *hbm(coupling, near, coupling_source, near_source, transfer, basis),
    )


def final_kernel(parts, roots, fold, leafs, base, out):
    branch = lax.axis_index("branch")
    others = [roots[(branch + 1 + i) % N_BRANCH] for i in range(N_BRANCH - 1)]
    row = jnp.concatenate([parts[...]] + others, axis=1)
    target = dot_nt(row, fold[...]).astype(bf16)
    far = dot_nt(target, leafs[...])
    width = LEAVES * R
    for g in range(2):
        out[g] = base[g] + far[:, g * width : (g + 1) * width]


def final_call(parts, roots, fold, leafs, base):
    return pl.pallas_call(
        final_kernel,
        out_shape=jax.ShapeDtypeStruct((2, RHS, LEAVES * R), f32),
        in_specs=[VMEM] * 5,
        out_specs=VMEM,
        compiler_params=pltpu.CompilerParams(vmem_limit_bytes=8 * MB),
        name="final",
    )(parts, roots, fold, leafs, base)


def per_device(
    values,
    leaf_basis,
    transfer,
    local_coupling,
    coupling_source,
    near_field,
    near_source,
    upper_transfer,
    upper_coupling,
    top_coupling,
):
    vals, coefs, sent, summit, downs, own, sib, cou, tops, bas, tra = up_call(
        values, leaf_basis, transfer, upper_transfer, upper_coupling, top_coupling
    )
    got = lax.all_to_all(sent, "leaf", 0, 0, axis_index_groups=[list(range(N_LEAF - 1, -1, -1))], tiled=True)
    lift = cast_call(own, sib)
    fold, leafs = prep_call(cou, tops, downs, bas, tra)
    rows = pack_call(vals, coefs)
    count = N_BRANCH * N_LEAF
    ring = ("branch", "leaf")
    even = lax.ppermute(rows, ring, [(i, i ^ 1) for i in range(count)])
    odd = lax.ppermute(
        rows, ring, [(i, ((i + 1) ^ 1) - 1) for i in range(1, count - 1)]
    )
    parts, fan = mid_call(got, summit, lift)
    parts, fan, even, fold, leafs = lax.optimization_barrier((parts, fan, even, fold, leafs))
    roots = lax.all_to_all(fan, "branch", 0, 0, tiled=True)
    base = local_call(
        rows, even, odd, coupling_source, near_source, local_coupling, near_field,
        transfer, leaf_basis,
    )
    return final_call(parts, roots, fold, leafs, base)


def solution(mesh):
    in_specs = (
        P(None, None, ("branch", "leaf")),
        P(("branch", "leaf"), None, None),
        P(("branch", "leaf"), None, None),
        P(None, ("branch", "leaf"), None, None, None),
        P(("branch", "leaf"), None),
        P(None, ("branch", "leaf"), None, None, None),
        P(("branch", "leaf"), None),
        P("branch", None, None, None),
        P(None, "branch", None, None, None),
        P(None, "branch", None, None, None),
    )
    out_specs = P(None, None, ("branch", "leaf"))
    return jax.shard_map(
        per_device, mesh=mesh, in_specs=in_specs, out_specs=out_specs, check_vma=False
    )
```
